32 devices in a mesh: gr: 4 (over z), gc: 8 (over y, x, core).
Axes of the slice: x: 2, y: 2, z: 4, core: 2. Of those that a mesh axis runs over, the one named last changes fastest.
Arguments:
- embeddings: bfloat16 [8192, 768], P(('gr', 'gc'))
- cluster_ids: int32 [8192], P(('gr', 'gc')), may hold values from 0 to 3, as said below
Outputs:
- neighbour_sum: float32 [8192, 768], P(('gr', 'gc'))
- density: float32 [8192], P(('gr', 'gc'))
The draws below stay inside these ranges and needn't reach their ends.
Inputs may be any that keep to these rules, and one draw needn't show every extreme that they name: `cluster_ids`: each device's 256 rows hold exactly 64 rows of every cluster.
All inputs are finite; a program needn't handle non-finite values.
Results may differ from the reference program's by a relative error of at most 0.0017.
Values may be sent and summed in bfloat16 or wider, within the bound.
No kernel may reach another device: no remote copies, remote signals or barrier semaphores. Data moves between devices by JAX's collectives and lax.ppermute only.
A program may use at most 128 MiB of HBM per device.

```python
import math
import jax
import jax.numpy as jnp
from jax import lax

D = 768
R_DEV = 256
CLUSTERS = 4
ROWS = 8192


def shared_ids(key):
    blocks = ROWS // R_DEV
    base = jnp.tile(jnp.arange(CLUSTERS, dtype=jnp.int32), R_DEV // CLUSTERS)
    keys = jax.random.split(jax.random.fold_in(key, 11), blocks)
    mixed = jax.vmap(lambda k: jax.random.permutation(k, base))(keys)
    return mixed.reshape(ROWS).astype(jnp.int32)


def draw_cluster_ids(key, part):
    return shared_ids(key)


def draw_embeddings(key, part):
    ids = shared_ids(key)
    centres = jax.random.normal(jax.random.fold_in(key, 7), (CLUSTERS, D), jnp.float32)
    noise = jax.random.normal(jax.random.fold_in(key, 13), (ROWS, D), jnp.float32)
    values = 0.8 * centres[ids] + 0.6 * noise
    return values.astype(jnp.bfloat16)


def setup_inputs(seed: int = 0) -> dict:
    key_of = jax.random.split(jax.random.key(seed), 3)
    embeddings = draw_embeddings(jax.random.fold_in(key_of[2], 71), 0)
    cluster_ids = draw_cluster_ids(jax.random.fold_in(key_of[2], 71), 0)
    return {"embeddings": embeddings, "cluster_ids": cluster_ids}


beta_scale = 16.0

def inverse_norms(embeddings):
    wide = embeddings.astype(jnp.float32)
    return lax.rsqrt(lax.optimization_barrier(jnp.sum(wide * wide, axis=1)) + 1e-06)

def reference(embeddings, cluster_ids):
    inv = inverse_norms(embeddings)
    block = math.gcd(ROWS, 2048)
    row_blocks = embeddings.reshape(ROWS // block, block, D)
    inv_blocks = inv.reshape(ROWS // block, block)
    id_blocks = cluster_ids.reshape(ROWS // block, block)

    def one_block(triple):
        rows, row_inv, row_ids = triple
        raw = jnp.dot(rows, embeddings.T, preferred_element_type=jnp.float32)
        sim = raw * row_inv[:, None] * inv[None, :]
        weight = jnp.where(row_ids[:, None] == cluster_ids[None, :], jnp.exp(beta_scale * (sim - 1.0)), jnp.float32(0.0))
        dens = lax.optimization_barrier(jnp.sum(weight, axis=1))
        coef = (weight * inv[None, :]).astype(jnp.bfloat16)
        total = jnp.dot(coef, embeddings, preferred_element_type=jnp.float32)
        return (total, dens)
    totals, denses = lax.map(one_block, (row_blocks, inv_blocks, id_blocks))
    return (totals.reshape(ROWS, D), denses.reshape(ROWS))
```

```python
import functools
import math

import jax
import jax.numpy as jnp
from jax import lax
from jax.experimental import pallas as pl
from jax.experimental.pallas import tpu as pltpu
from jax.sharding import PartitionSpec as P

beta_scale = 16.0
LANES = 128
VMEM = pl.BlockSpec(memory_space=pltpu.VMEM)
SMEM = pl.BlockSpec(memory_space=pltpu.SMEM)
GRANT = pltpu.CompilerParams(vmem_limit_bytes=40 * 1024 * 1024)


def placement(shift, ids, groups):
    count = ids.shape[1]
    first = lax.broadcasted_iota(jnp.int32, (count, count), 0)
    second = lax.broadcasted_iota(jnp.int32, (count, count), 1)
    turned = jnp.sum(jnp.where(first == second, ids, 0), axis=1, keepdims=True)
    earlier = jnp.where((turned == ids) & (first < second), 1, 0)
    rank = jnp.sum(earlier, axis=0, keepdims=True)
    place = ids - shift
    place = jnp.where(place < 0, place + groups, place)
    slot = place * (count // groups) + rank
    return jnp.where(first == slot, 1.0, 0.0).astype(jnp.bfloat16)


def sort_kernel(shift_ref, ids_ref, rows_ref, *out_refs):
    groups = len(out_refs)
    chosen = placement(shift_ref[0], ids_ref[...], groups)
    ordered = jnp.dot(chosen, rows_ref[...], preferred_element_type=jnp.float32)
    ordered = ordered.astype(jnp.bfloat16)
    size = ordered.shape[0] // groups
    for k, out_ref in enumerate(out_refs):
        out_ref[...] = ordered[k * size : (k + 1) * size, :]


def inverse_norms(rows):
    wide = rows.astype(jnp.float32)
    return lax.rsqrt(jnp.sum(wide * wide, axis=1, keepdims=True) + 1e-06)


def main_kernel(n_out, *refs):
    col_refs, out_refs = refs[:-n_out], refs[-n_out:]
    rows = col_refs[0][...]
    count, width = rows.shape
    scale = inverse_norms(rows) * (beta_scale * math.log2(math.e))
    first = lax.broadcasted_iota(jnp.int32, (count, count), 0)
    second = lax.broadcasted_iota(jnp.int32, (count, count), 1)
    total = jnp.zeros((count, width), jnp.float32)
    dens = jnp.zeros((count, LANES), jnp.float32)
    for col_ref in col_refs:
        cols = col_ref[...]
        col_inv = jnp.sum(
            jnp.where(first == second, inverse_norms(cols), 0.0), axis=0, keepdims=True
        )
        raw = lax.dot_general(
            rows, cols, (((1,), (1,)), ((), ())), preferred_element_type=jnp.float32
        )
        weight = jnp.exp2(raw * scale * col_inv - beta_scale * math.log2(math.e))
        for start in range(0, count, LANES):
            dens += weight[:, start : start + LANES]
        coef = (weight * col_inv).astype(jnp.bfloat16)
        total += jnp.dot(coef, cols, preferred_element_type=jnp.float32)
    dens = jnp.broadcast_to(jnp.sum(dens, axis=1, keepdims=True), dens.shape)
    size = count // n_out
    for k, out_ref in enumerate(out_refs):
        out_ref[:, :width] = total[k * size : (k + 1) * size, :]
        out_ref[:, width:] = dens[k * size : (k + 1) * size, :]


def restore_kernel(shift_ref, ids_ref, *refs):
    part_refs, (total_ref, dens_ref) = refs[:-2], refs[-2:]
    width = total_ref.shape[1]
    chosen = placement(shift_ref[0], ids_ref[...], len(part_refs))
    rest = jnp.concatenate([ref[...] for ref in part_refs], axis=0)
    back = jnp.zeros(rest.shape, jnp.float32)
    for _ in range(3):
        piece = rest.astype(jnp.bfloat16)
        rest = rest - piece.astype(jnp.float32)
        back += lax.dot_general(
            chosen, piece, (((0,), (0,)), ((), ())), preferred_element_type=jnp.float32
        )
    total_ref[...] = back[:, :width]
    first = lax.broadcasted_iota(jnp.int32, (LANES, LANES), 0)
    second = lax.broadcasted_iota(jnp.int32, (LANES, LANES), 1)
    for start in range(0, back.shape[0], LANES):
        dens = back[start : start + LANES, width:]
        dens_ref[:, start : start + LANES] = jnp.sum(
            jnp.where(first == second, dens, 0.0), axis=0, keepdims=True
        )


def on_device(n_gr, n_gc, embeddings, cluster_ids):
    count, width = embeddings.shape
    size = count // n_gr
    shift = lax.axis_index("gr").astype(jnp.int32).reshape(1)
    ids = cluster_ids.reshape(1, count)

    parts = pl.pallas_call(
        sort_kernel,
        out_shape=[jax.ShapeDtypeStruct((size, width), jnp.bfloat16)] * n_gr,
        in_specs=[SMEM, VMEM, VMEM],
        out_specs=[VMEM] * n_gr,
        compiler_params=GRANT,
        name="sort_rows",
    )(shift, ids, embeddings)

    def along_gr(part, step):
        pairs = [(i, (i + step) % n_gr) for i in range(n_gr)]
        return lax.ppermute(part, "gr", pairs)

    def along_gc(block, bits):
        return lax.ppermute(block, "gc", [(i, i ^ bits) for i in range(n_gc)])

    held = [parts[0]] + [along_gr(parts[k], k) for k in range(1, n_gr)]
    rows = jnp.concatenate(held, axis=0)
    same = [rows] + [along_gc(rows, bits) for bits in range(2, n_gc, 2)]
    other = [along_gc(block, 1) for block in same]

    sums = pl.pallas_call(
        functools.partial(main_kernel, n_gr),
        out_shape=[jax.ShapeDtypeStruct((size, width + LANES), jnp.float32)] * n_gr,
        in_specs=[VMEM] * n_gc,
        out_specs=[VMEM] * n_gr,
        compiler_params=GRANT,
        name="cluster_sums",
    )(*same, *other)

    back = [sums[0]] + [along_gr(sums[k], n_gr - k) for k in range(1, n_gr)]
    neighbour_sum, density = pl.pallas_call(
        restore_kernel,
        out_shape=[
            jax.ShapeDtypeStruct((count, width), jnp.float32),
            jax.ShapeDtypeStruct((1, count), jnp.float32),
        ],
        in_specs=[SMEM, VMEM] + [VMEM] * n_gr,
        out_specs=[VMEM, VMEM],
        compiler_params=GRANT,
        name="restore_rows",
    )(shift, ids, *back)
    return (neighbour_sum, density.reshape(count))


def solution(mesh):
    in_specs = (P(("gr", "gc"), None), P(("gr", "gc")))
    out_specs = (P(("gr", "gc"), None), P(("gr", "gc")))
    return jax.shard_map(
        functools.partial(on_device, mesh.shape["gr"], mesh.shape["gc"]),
        mesh=mesh,
        in_specs=in_specs,
        out_specs=out_specs,
        check_vma=False,
    )
```

```python
import functools
import math

import jax
import jax.numpy as jnp
from jax import lax
from jax.experimental import pallas as pl
from jax.experimental.pallas import tpu as pltpu
from jax.sharding import PartitionSpec as P

beta_scale = 16.0
LANES = 128
VMEM = pl.BlockSpec(memory_space=pltpu.VMEM)
SMEM = pl.BlockSpec(memory_space=pltpu.SMEM)
GRANT = pltpu.CompilerParams(vmem_limit_bytes=40 * 1024 * 1024)


def placement(own, ids, groups):
    count = ids.shape[1]
    first = lax.broadcasted_iota(jnp.int32, (count, count), 0)
    second = lax.broadcasted_iota(jnp.int32, (count, count), 1)
    turned = jnp.sum(jnp.where(first == second, ids, 0), axis=1, keepdims=True)
    earlier = jnp.where((turned == ids) & (first < second), 1, 0)
    rank = jnp.sum(earlier, axis=0, keepdims=True)
    slot = (ids ^ own) * (count // groups) + rank
    return jnp.where(first == slot, 1.0, 0.0).astype(jnp.bfloat16)


def sort_kernel(own_ref, ids_ref, rows_ref, *out_refs):
    groups = len(out_refs)
    chosen = placement(own_ref[0], ids_ref[...], groups)
    ordered = jnp.dot(chosen, rows_ref[...], preferred_element_type=jnp.float32)
    ordered = ordered.astype(jnp.bfloat16)
    size = ordered.shape[0] // groups
    for k, out_ref in enumerate(out_refs):
        out_ref[...] = ordered[k * size : (k + 1) * size, :]


def inverse_norms(rows):
    wide = rows.astype(jnp.float32)
    return lax.rsqrt(jnp.sum(wide * wide, axis=1, keepdims=True) + 1e-06)


def add_columns(rows, col_refs, total, dens):
    count = rows.shape[0]
    scale = inverse_norms(rows) * (beta_scale * math.log2(math.e))
    for col_ref in col_refs:
        cols = col_ref[...]
        size = cols.shape[0]
        first = lax.broadcasted_iota(jnp.int32, (size, size), 0)
        second = lax.broadcasted_iota(jnp.int32, (size, size), 1)
        col_inv = jnp.sum(
            jnp.where(first == second, inverse_norms(cols), 0.0), axis=0, keepdims=True
        )
        raw = lax.dot_general(
            rows, cols, (((1,), (1,)), ((), ())), preferred_element_type=jnp.float32
        )
        weight = jnp.exp2(raw * scale * col_inv - beta_scale * math.log2(math.e))
        for start in range(0, size, LANES):
            dens += weight[:, start : start + LANES]
        coef = (weight * col_inv).astype(jnp.bfloat16)
        total += jnp.dot(coef, cols, preferred_element_type=jnp.float32)
    return total, dens


def first_kernel(rows_ref, *refs):
    col_refs, (total_ref, dens_ref) = refs[:-2], refs[-2:]
    total = jnp.zeros(total_ref.shape, jnp.float32)
    dens = jnp.zeros(dens_ref.shape, jnp.float32)
    total, dens = add_columns(rows_ref[...], col_refs, total, dens)
    total_ref[...] = total
    dens_ref[...] = dens


def last_kernel(n_out, rows_ref, total_ref, dens_ref, *refs):
    col_refs, out_refs = refs[:-n_out], refs[-n_out:]
    count, width = rows_ref.shape
    total, dens = add_columns(rows_ref[...], col_refs, total_ref[...], dens_ref[...])
    dens = jnp.broadcast_to(jnp.sum(dens, axis=1, keepdims=True), dens.shape)
    size = count // n_out
    for k, out_ref in enumerate(out_refs):
        out_ref[:, :width] = total[k * size : (k + 1) * size, :]
        out_ref[:, width:] = dens[k * size : (k + 1) * size, :]


def restore_kernel(own_ref, ids_ref, *refs):
    part_refs, (total_ref, dens_ref) = refs[:-2], refs[-2:]
    width = total_ref.shape[1]
    chosen = placement(own_ref[0], ids_ref[...], len(part_refs))
    rest = jnp.concatenate([ref[...] for ref in part_refs], axis=0)
    back = jnp.zeros(rest.shape, jnp.float32)
    for _ in range(3):
        piece = rest.astype(jnp.bfloat16)
        rest = rest - piece.astype(jnp.float32)
        back += lax.dot_general(
            chosen, piece, (((0,), (0,)), ((), ())), preferred_element_type=jnp.float32
        )
    total_ref[...] = back[:, :width]
    first = lax.broadcasted_iota(jnp.int32, (LANES, LANES), 0)
    second = lax.broadcasted_iota(jnp.int32, (LANES, LANES), 1)
    for start in range(0, back.shape[0], LANES):
        dens = back[start : start + LANES, width:]
        dens_ref[:, start : start + LANES] = jnp.sum(
            jnp.where(first == second, dens, 0.0), axis=0, keepdims=True
        )


def on_device(n_gr, n_gc, embeddings, cluster_ids):
    count, width = embeddings.shape
    size = count // n_gr
    own = lax.axis_index("gr").astype(jnp.int32).reshape(1)
    ids = cluster_ids.reshape(1, count)

    parts = pl.pallas_call(
        sort_kernel,
        out_shape=[jax.ShapeDtypeStruct((size, width), jnp.bfloat16)] * n_gr,
        in_specs=[SMEM, VMEM, VMEM],
        out_specs=[VMEM] * n_gr,
        compiler_params=GRANT,
        name="sort_rows",
    )(own, ids, embeddings)

    def along_gr(part, bits):
        return lax.ppermute(part, "gr", [(i, i ^ bits) for i in range(n_gr)])

    def along_gc(block, bits):
        return lax.ppermute(block, "gc", [(i, i ^ bits) for i in range(n_gc)])

    def cost(pairs):
        return pl.CostEstimate(
            flops=4 * pairs * width,
            bytes_accessed=0,
            transcendentals=pairs,
        )

    held = [parts[0]] + [along_gr(parts[k], k) for k in range(1, n_gr)]
    chunks = []
    for piece in held:
        near = [piece] + [along_gc(piece, bits) for bits in range(2, n_gc, 2)]
        same = jnp.concatenate(near, axis=0)
        chunks.append((same, along_gc(same, 1)))
    rows = jnp.concatenate(held, axis=0)
    early = [cols for chunk in chunks[:-1] for cols in chunk]

    total, dens = pl.pallas_call(
        first_kernel,
        out_shape=[
            jax.ShapeDtypeStruct((count, width), jnp.float32),
            jax.ShapeDtypeStruct((count, LANES), jnp.float32),
        ],
        in_specs=[VMEM] * (1 + len(early)),
        out_specs=[VMEM] * 2,
        compiler_params=GRANT,
        cost_estimate=cost(count * size * n_gc * (n_gr - 1)),
        name="early_sums",
    )(rows, *early)
    sums = pl.pallas_call(
        functools.partial(last_kernel, n_gr),
        out_shape=[jax.ShapeDtypeStruct((size, width + LANES), jnp.float32)] * n_gr,
        in_specs=[VMEM] * 5,
        out_specs=[VMEM] * n_gr,
        compiler_params=GRANT,
        cost_estimate=cost(count * size * n_gc),
        name="last_sums",
    )(rows, total, dens, *chunks[-1])

    back = [sums[0]] + [along_gr(sums[k], k) for k in range(1, n_gr)]
    neighbour_sum, density = pl.pallas_call(
        restore_kernel,
        out_shape=[
            jax.ShapeDtypeStruct((count, width), jnp.float32),
            jax.ShapeDtypeStruct((1, count), jnp.float32),
        ],
        in_specs=[SMEM, VMEM] + [VMEM] * n_gr,
        out_specs=[VMEM, VMEM],
        compiler_params=GRANT,
        name="restore_rows",
    )(own, ids, *back)
    return (neighbour_sum, density.reshape(count))


def solution(mesh):
    in_specs = (P(("gr", "gc"), None), P(("gr", "gc")))
    out_specs = (P(("gr", "gc"), None), P(("gr", "gc")))
    return jax.shard_map(
        functools.partial(on_device, mesh.shape["gr"], mesh.shape["gc"]),
        mesh=mesh,
        in_specs=in_specs,
        out_specs=out_specs,
        check_vma=False,
    )
```

```python
import functools
import math

import jax
import jax.numpy as jnp
from jax import lax
from jax.experimental import pallas as pl
from jax.experimental.pallas import tpu as pltpu
from jax.sharding import PartitionSpec as P

beta_scale = 16.0
LANES = 128
VMEM = pl.BlockSpec(memory_space=pltpu.VMEM)
SMEM = pl.BlockSpec(memory_space=pltpu.SMEM)
GRANT = pltpu.CompilerParams(vmem_limit_bytes=40 * 1024 * 1024)


def placement(own, ids, groups):
    count = ids.shape[1]
    first = lax.broadcasted_iota(jnp.int32, (count, count), 0)
    second = lax.broadcasted_iota(jnp.int32, (count, count), 1)
    turned = jnp.sum(jnp.where(first == second, ids, 0), axis=1, keepdims=True)
    earlier = jnp.where((turned == ids) & (first < second), 1, 0)
    rank = jnp.sum(earlier, axis=0, keepdims=True)
    slot = (ids ^ own) * (count // groups) + rank
    return jnp.where(first == slot, 1.0, 0.0).astype(jnp.bfloat16)


def sort_kernel(own_ref, ids_ref, rows_ref, *out_refs):
    groups = len(out_refs)
    chosen = placement(own_ref[0], ids_ref[...], groups)
    ordered = jnp.dot(chosen, rows_ref[...], preferred_element_type=jnp.float32)
    ordered = ordered.astype(jnp.bfloat16)
    size = ordered.shape[0] // groups
    for k, out_ref in enumerate(out_refs):
        out_ref[...] = ordered[k * size : (k + 1) * size, :]


def inverse_norms(rows):
    wide = rows.astype(jnp.float32)
    return lax.rsqrt(jnp.sum(wide * wide, axis=1, keepdims=True) + 1e-06)


def add_columns(rows, col_refs, total, dens):
    count = rows.shape[0]
    scale = inverse_norms(rows) * (beta_scale * math.log2(math.e))
    blocks = [
        (col_ref, start)
        for col_ref in col_refs
        for start in range(0, col_ref.shape[0], count)
    ]
    for col_ref, start in blocks:
        cols = col_ref[start : start + count, :]
        size = cols.shape[0]
        first = lax.broadcasted_iota(jnp.int32, (size, size), 0)
        second = lax.broadcasted_iota(jnp.int32, (size, size), 1)
        col_inv = jnp.sum(
            jnp.where(first == second, inverse_norms(cols), 0.0), axis=0, keepdims=True
        )
        raw = lax.dot_general(
            rows, cols, (((1,), (1,)), ((), ())), preferred_element_type=jnp.float32
        )
        weight = jnp.exp2(raw * scale * col_inv - beta_scale * math.log2(math.e))
        for lane in range(0, size, LANES):
            dens += weight[:, lane : lane + LANES]
        coef = (weight * col_inv).astype(jnp.bfloat16)
        total += jnp.dot(coef, cols, preferred_element_type=jnp.float32)
    return total, dens


def first_kernel(rows_ref, *refs):
    col_refs, (total_ref, dens_ref) = refs[:-2], refs[-2:]
    total = jnp.zeros(total_ref.shape, jnp.float32)
    dens = jnp.zeros(dens_ref.shape, jnp.float32)
    total, dens = add_columns(rows_ref[...], col_refs, total, dens)
    total_ref[...] = total
    dens_ref[...] = dens


def last_kernel(n_out, rows_ref, total_ref, dens_ref, *refs):
    col_refs, out_refs = refs[:-n_out], refs[-n_out:]
    count, width = rows_ref.shape
    total, dens = add_columns(rows_ref[...], col_refs, total_ref[...], dens_ref[...])
    dens = jnp.broadcast_to(jnp.sum(dens, axis=1, keepdims=True), dens.shape)
    size = count // n_out
    for k, out_ref in enumerate(out_refs):
        out_ref[:, :width] = total[k * size : (k + 1) * size, :]
        out_ref[:, width:] = dens[k * size : (k + 1) * size, :]


def restore_kernel(own_ref, ids_ref, *refs):
    part_refs, (total_ref, dens_ref) = refs[:-2], refs[-2:]
    width = total_ref.shape[1]
    chosen = placement(own_ref[0], ids_ref[...], len(part_refs))
    rest = jnp.concatenate([ref[...] for ref in part_refs], axis=0)
    back = jnp.zeros(rest.shape, jnp.float32)
    for _ in range(3):
        piece = rest.astype(jnp.bfloat16)
        rest = rest - piece.astype(jnp.float32)
        back += lax.dot_general(
            chosen, piece, (((0,), (0,)), ((), ())), preferred_element_type=jnp.float32
        )
    total_ref[...] = back[:, :width]
    first = lax.broadcasted_iota(jnp.int32, (LANES, LANES), 0)
    second = lax.broadcasted_iota(jnp.int32, (LANES, LANES), 1)
    for start in range(0, back.shape[0], LANES):
        dens = back[start : start + LANES, width:]
        dens_ref[:, start : start + LANES] = jnp.sum(
            jnp.where(first == second, dens, 0.0), axis=0, keepdims=True
        )


def on_device(n_gr, n_gc, embeddings, cluster_ids):
    count, width = embeddings.shape
    size = count // n_gr
    own = lax.axis_index("gr").astype(jnp.int32).reshape(1)
    ids = cluster_ids.reshape(1, count)

    parts = pl.pallas_call(
        sort_kernel,
        out_shape=[jax.ShapeDtypeStruct((size, width), jnp.bfloat16)] * n_gr,
        in_specs=[SMEM, VMEM, VMEM],
        out_specs=[VMEM] * n_gr,
        compiler_params=GRANT,
        name="sort_rows",
    )(own, ids, embeddings)

    def along_gr(part, bits):
        return lax.ppermute(part, "gr", [(i, i ^ bits) for i in range(n_gr)])

    bits = [1 << k for k in range(1, n_gc.bit_length() - 1)]

    def in_plane(block, step):
        pairs = [(i, i ^ bits[(step + i % 2) % len(bits)]) for i in range(n_gc)]
        return lax.ppermute(block, "gc", pairs)

    def other_core(block):
        return lax.ppermute(block, "gc", [(i, i ^ 1) for i in range(n_gc)])

    def cost(pairs):
        return pl.CostEstimate(
            flops=4 * pairs * width,
            bytes_accessed=0,
            transcendentals=pairs,
        )

    held = [parts[0]] + [along_gr(parts[k], k) for k in range(1, n_gr)]
    half = n_gr // 2
    first = jnp.concatenate(held[:half], axis=0)
    for step in range(len(bits)):
        first = jnp.concatenate([first, in_plane(first, step)], axis=0)
    second = jnp.concatenate(held[half:], axis=0)
    for step in range(len(bits) - 1):
        second = jnp.concatenate([second, in_plane(second, step)], axis=0)
    third = in_plane(second, len(bits) - 1)
    rows = jnp.concatenate(held, axis=0)
    early = [first, other_core(first), second, other_core(second)]

    total, dens = pl.pallas_call(
        first_kernel,
        out_shape=[
            jax.ShapeDtypeStruct((count, width), jnp.float32),
            jax.ShapeDtypeStruct((count, LANES), jnp.float32),
        ],
        in_specs=[VMEM] * (1 + len(early)),
        out_specs=[VMEM] * 2,
        compiler_params=GRANT,
        cost_estimate=cost(count * sum(cols.shape[0] for cols in early)),
        name="early_sums",
    )(rows, *early)
    third, total = lax.optimization_barrier((third, total))
    late = [third, other_core(third)]
    sums = pl.pallas_call(
        functools.partial(last_kernel, n_gr),
        out_shape=[jax.ShapeDtypeStruct((size, width + LANES), jnp.float32)] * n_gr,
        in_specs=[VMEM] * (3 + len(late)),
        out_specs=[VMEM] * n_gr,
        compiler_params=GRANT,
        cost_estimate=cost(count * sum(cols.shape[0] for cols in late)),
        name="last_sums",
    )(rows, total, dens, *late)

    back = [sums[0]] + [along_gr(sums[k], k) for k in range(1, n_gr)]
    neighbour_sum, density = pl.pallas_call(
        restore_kernel,
        out_shape=[
            jax.ShapeDtypeStruct((count, width), jnp.float32),
            jax.ShapeDtypeStruct((1, count), jnp.float32),
        ],
        in_specs=[SMEM, VMEM] + [VMEM] * n_gr,
        out_specs=[VMEM, VMEM],
        compiler_params=GRANT,
        name="restore_rows",
    )(own, ids, *back)
    return (neighbour_sum, density.reshape(count))


def solution(mesh):
    in_specs = (P(("gr", "gc"), None), P(("gr", "gc")))
    out_specs = (P(("gr", "gc"), None), P(("gr", "gc")))
    return jax.shard_map(
        functools.partial(on_device, mesh.shape["gr"], mesh.shape["gc"]),
        mesh=mesh,
        in_specs=in_specs,
        out_specs=out_specs,
        check_vma=False,
    )
```

```python
import functools
import math

import jax
import jax.numpy as jnp
from jax import lax
from jax.experimental import pallas as pl
from jax.experimental.pallas import tpu as pltpu
from jax.sharding import PartitionSpec as P

beta_scale = 16.0
LANES = 128
EXTRA = 8
TOP = 14.0
VMEM = pl.BlockSpec(memory_space=pltpu.VMEM)
SMEM = pl.BlockSpec(memory_space=pltpu.SMEM)
GRANT = pltpu.CompilerParams(vmem_limit_bytes=40 * 1024 * 1024)


def diagonal(count):
    first = lax.broadcasted_iota(jnp.int32, (count, count), 0)
    second = lax.broadcasted_iota(jnp.int32, (count, count), 1)
    return first == second


def as_row(column):
    return jnp.sum(
        jnp.where(diagonal(column.shape[0]), column, jnp.zeros_like(column)),
        axis=0,
        keepdims=True,
    )


def as_column(row):
    return jnp.sum(
        jnp.where(diagonal(row.shape[1]), row, jnp.zeros_like(row)),
        axis=1,
        keepdims=True,
    )


def placement(own, ids, groups):
    count = ids.shape[1]
    first = lax.broadcasted_iota(jnp.int32, (count, count), 0)
    second = lax.broadcasted_iota(jnp.int32, (count, count), 1)
    earlier = jnp.where((as_column(ids) == ids) & (first < second), 1, 0)
    rank = jnp.sum(earlier, axis=0, keepdims=True)
    slot = (ids ^ own) * (count // groups) + rank
    return jnp.where(first == slot, 1.0, 0.0)


def sort_kernel(own_ref, ids_ref, rows_ref, *out_refs):
    groups = len(out_refs)
    chosen = placement(own_ref[0], ids_ref[...], groups).astype(jnp.bfloat16)
    ordered = jnp.dot(chosen, rows_ref[...], preferred_element_type=jnp.float32)
    ordered = ordered.astype(jnp.bfloat16)
    size = ordered.shape[0] // groups
    for k, out_ref in enumerate(out_refs):
        out_ref[...] = ordered[k * size : (k + 1) * size, :]


def inverse_norms(rows):
    wide = rows.astype(jnp.float32)
    return lax.rsqrt(jnp.sum(wide * wide, axis=1, keepdims=True) + 1e-06)


def add_columns(rows, col_refs, total, dens):
    count = rows.shape[0]
    scale = inverse_norms(rows) * (beta_scale * math.log2(math.e))
    blocks = [
        (col_ref, start)
        for col_ref in col_refs
        for start in range(0, col_ref.shape[0], count)
    ]
    for col_ref, start in blocks:
        cols = col_ref[start : start + count, :]
        col_inv = as_row(inverse_norms(cols))
        raw = lax.dot_general(
            rows, cols, (((1,), (1,)), ((), ())), preferred_element_type=jnp.float32
        )
        weight = jnp.exp2(raw * scale * col_inv - beta_scale * math.log2(math.e))
        for lane in range(0, count, LANES):
            dens += weight[:, lane : lane + LANES]
        coef = (weight * col_inv).astype(jnp.bfloat16)
        total += jnp.dot(coef, cols, preferred_element_type=jnp.float32)
    return total, dens


def first_kernel(rows_ref, *refs):
    col_refs, (total_ref, dens_ref) = refs[:-2], refs[-2:]
    total = jnp.zeros(total_ref.shape, jnp.float32)
    dens = jnp.zeros(dens_ref.shape, jnp.float32)
    total, dens = add_columns(rows_ref[...], col_refs, total, dens)
    total_ref[...] = total
    dens_ref[...] = dens


def exponent(value):
    return jnp.floor(jnp.log2(jnp.maximum(value, 1e-37)))


def last_kernel(own_ref, rows_ref, total_ref, dens_ref, *refs):
    col_refs, out_ref = refs[:-1], refs[-1]
    groups, padded, width = out_ref.shape
    size = padded - EXTRA
    total, dens = add_columns(rows_ref[...], col_refs, total_ref[...], dens_ref[...])
    dens = jnp.sum(dens, axis=1, keepdims=True)
    power = exponent(jnp.max(jnp.abs(total), axis=1, keepdims=True))
    total = total * jnp.exp2(TOP - power)
    dens_power = exponent(dens)
    part = dens * jnp.exp2(-dens_power)
    aside = [power, dens_power]
    for k in range(3):
        piece = part.astype(jnp.bfloat16).astype(jnp.float32)
        aside.append(piece * 2.0 ** (8 * k))
        part = part - piece
    for k in range(groups):
        slot = own_ref[0] ^ k
        rows = slice(k * size, (k + 1) * size)
        out_ref[slot, :size, :] = total[rows, :]
        out_ref[slot, size:, :] = jnp.zeros((EXTRA, width), jnp.float32)
        for line, column in enumerate(aside):
            out_ref[slot, size + line : size + line + 1, :size] = as_row(column[rows, :])


def restore_kernel(ids_ref, parts_ref, total_ref, dens_ref):
    groups, padded, width = parts_ref.shape
    size = padded - EXTRA
    chosen = placement(0, ids_ref[...], groups)
    sums, dens = [], []
    for k in range(groups):
        power, dens_power, *pieces = [
            as_column(parts_ref[k, size + line : size + line + 1, :size])
            for line in range(5)
        ]
        sums.append(parts_ref[k, :size, :] * jnp.exp2(power - TOP))
        part = sum(piece * 2.0 ** (-8 * j) for j, piece in enumerate(pieces))
        dens.append(part * jnp.exp2(dens_power))
    dens_ref[...] = jnp.sum(
        chosen * jnp.concatenate(dens, axis=0), axis=0, keepdims=True
    )
    rest = jnp.concatenate(sums, axis=0)
    chosen = chosen.astype(jnp.bfloat16)
    back = jnp.zeros(rest.shape, jnp.float32)
    for _ in range(2):
        piece = rest.astype(jnp.bfloat16)
        rest = rest - piece.astype(jnp.float32)
        back += lax.dot_general(
            chosen, piece, (((0,), (0,)), ((), ())), preferred_element_type=jnp.float32
        )
    total_ref[...] = back


def on_device(n_gr, n_gc, embeddings, cluster_ids):
    count, width = embeddings.shape
    size = count // n_gr
    own = lax.axis_index("gr").astype(jnp.int32).reshape(1)
    ids = cluster_ids.reshape(1, count)

    parts = pl.pallas_call(
        sort_kernel,
        out_shape=[jax.ShapeDtypeStruct((size, width), jnp.bfloat16)] * n_gr,
        in_specs=[SMEM, VMEM, VMEM],
        out_specs=[VMEM] * n_gr,
        compiler_params=GRANT,
        name="sort_rows",
    )(own, ids, embeddings)

    def along_gr(part, bits):
        return lax.ppermute(part, "gr", [(i, i ^ bits) for i in range(n_gr)])

    def along_gc(block, bits):
        return lax.ppermute(block, "gc", [(i, i ^ bits) for i in range(n_gc)])

    def cost(pairs):
        return pl.CostEstimate(
            flops=4 * pairs * width,
            bytes_accessed=0,
            transcendentals=pairs,
        )

    held = [parts[0]] + [along_gr(parts[k], k) for k in range(1, n_gr)]
    half = n_gr // 2
    chunks = []
    for pieces in (held[:half], held[half:]):
        block = jnp.concatenate(pieces, axis=0)
        near = [block] + [along_gc(block, bits) for bits in range(2, n_gc, 2)]
        same = jnp.concatenate(near, axis=0)
        chunks.append([same, along_gc(same, 1)])
    rows = jnp.concatenate(held, axis=0)

    total, dens = pl.pallas_call(
        first_kernel,
        out_shape=[
            jax.ShapeDtypeStruct((count, width), jnp.float32),
            jax.ShapeDtypeStruct((count, LANES), jnp.float32),
        ],
        in_specs=[VMEM] * 3,
        out_specs=[VMEM] * 2,
        compiler_params=GRANT,
        cost_estimate=cost(count * count * n_gc // 2),
        name="early_sums",
    )(rows, *chunks[0])
    sums = pl.pallas_call(
        last_kernel,
        out_shape=jax.ShapeDtypeStruct((n_gr, size + EXTRA, width), jnp.float32),
        in_specs=[SMEM] + [VMEM] * 5,
        out_specs=VMEM,
        compiler_params=GRANT,
        cost_estimate=cost(count * count * n_gc // 2),
        name="last_sums",
    )(own, rows, total, dens, *chunks[1])

    back = lax.all_to_all(sums.astype(jnp.float16), "gr", 0, 0)
    neighbour_sum, density = pl.pallas_call(
        restore_kernel,
        out_shape=[
            jax.ShapeDtypeStruct((count, width), jnp.float32),
            jax.ShapeDtypeStruct((1, count), jnp.float32),
        ],
        in_specs=[VMEM, VMEM],
        out_specs=[VMEM, VMEM],
        compiler_params=GRANT,
        name="restore_rows",
    )(ids, back.astype(jnp.float32))
    return (neighbour_sum, density.reshape(count))


def solution(mesh):
    in_specs = (P(("gr", "gc"), None), P(("gr", "gc")))
    out_specs = (P(("gr", "gc"), None), P(("gr", "gc")))
    return jax.shard_map(
        functools.partial(on_device, mesh.shape["gr"], mesh.shape["gc"]),
        mesh=mesh,
        in_specs=in_specs,
        out_specs=out_specs,
        check_vma=False,
    )
```

```python
import functools
import math

import jax
import jax.numpy as jnp
from jax import lax
from jax.experimental import pallas as pl
from jax.experimental.pallas import tpu as pltpu
from jax.sharding import PartitionSpec as P

beta_scale = 16.0
LANES = 128
EXTRA = 8
TOP = 14.0
VMEM = pl.BlockSpec(memory_space=pltpu.VMEM)
SMEM = pl.BlockSpec(memory_space=pltpu.SMEM)
GRANT = pltpu.CompilerParams(vmem_limit_bytes=40 * 1024 * 1024)


def diagonal(count):
    first = lax.broadcasted_iota(jnp.int32, (count, count), 0)
    second = lax.broadcasted_iota(jnp.int32, (count, count), 1)
    return first == second


def as_row(column):
    return jnp.sum(
        jnp.where(diagonal(column.shape[0]), column, jnp.zeros_like(column)),
        axis=0,
        keepdims=True,
    )


def as_column(row):
    return jnp.sum(
        jnp.where(diagonal(row.shape[1]), row, jnp.zeros_like(row)),
        axis=1,
        keepdims=True,
    )


def placement(own, ids, groups):
    count = ids.shape[1]
    first = lax.broadcasted_iota(jnp.int32, (count, count), 0)
    second = lax.broadcasted_iota(jnp.int32, (count, count), 1)
    earlier = jnp.where((as_column(ids) == ids) & (first < second), 1, 0)
    rank = jnp.sum(earlier, axis=0, keepdims=True)
    slot = (ids ^ own) * (count // groups) + rank
    return jnp.where(first == slot, 1.0, 0.0)


def sort_kernel(own_ref, ids_ref, rows_ref, *out_refs):
    groups = len(out_refs)
    chosen = placement(own_ref[0], ids_ref[...], groups).astype(jnp.bfloat16)
    ordered = jnp.dot(chosen, rows_ref[...], preferred_element_type=jnp.float32)
    ordered = ordered.astype(jnp.bfloat16)
    size = ordered.shape[0] // groups
    for k, out_ref in enumerate(out_refs):
        out_ref[...] = ordered[k * size : (k + 1) * size, :]


def inverse_norms(rows):
    wide = rows.astype(jnp.float32)
    return lax.rsqrt(jnp.sum(wide * wide, axis=1, keepdims=True) + 1e-06)


def add_columns(rows, col_refs, total, dens):
    count = rows.shape[0]
    scale = inverse_norms(rows) * (beta_scale * math.log2(math.e))
    blocks = [
        (col_ref, start)
        for col_ref in col_refs
        for start in range(0, col_ref.shape[0], count)
    ]
    for col_ref, start in blocks:
        cols = col_ref[start : start + count, :]
        col_inv = as_row(inverse_norms(cols))
        raw = lax.dot_general(
            rows, cols, (((1,), (1,)), ((), ())), preferred_element_type=jnp.float32
        )
        weight = jnp.exp2(raw * scale * col_inv - beta_scale * math.log2(math.e))
        for lane in range(0, count, LANES):
            dens += weight[:, lane : lane + LANES]
        coef = (weight * col_inv).astype(jnp.bfloat16)
        total += jnp.dot(coef, cols, preferred_element_type=jnp.float32)
    return total, dens


def first_kernel(rows_ref, *refs):
    col_refs, (total_ref, dens_ref) = refs[:-2], refs[-2:]
    total = jnp.zeros(total_ref.shape, jnp.float32)
    dens = jnp.zeros(dens_ref.shape, jnp.float32)
    total, dens = add_columns(rows_ref[...], col_refs, total, dens)
    total_ref[...] = total
    dens_ref[...] = dens


def exponent(value):
    return jnp.floor(jnp.log2(jnp.maximum(value, 1e-37)))


def last_kernel(groups, rows_ref, total_ref, dens_ref, *refs):
    col_refs, out_refs = refs[:-groups], refs[-groups:]
    padded, width = out_refs[0].shape
    size = padded - EXTRA
    total, dens = add_columns(rows_ref[...], col_refs, total_ref[...], dens_ref[...])
    dens = jnp.sum(dens, axis=1, keepdims=True)
    power = exponent(jnp.max(jnp.abs(total), axis=1, keepdims=True))
    total = total * jnp.exp2(TOP - power)
    dens_power = exponent(dens)
    part = dens * jnp.exp2(-dens_power)
    aside = [power, dens_power]
    for k in range(3):
        piece = part.astype(jnp.bfloat16).astype(jnp.float32)
        aside.append(piece * 2.0 ** (8 * k))
        part = part - piece
    for k, out_ref in enumerate(out_refs):
        rows = slice(k * size, (k + 1) * size)
        out_ref[:size, :] = total[rows, :]
        out_ref[size:, :] = jnp.zeros((EXTRA, width), jnp.float32)
        for line, column in enumerate(aside):
            out_ref[size + line : size + line + 1, :size] = as_row(column[rows, :])


def restore_kernel(own_ref, ids_ref, *refs):
    part_refs, (total_ref, dens_ref) = refs[:-2], refs[-2:]
    groups = len(part_refs)
    size = part_refs[0].shape[0] - EXTRA
    chosen = placement(own_ref[0], ids_ref[...], groups)
    sums, dens = [], []
    for part_ref in part_refs:
        power, dens_power, *pieces = [
            as_column(part_ref[size + line : size + line + 1, :size])
            for line in range(5)
        ]
        sums.append(part_ref[:size, :] * jnp.exp2(power - TOP))
        part = sum(piece * 2.0 ** (-8 * j) for j, piece in enumerate(pieces))
        dens.append(part * jnp.exp2(dens_power))
    dens_ref[...] = jnp.sum(
        chosen * jnp.concatenate(dens, axis=0), axis=0, keepdims=True
    )
    rest = jnp.concatenate(sums, axis=0)
    chosen = chosen.astype(jnp.bfloat16)
    back = jnp.zeros(rest.shape, jnp.float32)
    for _ in range(2):
        piece = rest.astype(jnp.bfloat16)
        rest = rest - piece.astype(jnp.float32)
        back += lax.dot_general(
            chosen, piece, (((0,), (0,)), ((), ())), preferred_element_type=jnp.float32
        )
    total_ref[...] = back


def on_device(n_gr, n_gc, embeddings, cluster_ids):
    count, width = embeddings.shape
    size = count // n_gr
    own = lax.axis_index("gr").astype(jnp.int32).reshape(1)
    ids = cluster_ids.reshape(1, count)

    parts = pl.pallas_call(
        sort_kernel,
        out_shape=[jax.ShapeDtypeStruct((size, width), jnp.bfloat16)] * n_gr,
        in_specs=[SMEM, VMEM, VMEM],
        out_specs=[VMEM] * n_gr,
        compiler_params=GRANT,
        name="sort_rows",
    )(own, ids, embeddings)

    def along_gr(part, bits):
        return lax.ppermute(part, "gr", [(i, i ^ bits) for i in range(n_gr)])

    bits = [1 << k for k in range(1, n_gc.bit_length() - 1)]

    def in_plane(block, step):
        pairs = [(i, i ^ bits[(step + i % 2) % len(bits)]) for i in range(n_gc)]
        return lax.ppermute(block, "gc", pairs)

    def other_core(block):
        return lax.ppermute(block, "gc", [(i, i ^ 1) for i in range(n_gc)])

    def doubled(block, steps):
        for step in range(steps):
            block = jnp.concatenate([block, in_plane(block, step)], axis=0)
        return block

    def cost(*blocks):
        pairs = count * sum(block.shape[0] for block in blocks)
        return pl.CostEstimate(
            flops=4 * pairs * width,
            bytes_accessed=0,
            transcendentals=pairs,
        )

    held = [None] * n_gr
    held[0] = parts[0]
    for k in sorted(range(1, n_gr), reverse=True):
        held[k] = along_gr(parts[k], k)
    start = doubled(held[0], len(bits))
    second = doubled(held[1], len(bits) - 1)
    second, others = lax.optimization_barrier((second, held[2:]))
    second = jnp.concatenate([second, in_plane(second, len(bits) - 1)], axis=0)
    start = jnp.concatenate([start, second], axis=0)
    rest = doubled(jnp.concatenate(others, axis=0), len(bits) - 1)
    last = in_plane(rest, len(bits) - 1)
    rows = jnp.concatenate(held, axis=0)
    near = jnp.concatenate([start, rest], axis=0)
    early = [near, other_core(near)]

    total, dens = pl.pallas_call(
        first_kernel,
        out_shape=[
            jax.ShapeDtypeStruct((count, width), jnp.float32),
            jax.ShapeDtypeStruct((count, LANES), jnp.float32),
        ],
        in_specs=[VMEM] * (1 + len(early)),
        out_specs=[VMEM] * 2,
        compiler_params=GRANT,
        cost_estimate=cost(*early),
        name="early_sums",
    )(rows, *early)
    last, total = lax.optimization_barrier((last, total))
    late = [last, other_core(last)]
    sums = pl.pallas_call(
        functools.partial(last_kernel, n_gr),
        out_shape=[jax.ShapeDtypeStruct((size + EXTRA, width), jnp.float32)] * n_gr,
        in_specs=[VMEM] * 5,
        out_specs=[VMEM] * n_gr,
        compiler_params=GRANT,
        cost_estimate=cost(*late),
        name="last_sums",
    )(rows, total, dens, *late)

    sent = [part.astype(jnp.float16) for part in sums]
    back = [None] * n_gr
    back[0] = sent[0]
    for k in sorted(range(1, n_gr), reverse=True):
        back[k] = along_gr(sent[k], k)
    back = [part.astype(jnp.float32) for part in back]
    neighbour_sum, density = pl.pallas_call(
        restore_kernel,
        out_shape=[
            jax.ShapeDtypeStruct((count, width), jnp.float32),
            jax.ShapeDtypeStruct((1, count), jnp.float32),
        ],
        in_specs=[SMEM, VMEM] + [VMEM] * n_gr,
        out_specs=[VMEM, VMEM],
        compiler_params=GRANT,
        name="restore_rows",
    )(own, ids, *back)
    return (neighbour_sum, density.reshape(count))


def solution(mesh):
    in_specs = (P(("gr", "gc"), None), P(("gr", "gc")))
    out_specs = (P(("gr", "gc"), None), P(("gr", "gc")))
    return jax.shard_map(
        functools.partial(on_device, mesh.shape["gr"], mesh.shape["gc"]),
        mesh=mesh,
        in_specs=in_specs,
        out_specs=out_specs,
        check_vma=False,
    )
```

```python
import functools
import math

import jax
import jax.numpy as jnp
from jax import lax
from jax.experimental import pallas as pl
from jax.experimental.pallas import tpu as pltpu
from jax.sharding import PartitionSpec as P

beta_scale = 16.0
LANES = 128
EXTRA = 8
TOP = 14.0
VMEM = pl.BlockSpec(memory_space=pltpu.VMEM)
SMEM = pl.BlockSpec(memory_space=pltpu.SMEM)
GRANT = pltpu.CompilerParams(vmem_limit_bytes=40 * 1024 * 1024)


def diagonal(count):
    first = lax.broadcasted_iota(jnp.int32, (count, count), 0)
    second = lax.broadcasted_iota(jnp.int32, (count, count), 1)
    return first == second


def as_row(column):
    return jnp.sum(
        jnp.where(diagonal(column.shape[0]), column, jnp.zeros_like(column)),
        axis=0,
        keepdims=True,
    )


def as_column(row):
    return jnp.sum(
        jnp.where(diagonal(row.shape[1]), row, jnp.zeros_like(row)),
        axis=1,
        keepdims=True,
    )


def placement(own, ids, groups):
    count = ids.shape[1]
    first = lax.broadcasted_iota(jnp.int32, (count, count), 0)
    second = lax.broadcasted_iota(jnp.int32, (count, count), 1)
    earlier = jnp.where((as_column(ids) == ids) & (first < second), 1, 0)
    rank = jnp.sum(earlier, axis=0, keepdims=True)
    slot = (ids ^ own) * (count // groups) + rank
    return jnp.where(first == slot, 1.0, 0.0)


def sort_kernel(own_ref, ids_ref, rows_ref, *out_refs):
    groups = len(out_refs)
    chosen = placement(own_ref[0], ids_ref[...], groups).astype(jnp.bfloat16)
    ordered = jnp.dot(chosen, rows_ref[...], preferred_element_type=jnp.float32)
    ordered = ordered.astype(jnp.bfloat16)
    size = ordered.shape[0] // groups
    for k, out_ref in enumerate(out_refs[::-1]):
        out_ref[...] = ordered[k * size : (k + 1) * size, :]


def inverse_norms(rows):
    wide = rows.astype(jnp.float32)
    return lax.rsqrt(jnp.sum(wide * wide, axis=1, keepdims=True) + 1e-06)


def add_columns(rows, col_refs, total, dens):
    count = rows.shape[0]
    scale = inverse_norms(rows) * (beta_scale * math.log2(math.e))
    blocks = [
        (col_ref, start)
        for col_ref in col_refs
        for start in range(0, col_ref.shape[0], count)
    ]
    for col_ref, start in blocks:
        cols = col_ref[start : min(start + count, col_ref.shape[0]), :]
        size = cols.shape[0]
        col_inv = as_row(inverse_norms(cols))
        raw = lax.dot_general(
            rows, cols, (((1,), (1,)), ((), ())), preferred_element_type=jnp.float32
        )
        weight = jnp.exp2(raw * scale * col_inv - beta_scale * math.log2(math.e))
        whole = size - size % LANES
        for lane in range(0, whole, LANES):
            dens += weight[:, lane : lane + LANES]
        if whole < size:
            part = jnp.sum(weight[:, whole:], axis=1, keepdims=True)
            dens += jnp.where(lax.broadcasted_iota(jnp.int32, dens.shape, 1) == 0, part, 0.0)
        coef = (weight * col_inv).astype(jnp.bfloat16)
        total += jnp.dot(coef, cols, preferred_element_type=jnp.float32)
    return total, dens


def first_kernel(rows_ref, *refs):
    col_refs, (total_ref, dens_ref) = refs[:-2], refs[-2:]
    total = jnp.zeros(total_ref.shape, jnp.float32)
    dens = jnp.zeros(dens_ref.shape, jnp.float32)
    total, dens = add_columns(rows_ref[...], col_refs, total, dens)
    total_ref[...] = total
    dens_ref[...] = dens


def exponent(value):
    return jnp.floor(jnp.log2(jnp.maximum(value, 1e-37)))


def last_kernel(groups, rows_ref, total_ref, dens_ref, *refs):
    col_refs, out_refs = refs[:-groups], refs[-groups:]
    padded, width = out_refs[0].shape
    size = padded - EXTRA
    total, dens = add_columns(rows_ref[...], col_refs, total_ref[...], dens_ref[...])
    dens = jnp.sum(dens, axis=1, keepdims=True)
    power = exponent(jnp.max(jnp.abs(total), axis=1, keepdims=True))
    total = total * jnp.exp2(TOP - power)
    dens_power = exponent(dens)
    part = dens * jnp.exp2(-dens_power)
    aside = [power, dens_power]
    for k in range(3):
        piece = part.astype(jnp.bfloat16).astype(jnp.float32)
        aside.append(piece * 2.0 ** (8 * k))
        part = part - piece
    for k, out_ref in enumerate(out_refs[::-1]):
        rows = slice(k * size, (k + 1) * size)
        out_ref[:size, :] = total[rows, :]
        out_ref[size:, :] = jnp.zeros((EXTRA, width), jnp.float32)
        for line, column in enumerate(aside):
            out_ref[size + line : size + line + 1, :size] = as_row(column[rows, :])


def restore_kernel(own_ref, ids_ref, *refs):
    part_refs, (total_ref, dens_ref) = refs[:-2], refs[-2:]
    groups = len(part_refs)
    size = part_refs[0].shape[0] - EXTRA
    chosen = placement(own_ref[0], ids_ref[...], groups)
    sums, dens = [], []
    for part_ref in part_refs[::-1]:
        power, dens_power, *pieces = [
            as_column(part_ref[size + line : size + line + 1, :size])
            for line in range(5)
        ]
        sums.append(part_ref[:size, :] * jnp.exp2(power - TOP))
        part = sum(piece * 2.0 ** (-8 * j) for j, piece in enumerate(pieces))
        dens.append(part * jnp.exp2(dens_power))
    dens_ref[...] = jnp.sum(
        chosen * jnp.concatenate(dens, axis=0), axis=0, keepdims=True
    )
    rest = jnp.concatenate(sums, axis=0)
    chosen = chosen.astype(jnp.bfloat16)
    back = jnp.zeros(rest.shape, jnp.float32)
    for _ in range(2):
        piece = rest.astype(jnp.bfloat16)
        rest = rest - piece.astype(jnp.float32)
        back += lax.dot_general(
            chosen, piece, (((0,), (0,)), ((), ())), preferred_element_type=jnp.float32
        )
    total_ref[...] = back


def on_device(n_gr, n_gc, embeddings, cluster_ids):
    count, width = embeddings.shape
    size = count // n_gr
    own = lax.axis_index("gr").astype(jnp.int32).reshape(1)
    ids = cluster_ids.reshape(1, count)

    parts = pl.pallas_call(
        sort_kernel,
        out_shape=[jax.ShapeDtypeStruct((size, width), jnp.bfloat16)] * n_gr,
        in_specs=[SMEM, VMEM, VMEM],
        out_specs=[VMEM] * n_gr,
        compiler_params=GRANT,
        name="sort_rows",
    )(own, ids, embeddings)[::-1]

    def along_gr(part, bits):
        return lax.ppermute(part, "gr", [(i, i ^ bits) for i in range(n_gr)])

    def along_gc(block, bits):
        return lax.ppermute(block, "gc", [(i, i ^ bits) for i in range(n_gc)])

    def other_core(block):
        return along_gc(block, 1)

    def cost(*blocks):
        pairs = count * sum(block.shape[0] for block in blocks)
        return pl.CostEstimate(
            flops=4 * pairs * width,
            bytes_accessed=0,
            transcendentals=pairs,
        )

    held = [parts[0]] + [along_gr(parts[k], k) for k in range(1, n_gr)]
    half = n_gr // 2
    chunks = []
    for pieces in (held[:half], held[half:]):
        block = jnp.concatenate(pieces, axis=0)
        near = [block] + [along_gc(block, k) for k in range(2, n_gc, 2)]
        chunks.append(jnp.concatenate(near, axis=0))
    rows = jnp.concatenate(held, axis=0)
    early = [chunks[0], other_core(chunks[0]), chunks[1]]

    total, dens = pl.pallas_call(
        first_kernel,
        out_shape=[
            jax.ShapeDtypeStruct((count, width), jnp.float32),
            jax.ShapeDtypeStruct((count, LANES), jnp.float32),
        ],
        in_specs=[VMEM] * (1 + len(early)),
        out_specs=[VMEM] * 2,
        compiler_params=GRANT,
        cost_estimate=cost(*early),
        name="early_sums",
    )(rows, *early)
    late = [other_core(chunks[1])]
    sums = pl.pallas_call(
        functools.partial(last_kernel, n_gr),
        out_shape=[jax.ShapeDtypeStruct((size + EXTRA, width), jnp.float32)] * n_gr,
        in_specs=[VMEM] * (3 + len(late)),
        out_specs=[VMEM] * n_gr,
        compiler_params=GRANT,
        cost_estimate=cost(*late),
        name="last_sums",
    )(rows, total, dens, *late)[::-1]

    sent = [part.astype(jnp.float16) for part in sums]
    back = [None] * n_gr
    back[0] = sent[0]
    for k in sorted(range(1, n_gr), reverse=True):
        back[k] = along_gr(sent[k], k)
    back = [part.astype(jnp.float32) for part in back]
    neighbour_sum, density = pl.pallas_call(
        restore_kernel,
        out_shape=[
            jax.ShapeDtypeStruct((count, width), jnp.float32),
            jax.ShapeDtypeStruct((1, count), jnp.float32),
        ],
        in_specs=[SMEM, VMEM] + [VMEM] * n_gr,
        out_specs=[VMEM, VMEM],
        compiler_params=GRANT,
        name="restore_rows",
    )(own, ids, *back[::-1])
    return (neighbour_sum, density.reshape(count))


def solution(mesh):
    in_specs = (P(("gr", "gc"), None), P(("gr", "gc")))
    out_specs = (P(("gr", "gc"), None), P(("gr", "gc")))
    return jax.shard_map(
        functools.partial(on_device, mesh.shape["gr"], mesh.shape["gc"]),
        mesh=mesh,
        in_specs=in_specs,
        out_specs=out_specs,
        check_vma=False,
    )
```

```python
import functools
import math

import jax
import jax.numpy as jnp
from jax import lax
from jax.experimental import pallas as pl
from jax.experimental.pallas import tpu as pltpu
from jax.sharding import PartitionSpec as P

beta_scale = 16.0
LANES = 128
EXTRA = 8
TOP = 14.0
VMEM = pl.BlockSpec(memory_space=pltpu.VMEM)
SMEM = pl.BlockSpec(memory_space=pltpu.SMEM)
GRANT = pltpu.CompilerParams(vmem_limit_bytes=40 * 1024 * 1024)


def diagonal(count):
    first = lax.broadcasted_iota(jnp.int32, (count, count), 0)
    second = lax.broadcasted_iota(jnp.int32, (count, count), 1)
    return first == second


def as_row(column):
    return jnp.sum(
        jnp.where(diagonal(column.shape[0]), column, jnp.zeros_like(column)),
        axis=0,
        keepdims=True,
    )


def as_column(row):
    return jnp.sum(
        jnp.where(diagonal(row.shape[1]), row, jnp.zeros_like(row)),
        axis=1,
        keepdims=True,
    )


def placement(own, ids, groups):
    count = ids.shape[1]
    first = lax.broadcasted_iota(jnp.int32, (count, count), 0)
    second = lax.broadcasted_iota(jnp.int32, (count, count), 1)
    earlier = jnp.where((as_column(ids) == ids) & (first < second), 1, 0)
    rank = jnp.sum(earlier, axis=0, keepdims=True)
    slot = (ids ^ own) * (count // groups) + rank
    return jnp.where(first == slot, 1.0, 0.0)


def sort_kernel(own_ref, ids_ref, rows_ref, *out_refs):
    groups = len(out_refs)
    chosen = placement(own_ref[0], ids_ref[...], groups).astype(jnp.bfloat16)
    ordered = jnp.dot(chosen, rows_ref[...], preferred_element_type=jnp.float32)
    ordered = ordered.astype(jnp.bfloat16)
    size = ordered.shape[0] // groups
    for k, out_ref in enumerate(out_refs[::-1]):
        out_ref[...] = ordered[k * size : (k + 1) * size, :]


def inverse_norms(rows):
    wide = rows.astype(jnp.float32)
    return lax.rsqrt(jnp.sum(wide * wide, axis=1, keepdims=True) + 1e-06)


def add_columns(rows, col_refs, total, dens):
    count = rows.shape[0]
    scale = inverse_norms(rows) * (beta_scale * math.log2(math.e))
    blocks = [
        (col_ref, start)
        for col_ref in col_refs
        for start in range(0, col_ref.shape[0], count)
    ]
    for col_ref, start in blocks:
        cols = col_ref[start : min(start + count, col_ref.shape[0]), :]
        size = cols.shape[0]
        col_inv = as_row(inverse_norms(cols))
        raw = lax.dot_general(
            rows, cols, (((1,), (1,)), ((), ())), preferred_element_type=jnp.float32
        )
        weight = jnp.exp2(raw * scale * col_inv - beta_scale * math.log2(math.e))
        whole = size - size % LANES
        for lane in range(0, whole, LANES):
            dens += weight[:, lane : lane + LANES]
        if whole < size:
            part = jnp.sum(weight[:, whole:], axis=1, keepdims=True)
            dens += jnp.where(lax.broadcasted_iota(jnp.int32, dens.shape, 1) == 0, part, 0.0)
        coef = (weight * col_inv).astype(jnp.bfloat16)
        total += jnp.dot(coef, cols, preferred_element_type=jnp.float32)
    return total, dens


def first_kernel(rows_ref, *refs):
    col_refs, (total_ref, dens_ref) = refs[:-2], refs[-2:]
    total = jnp.zeros(total_ref.shape, jnp.float32)
    dens = jnp.zeros(dens_ref.shape, jnp.float32)
    total, dens = add_columns(rows_ref[...], col_refs, total, dens)
    total_ref[...] = total
    dens_ref[...] = dens


def middle_kernel(rows_ref, total_ref, dens_ref, *refs):
    col_refs, (total_out, dens_out) = refs[:-2], refs[-2:]
    total, dens = add_columns(rows_ref[...], col_refs, total_ref[...], dens_ref[...])
    total_out[...] = total
    dens_out[...] = dens


def exponent(value):
    return jnp.floor(jnp.log2(jnp.maximum(value, 1e-37)))


def last_kernel(groups, rows_ref, total_ref, dens_ref, *refs):
    col_refs, out_refs = refs[:-groups], refs[-groups:]
    padded, width = out_refs[0].shape
    size = padded - EXTRA
    total, dens = add_columns(rows_ref[...], col_refs, total_ref[...], dens_ref[...])
    dens = jnp.sum(dens, axis=1, keepdims=True)
    power = exponent(jnp.max(jnp.abs(total), axis=1, keepdims=True))
    total = total * jnp.exp2(TOP - power)
    dens_power = exponent(dens)
    part = dens * jnp.exp2(-dens_power)
    aside = [power, dens_power]
    for k in range(3):
        piece = part.astype(jnp.bfloat16).astype(jnp.float32)
        aside.append(piece * 2.0 ** (8 * k))
        part = part - piece
    for k, out_ref in enumerate(out_refs[::-1]):
        rows = slice(k * size, (k + 1) * size)
        out_ref[:size, :] = total[rows, :]
        out_ref[size:, :] = jnp.zeros((EXTRA, width), jnp.float32)
        for line, column in enumerate(aside):
            out_ref[size + line : size + line + 1, :size] = as_row(column[rows, :])


def restore_kernel(own_ref, ids_ref, *refs):
    part_refs, (total_ref, dens_ref) = refs[:-2], refs[-2:]
    groups = len(part_refs)
    size = part_refs[0].shape[0] - EXTRA
    chosen = placement(own_ref[0], ids_ref[...], groups)
    sums, dens = [], []
    for part_ref in part_refs[::-1]:
        power, dens_power, *pieces = [
            as_column(part_ref[size + line : size + line + 1, :size])
            for line in range(5)
        ]
        sums.append(part_ref[:size, :] * jnp.exp2(power - TOP))
        part = sum(piece * 2.0 ** (-8 * j) for j, piece in enumerate(pieces))
        dens.append(part * jnp.exp2(dens_power))
    dens_ref[...] = jnp.sum(
        chosen * jnp.concatenate(dens, axis=0), axis=0, keepdims=True
    )
    rest = jnp.concatenate(sums, axis=0)
    chosen = chosen.astype(jnp.bfloat16)
    back = jnp.zeros(rest.shape, jnp.float32)
    for _ in range(2):
        piece = rest.astype(jnp.bfloat16)
        rest = rest - piece.astype(jnp.float32)
        back += lax.dot_general(
            chosen, piece, (((0,), (0,)), ((), ())), preferred_element_type=jnp.float32
        )
    total_ref[...] = back


def on_device(n_gr, n_gc, embeddings, cluster_ids):
    count, width = embeddings.shape
    size = count // n_gr
    own = lax.axis_index("gr").astype(jnp.int32).reshape(1)
    ids = cluster_ids.reshape(1, count)

    parts = pl.pallas_call(
        sort_kernel,
        out_shape=[jax.ShapeDtypeStruct((size, width), jnp.bfloat16)] * n_gr,
        in_specs=[SMEM, VMEM, VMEM],
        out_specs=[VMEM] * n_gr,
        compiler_params=GRANT,
        name="sort_rows",
    )(own, ids, embeddings)[::-1]

    def along_gr(part, bits):
        return lax.ppermute(part, "gr", [(i, i ^ bits) for i in range(n_gr)])

    def along_gc(block, bits):
        return lax.ppermute(block, "gc", [(i, i ^ bits) for i in range(n_gc)])

    def other_core(block):
        return along_gc(block, 1)

    def cost(*blocks):
        pairs = count * sum(block.shape[0] for block in blocks)
        return pl.CostEstimate(
            flops=4 * pairs * width,
            bytes_accessed=0,
            transcendentals=pairs,
        )

    held = [parts[0]] + [along_gr(parts[k], k) for k in range(1, n_gr)]
    half = n_gr // 2
    chunks = []
    for pieces in (held[:half], held[half:]):
        block = jnp.concatenate(pieces, axis=0)
        near = [block] + [along_gc(block, k) for k in range(2, n_gc, 2)]
        chunks.append(jnp.concatenate(near, axis=0))
    rows = jnp.concatenate(held, axis=0)
    chunks[0], rows = lax.optimization_barrier((chunks[0], rows))
    early = [chunks[0], other_core(chunks[0])]

    total, dens = pl.pallas_call(
        first_kernel,
        out_shape=[
            jax.ShapeDtypeStruct((count, width), jnp.float32),
            jax.ShapeDtypeStruct((count, LANES), jnp.float32),
        ],
        in_specs=[VMEM] * (1 + len(early)),
        out_specs=[VMEM] * 2,
        compiler_params=GRANT,
        cost_estimate=cost(*early),
        name="early_sums",
    )(rows, *early)
    total, dens = pl.pallas_call(
        middle_kernel,
        out_shape=[
            jax.ShapeDtypeStruct((count, width), jnp.float32),
            jax.ShapeDtypeStruct((count, LANES), jnp.float32),
        ],
        in_specs=[VMEM] * 4,
        out_specs=[VMEM] * 2,
        compiler_params=GRANT,
        cost_estimate=cost(chunks[1]),
        name="middle_sums",
    )(rows, total, dens, chunks[1])
    late = [other_core(chunks[1])]
    sums = pl.pallas_call(
        functools.partial(last_kernel, n_gr),
        out_shape=[jax.ShapeDtypeStruct((size + EXTRA, width), jnp.float32)] * n_gr,
        in_specs=[VMEM] * (3 + len(late)),
        out_specs=[VMEM] * n_gr,
        compiler_params=GRANT,
        cost_estimate=cost(*late),
        name="last_sums",
    )(rows, total, dens, *late)[::-1]

    sent = [part.astype(jnp.float16) for part in sums]
    back = [None] * n_gr
    back[0] = sent[0]
    for k in sorted(range(1, n_gr), reverse=True):
        back[k] = along_gr(sent[k], k)
    back = [part.astype(jnp.float32) for part in back]
    neighbour_sum, density = pl.pallas_call(
        restore_kernel,
        out_shape=[
            jax.ShapeDtypeStruct((count, width), jnp.float32),
            jax.ShapeDtypeStruct((1, count), jnp.float32),
        ],
        in_specs=[SMEM, VMEM] + [VMEM] * n_gr,
        out_specs=[VMEM, VMEM],
        compiler_params=GRANT,
        name="restore_rows",
    )(own, ids, *back[::-1])
    return (neighbour_sum, density.reshape(count))


def solution(mesh):
    in_specs = (P(("gr", "gc"), None), P(("gr", "gc")))
    out_specs = (P(("gr", "gc"), None), P(("gr", "gc")))
    return jax.shard_map(
        functools.partial(on_device, mesh.shape["gr"], mesh.shape["gc"]),
        mesh=mesh,
        in_specs=in_specs,
        out_specs=out_specs,
        check_vma=False,
    )
```

```python
import functools
import math

import jax
import jax.numpy as jnp
from jax import lax
from jax.experimental import pallas as pl
from jax.experimental.pallas import tpu as pltpu
from jax.sharding import PartitionSpec as P

beta_scale = 16.0
LANES = 128
SUBLANES = 8
TOP = 14.0
VMEM = pl.BlockSpec(memory_space=pltpu.VMEM)
HBM = pl.BlockSpec(memory_space=pltpu.HBM)
SMEM = pl.BlockSpec(memory_space=pltpu.SMEM)
GRANT = pltpu.CompilerParams(vmem_limit_bytes=40 * 1024 * 1024)


def in_hbm(array):
    return pltpu.with_memory_space_constraint(array, pltpu.HBM)


def diagonal(count):
    first = lax.broadcasted_iota(jnp.int32, (count, count), 0)
    second = lax.broadcasted_iota(jnp.int32, (count, count), 1)
    return first == second


def as_row(column):
    return jnp.sum(
        jnp.where(diagonal(column.shape[0]), column, jnp.zeros_like(column)),
        axis=0,
        keepdims=True,
    )


def as_column(row):
    return jnp.sum(
        jnp.where(diagonal(row.shape[1]), row, jnp.zeros_like(row)),
        axis=1,
        keepdims=True,
    )


def placement(own, ids, groups):
    count = ids.shape[1]
    first = lax.broadcasted_iota(jnp.int32, (count, count), 0)
    second = lax.broadcasted_iota(jnp.int32, (count, count), 1)
    earlier = jnp.where((as_column(ids) == ids) & (first < second), 1, 0)
    rank = jnp.sum(earlier, axis=0, keepdims=True)
    slot = (ids ^ own) * (count // groups) + rank
    return jnp.where(first == slot, 1.0, 0.0)


def sort_kernel(own_ref, ids_hbm, rows_hbm, *refs):
    out_refs, (ids_ref, rows_ref, ids_sem, rows_sem) = refs[:-4], refs[-4:]
    groups = len(out_refs)
    ids_copy = pltpu.make_async_copy(ids_hbm, ids_ref, ids_sem)
    rows_copy = pltpu.make_async_copy(rows_hbm, rows_ref, rows_sem)
    ids_copy.start()
    rows_copy.start()
    ids_copy.wait()
    chosen = placement(own_ref[0], ids_ref[...], groups).astype(jnp.bfloat16)
    rows_copy.wait()
    ordered = jnp.dot(chosen, rows_ref[...], preferred_element_type=jnp.float32)
    ordered = ordered.astype(jnp.bfloat16)
    size = ordered.shape[0] // groups
    for k, out_ref in enumerate(out_refs[::-1]):
        out_ref[...] = ordered[k * size : (k + 1) * size, :]


def inverse_norms(rows):
    wide = rows.astype(jnp.float32)
    return lax.rsqrt(jnp.sum(wide * wide, axis=1, keepdims=True) + 1e-06)


def add_columns(rows, col_refs, total, dens):
    count = rows.shape[0]
    scale = inverse_norms(rows) * (beta_scale * math.log2(math.e))
    blocks = [
        (col_ref, start)
        for col_ref in col_refs
        for start in range(0, col_ref.shape[0], count)
    ]
    for col_ref, start in blocks:
        cols = col_ref[start : min(start + count, col_ref.shape[0]), :]
        size = cols.shape[0]
        col_inv = as_row(inverse_norms(cols))
        raw = lax.dot_general(
            rows, cols, (((1,), (1,)), ((), ())), preferred_element_type=jnp.float32
        )
        weight = jnp.exp2(raw * scale * col_inv - beta_scale * math.log2(math.e))
        whole = size - size % LANES
        for lane in range(0, whole, LANES):
            dens += weight[:, lane : lane + LANES]
        if whole < size:
            part = jnp.sum(weight[:, whole:], axis=1, keepdims=True)
            dens += jnp.where(lax.broadcasted_iota(jnp.int32, dens.shape, 1) == 0, part, 0.0)
        coef = (weight * col_inv).astype(jnp.bfloat16)
        total += jnp.dot(coef, cols, preferred_element_type=jnp.float32)
    return total, dens


def first_kernel(rows_ref, *refs):
    col_refs, (total_ref, dens_ref) = refs[:-2], refs[-2:]
    total = jnp.zeros(total_ref.shape, jnp.float32)
    dens = jnp.zeros(dens_ref.shape, jnp.float32)
    total, dens = add_columns(rows_ref[...], col_refs, total, dens)
    total_ref[...] = total
    dens_ref[...] = dens


def middle_kernel(rows_ref, total_ref, dens_ref, *refs):
    col_refs, (total_out, dens_out) = refs[:-2], refs[-2:]
    total, dens = add_columns(rows_ref[...], col_refs, total_ref[...], dens_ref[...])
    total_out[...] = total
    dens_out[...] = dens


def last_kernel(groups, rows_ref, total_ref, dens_ref, *refs):
    col_refs, out_refs, aside_refs = (
        refs[: -2 * groups],
        refs[-2 * groups : -groups],
        refs[-groups:],
    )
    size = out_refs[0].shape[0]
    total, dens = add_columns(rows_ref[...], col_refs, total_ref[...], dens_ref[...])
    dens = jnp.sum(dens, axis=1, keepdims=True)
    largest = jnp.max(jnp.abs(total), axis=1, keepdims=True)
    power = jnp.floor(jnp.log2(jnp.maximum(largest, 1e-37)))
    total = total * jnp.exp2(TOP - power)
    for k in range(groups):
        rows = slice(k * size, (k + 1) * size)
        out_refs[k][...] = total[rows, :]
        aside_refs[k][0:1, :size] = as_row(dens[rows, :])
        aside_refs[k][1:2, :size] = as_row(power[rows, :])


def restore_kernel(own_ref, ids_ref, *refs):
    refs, (total_ref, dens_ref) = refs[:-2], refs[-2:]
    groups = len(refs) // 2
    size = refs[0].shape[0]
    chosen = placement(own_ref[0], ids_ref[...], groups)
    sums, dens = [], []
    for part_ref, aside_ref in zip(refs[groups - 1 :: -1], refs[: groups - 1 : -1]):
        dens.append(as_column(aside_ref[0:1, :size]))
        power = as_column(aside_ref[1:2, :size])
        sums.append(part_ref[...] * jnp.exp2(power - TOP))
    dens_ref[...] = jnp.sum(
        chosen * jnp.concatenate(dens, axis=0), axis=0, keepdims=True
    )
    rest = jnp.concatenate(sums, axis=0)
    chosen = chosen.astype(jnp.bfloat16)
    back = jnp.zeros(rest.shape, jnp.float32)
    for _ in range(2):
        piece = rest.astype(jnp.bfloat16)
        rest = rest - piece.astype(jnp.float32)
        back += lax.dot_general(
            chosen, piece, (((0,), (0,)), ((), ())), preferred_element_type=jnp.float32
        )
    total_ref[...] = back


def on_device(n_gr, n_gc, embeddings, cluster_ids):
    count, width = embeddings.shape
    size = count // n_gr
    own = lax.axis_index("gr").astype(jnp.int32).reshape(1)
    ids = cluster_ids.reshape(1, count)

    parts = pl.pallas_call(
        sort_kernel,
        out_shape=[jax.ShapeDtypeStruct((size, width), jnp.bfloat16)] * n_gr,
        in_specs=[SMEM, HBM, HBM],
        out_specs=[VMEM] * n_gr,
        scratch_shapes=[
            pltpu.VMEM((1, count), jnp.int32),
            pltpu.VMEM((count, width), embeddings.dtype),
            pltpu.SemaphoreType.DMA,
            pltpu.SemaphoreType.DMA,
        ],
        compiler_params=GRANT,
        name="sort_rows",
    )(own, in_hbm(ids), in_hbm(embeddings))[::-1]

    def along_gr(part, bits):
        return lax.ppermute(part, "gr", [(i, i ^ bits) for i in range(n_gr)])

    def along_gc(block, bits):
        return lax.ppermute(block, "gc", [(i, i ^ bits) for i in range(n_gc)])

    def other_core(block):
        return along_gc(block, 1)

    def cost(*blocks):
        pairs = count * sum(block.shape[0] for block in blocks)
        return pl.CostEstimate(
            flops=4 * pairs * width,
            bytes_accessed=0,
            transcendentals=pairs,
        )

    held = [parts[0]] + [along_gr(parts[k], k) for k in range(1, n_gr)]
    half = n_gr // 2
    chunks = []
    for pieces in (held[:half], held[half:]):
        block = jnp.concatenate(pieces, axis=0)
        near = [block] + [along_gc(block, k) for k in range(2, n_gc, 2)]
        chunks.append(jnp.concatenate(near, axis=0))
    rows = jnp.concatenate(held, axis=0)
    chunks[0], rows = lax.optimization_barrier((chunks[0], rows))
    early = [chunks[0], other_core(chunks[0])]

    total, dens = pl.pallas_call(
        first_kernel,
        out_shape=[
            jax.ShapeDtypeStruct((count, width), jnp.float32),
            jax.ShapeDtypeStruct((count, LANES), jnp.float32),
        ],
        in_specs=[VMEM] * (1 + len(early)),
        out_specs=[VMEM] * 2,
        compiler_params=GRANT,
        cost_estimate=cost(*early),
        name="early_sums",
    )(rows, *early)
    total, dens = pl.pallas_call(
        middle_kernel,
        out_shape=[
            jax.ShapeDtypeStruct((count, width), jnp.float32),
            jax.ShapeDtypeStruct((count, LANES), jnp.float32),
        ],
        in_specs=[VMEM] * 4,
        out_specs=[VMEM] * 2,
        compiler_params=GRANT,
        cost_estimate=cost(chunks[1]),
        name="middle_sums",
    )(rows, total, dens, chunks[1])
    late = [other_core(chunks[1])]
    sums = pl.pallas_call(
        functools.partial(last_kernel, n_gr),
        out_shape=[jax.ShapeDtypeStruct((size, width), jnp.float32)] * n_gr
        + [jax.ShapeDtypeStruct((SUBLANES, LANES), jnp.float32)] * n_gr,
        in_specs=[VMEM] * (3 + len(late)),
        out_specs=[VMEM] * (2 * n_gr),
        compiler_params=GRANT,
        cost_estimate=cost(*late),
        name="last_sums",
    )(rows, total, dens, *late)
    sums, asides = sums[:n_gr], sums[n_gr:]

    sent = [part.astype(jnp.float16) for part in sums]
    back = [sent[0]] + [along_gr(sent[k], k) for k in range(1, n_gr)]
    back = [part.astype(jnp.float32) for part in back]
    beside = [asides[0]] + [along_gr(asides[k], k) for k in range(1, n_gr)]
    neighbour_sum, density = pl.pallas_call(
        restore_kernel,
        out_shape=[
            jax.ShapeDtypeStruct((count, width), jnp.float32),
            jax.ShapeDtypeStruct((1, count), jnp.float32),
        ],
        in_specs=[SMEM, VMEM] + [VMEM] * (2 * n_gr),
        out_specs=[VMEM, VMEM],
        compiler_params=GRANT,
        name="restore_rows",
    )(own, ids, *back[::-1], *beside[::-1])
    return (neighbour_sum, density.reshape(count))


def solution(mesh):
    in_specs = (P(("gr", "gc"), None), P(("gr", "gc")))
    out_specs = (P(("gr", "gc"), None), P(("gr", "gc")))
    return jax.shard_map(
        functools.partial(on_device, mesh.shape["gr"], mesh.shape["gc"]),
        mesh=mesh,
        in_specs=in_specs,
        out_specs=out_specs,
        check_vma=False,
    )
```

```python
import functools
import math

import jax
import jax.numpy as jnp
from jax import lax
from jax.experimental import pallas as pl
from jax.experimental.pallas import tpu as pltpu
from jax.sharding import PartitionSpec as P

beta_scale = 16.0
LANES = 128
EXTRA = 8
TOP = 14.0
VMEM = pl.BlockSpec(memory_space=pltpu.VMEM)
HBM = pl.BlockSpec(memory_space=pltpu.HBM)
SMEM = pl.BlockSpec(memory_space=pltpu.SMEM)
GRANT = pltpu.CompilerParams(vmem_limit_bytes=40 * 1024 * 1024)


def in_hbm(array):
    return pltpu.with_memory_space_constraint(array, pltpu.HBM)


def diagonal(count):
    first = lax.broadcasted_iota(jnp.int32, (count, count), 0)
    second = lax.broadcasted_iota(jnp.int32, (count, count), 1)
    return first == second


def as_row(column):
    return jnp.sum(
        jnp.where(diagonal(column.shape[0]), column, jnp.zeros_like(column)),
        axis=0,
        keepdims=True,
    )


def as_column(row):
    return jnp.sum(
        jnp.where(diagonal(row.shape[1]), row, jnp.zeros_like(row)),
        axis=1,
        keepdims=True,
    )


def placement(own, ids, groups):
    count = ids.shape[1]
    first = lax.broadcasted_iota(jnp.int32, (count, count), 0)
    second = lax.broadcasted_iota(jnp.int32, (count, count), 1)
    earlier = jnp.where((as_column(ids) == ids) & (first < second), 1, 0)
    rank = jnp.sum(earlier, axis=0, keepdims=True)
    slot = (ids ^ own) * (count // groups) + rank
    return jnp.where(first == slot, 1.0, 0.0)


def sort_kernel(own_ref, ids_hbm, rows_hbm, *refs):
    chosen_ref, *out_refs = refs[:-4]
    ids_ref, rows_ref, ids_sem, rows_sem = refs[-4:]
    groups = len(out_refs)
    ids_copy = pltpu.make_async_copy(ids_hbm, ids_ref, ids_sem)
    rows_copy = pltpu.make_async_copy(rows_hbm, rows_ref, rows_sem)
    ids_copy.start()
    rows_copy.start()
    ids_copy.wait()
    chosen = placement(own_ref[0], ids_ref[...], groups).astype(jnp.bfloat16)
    chosen_ref[...] = chosen
    rows_copy.wait()
    ordered = jnp.dot(chosen, rows_ref[...], preferred_element_type=jnp.float32)
    ordered = ordered.astype(jnp.bfloat16)
    size = ordered.shape[0] // groups
    for k, out_ref in enumerate(out_refs):
        out_ref[...] = ordered[k * size : (k + 1) * size, :]


def inverse_norms(rows):
    wide = rows.astype(jnp.float32)
    return lax.rsqrt(jnp.sum(wide * wide, axis=1, keepdims=True) + 1e-06)


def add_columns(rows, col_refs, total, dens):
    count = rows.shape[0]
    scale = inverse_norms(rows) * (beta_scale * math.log2(math.e))
    blocks = [
        (col_ref, start)
        for col_ref in col_refs
        for start in range(0, col_ref.shape[0], count)
    ]
    for col_ref, start in blocks:
        cols = col_ref[start : min(start + count, col_ref.shape[0]), :]
        size = cols.shape[0]
        col_inv = as_row(inverse_norms(cols))
        raw = lax.dot_general(
            rows, cols, (((1,), (1,)), ((), ())), preferred_element_type=jnp.float32
        )
        weight = jnp.exp2(raw * scale * col_inv - beta_scale * math.log2(math.e))
        whole = size - size % LANES
        for lane in range(0, whole, LANES):
            dens += weight[:, lane : lane + LANES]
        if whole < size:
            part = jnp.sum(weight[:, whole:], axis=1, keepdims=True)
            dens += jnp.where(lax.broadcasted_iota(jnp.int32, dens.shape, 1) == 0, part, 0.0)
        coef = (weight * col_inv).astype(jnp.bfloat16)
        total += jnp.dot(coef, cols, preferred_element_type=jnp.float32)
    return total, dens


def first_kernel(rows_ref, *refs):
    col_refs, (total_ref, dens_ref) = refs[:-2], refs[-2:]
    total = jnp.zeros(total_ref.shape, jnp.float32)
    dens = jnp.zeros(dens_ref.shape, jnp.float32)
    total, dens = add_columns(rows_ref[...], col_refs, total, dens)
    total_ref[...] = total
    dens_ref[...] = dens


def middle_kernel(rows_ref, total_ref, dens_ref, *refs):
    col_refs, (total_out, dens_out) = refs[:-2], refs[-2:]
    total, dens = add_columns(rows_ref[...], col_refs, total_ref[...], dens_ref[...])
    total_out[...] = total
    dens_out[...] = dens


def exponent(value):
    return jnp.floor(jnp.log2(jnp.maximum(value, 1e-30)))


def last_kernel(groups, rows_ref, total_ref, dens_ref, *refs):
    col_refs, out_refs = refs[:-groups], refs[-groups:]
    padded, width = out_refs[0].shape
    size = padded - EXTRA
    total, dens = add_columns(rows_ref[...], col_refs, total_ref[...], dens_ref[...])
    dens = jnp.sum(dens, axis=1, keepdims=True)
    power = exponent(jnp.max(jnp.abs(total), axis=1, keepdims=True))
    total = total * jnp.exp2(TOP - power)
    dens_power = exponent(dens)
    part = dens * jnp.exp2(-dens_power)
    aside = [power, dens_power]
    for k in range(3):
        piece = part.astype(jnp.bfloat16).astype(jnp.float32)
        aside.append(piece * 2.0 ** (8 * k))
        part = part - piece
    for k, out_ref in enumerate(out_refs[::-1]):
        rows = slice(k * size, (k + 1) * size)
        out_ref[:size, :] = total[rows, :]
        out_ref[size:, :] = jnp.zeros((EXTRA, width), jnp.float32)
        for line, column in enumerate(aside):
            out_ref[size + line : size + line + 1, :size] = as_row(column[rows, :])


def restore_kernel(chosen_ref, *refs):
    part_refs, (total_ref, dens_ref) = refs[:-2], refs[-2:]
    groups = len(part_refs)
    size = part_refs[0].shape[0] - EXTRA
    chosen = chosen_ref[...]
    sums, dens = [], []
    for part_ref in part_refs[::-1]:
        power, dens_power, *pieces = [
            as_column(part_ref[size + line : size + line + 1, :size])
            for line in range(5)
        ]
        sums.append(part_ref[:size, :] * jnp.exp2(power - TOP))
        part = sum(piece * 2.0 ** (-8 * j) for j, piece in enumerate(pieces))
        dens.append(part * jnp.exp2(dens_power))
    dens_ref[...] = jnp.sum(
        chosen.astype(jnp.float32) * jnp.concatenate(dens, axis=0), axis=0, keepdims=True
    )
    rest = jnp.concatenate(sums, axis=0)
    back = jnp.zeros(rest.shape, jnp.float32)
    for _ in range(2):
        piece = rest.astype(jnp.bfloat16)
        rest = rest - piece.astype(jnp.float32)
        back += lax.dot_general(
            chosen, piece, (((0,), (0,)), ((), ())), preferred_element_type=jnp.float32
        )
    total_ref[...] = back


def on_device(n_gr, n_gc, embeddings, cluster_ids):
    count, width = embeddings.shape
    size = count // n_gr
    own = lax.axis_index("gr").astype(jnp.int32).reshape(1)
    ids = cluster_ids.reshape(1, count)

    chosen, *parts = pl.pallas_call(
        sort_kernel,
        out_shape=[jax.ShapeDtypeStruct((count, count), jnp.bfloat16)]
        + [jax.ShapeDtypeStruct((size, width), jnp.bfloat16)] * n_gr,
        in_specs=[SMEM, HBM, HBM],
        out_specs=[VMEM] * (1 + n_gr),
        scratch_shapes=[
            pltpu.VMEM((1, count), jnp.int32),
            pltpu.VMEM((count, width), embeddings.dtype),
            pltpu.SemaphoreType.DMA,
            pltpu.SemaphoreType.DMA,
        ],
        compiler_params=GRANT,
        name="sort_rows",
    )(own, in_hbm(ids), in_hbm(embeddings))

    def along_gr(part, bits):
        return lax.ppermute(part, "gr", [(i, i ^ bits) for i in range(n_gr)])

    def along_gc(block, bits):
        return lax.ppermute(block, "gc", [(i, i ^ bits) for i in range(n_gc)])

    def other_core(block):
        return along_gc(block, 1)

    def cost(*blocks):
        pairs = count * sum(block.shape[0] for block in blocks)
        return pl.CostEstimate(
            flops=4 * pairs * width,
            bytes_accessed=0,
            transcendentals=pairs,
        )

    held = [parts[0]] + [along_gr(parts[k], k) for k in range(1, n_gr)]
    half = n_gr // 2
    chunks = []
    for pieces in (held[:half], held[half:]):
        block = jnp.concatenate(pieces, axis=0)
        near = [block] + [along_gc(block, k) for k in range(2, n_gc, 2)]
        chunks.append(jnp.concatenate(near, axis=0))
    rows = jnp.concatenate(held, axis=0)
    chunks[0], rows = lax.optimization_barrier((chunks[0], rows))
    early = [chunks[0], other_core(chunks[0])]

    total, dens = pl.pallas_call(
        first_kernel,
        out_shape=[
            jax.ShapeDtypeStruct((count, width), jnp.float32),
            jax.ShapeDtypeStruct((count, LANES), jnp.float32),
        ],
        in_specs=[VMEM] * (1 + len(early)),
        out_specs=[VMEM] * 2,
        compiler_params=GRANT,
        cost_estimate=cost(*early),
        name="early_sums",
    )(rows, *early)
    total, dens = pl.pallas_call(
        middle_kernel,
        out_shape=[
            jax.ShapeDtypeStruct((count, width), jnp.float32),
            jax.ShapeDtypeStruct((count, LANES), jnp.float32),
        ],
        in_specs=[VMEM] * 4,
        out_specs=[VMEM] * 2,
        compiler_params=GRANT,
        cost_estimate=cost(chunks[1]),
        name="middle_sums",
    )(rows, total, dens, chunks[1])
    late = [other_core(chunks[1])]
    sums = pl.pallas_call(
        functools.partial(last_kernel, n_gr),
        out_shape=[jax.ShapeDtypeStruct((size + EXTRA, width), jnp.float32)] * n_gr,
        in_specs=[VMEM] * (3 + len(late)),
        out_specs=[VMEM] * n_gr,
        compiler_params=GRANT,
        cost_estimate=cost(*late),
        name="last_sums",
    )(rows, total, dens, *late)[::-1]

    sent = [part.astype(jnp.float16) for part in sums]
    back = [None] * n_gr
    back[0] = sent[0]
    for k in sorted(range(1, n_gr), reverse=True):
        back[k] = along_gr(sent[k], k)
    back = [part.astype(jnp.float32) for part in back]
    neighbour_sum, density = pl.pallas_call(
        restore_kernel,
        out_shape=[
            jax.ShapeDtypeStruct((count, width), jnp.float32),
            jax.ShapeDtypeStruct((1, count), jnp.float32),
        ],
        in_specs=[VMEM] * (1 + n_gr),
        out_specs=[VMEM, VMEM],
        compiler_params=GRANT,
        name="restore_rows",
    )(chosen, *back[::-1])
    return (neighbour_sum, density.reshape(count))


def solution(mesh):
    in_specs = (P(("gr", "gc"), None), P(("gr", "gc")))
    out_specs = (P(("gr", "gc"), None), P(("gr", "gc")))
    return jax.shard_map(
        functools.partial(on_device, mesh.shape["gr"], mesh.shape["gc"]),
        mesh=mesh,
        in_specs=in_specs,
        out_specs=out_specs,
        check_vma=False,
    )
```

```python
import functools
import math

import jax
import jax.numpy as jnp
from jax import lax
from jax.experimental import pallas as pl
from jax.experimental.pallas import tpu as pltpu
from jax.sharding import PartitionSpec as P

beta_scale = 16.0
LANES = 128
EXTRA = 8
TOP = 14.0
VMEM = pl.BlockSpec(memory_space=pltpu.VMEM)
HBM = pl.BlockSpec(memory_space=pltpu.HBM)
SMEM = pl.BlockSpec(memory_space=pltpu.SMEM)
GRANT = pltpu.CompilerParams(vmem_limit_bytes=40 * 1024 * 1024)


def in_hbm(array):
    return pltpu.with_memory_space_constraint(array, pltpu.HBM)


def diagonal(count):
    first = lax.broadcasted_iota(jnp.int32, (count, count), 0)
    second = lax.broadcasted_iota(jnp.int32, (count, count), 1)
    return first == second


def as_row(column):
    return jnp.sum(
        jnp.where(diagonal(column.shape[0]), column, jnp.zeros_like(column)),
        axis=0,
        keepdims=True,
    )


def as_column(row):
    return jnp.sum(
        jnp.where(diagonal(row.shape[1]), row, jnp.zeros_like(row)),
        axis=1,
        keepdims=True,
    )


def placement(own, ids, groups):
    count = ids.shape[1]
    first = lax.broadcasted_iota(jnp.int32, (count, count), 0)
    second = lax.broadcasted_iota(jnp.int32, (count, count), 1)
    earlier = jnp.where((as_column(ids) == ids) & (first < second), 1, 0)
    rank = jnp.sum(earlier, axis=0, keepdims=True)
    slot = (ids ^ own) * (count // groups) + rank
    return jnp.where(first == slot, 1.0, 0.0)


def sort_kernel(own_ref, ids_hbm, rows_hbm, *refs):
    chosen_ref, *out_refs = refs[:-4]
    ids_ref, rows_ref, ids_sem, rows_sem = refs[-4:]
    groups = len(out_refs)
    ids_copy = pltpu.make_async_copy(ids_hbm, ids_ref, ids_sem)
    rows_copy = pltpu.make_async_copy(rows_hbm, rows_ref, rows_sem)
    ids_copy.start()
    rows_copy.start()
    ids_copy.wait()
    chosen = placement(own_ref[0], ids_ref[...], groups).astype(jnp.bfloat16)
    chosen_ref[...] = chosen
    rows_copy.wait()
    ordered = jnp.dot(chosen, rows_ref[...], preferred_element_type=jnp.float32)
    ordered = ordered.astype(jnp.bfloat16)
    size = ordered.shape[0] // groups
    for k, out_ref in enumerate(out_refs):
        out_ref[...] = ordered[k * size : (k + 1) * size, :]


def inverse_norms(rows):
    wide = rows.astype(jnp.float32)
    return lax.rsqrt(jnp.sum(wide * wide, axis=1, keepdims=True) + 1e-06)


def add_columns(rows, col_refs, total, dens):
    count = rows.shape[0]
    scale = inverse_norms(rows) * (beta_scale * math.log2(math.e))
    blocks = [
        (col_ref, start)
        for col_ref in col_refs
        for start in range(0, col_ref.shape[0], count)
    ]
    for col_ref, start in blocks:
        cols = col_ref[start : min(start + count, col_ref.shape[0]), :]
        size = cols.shape[0]
        col_inv = as_row(inverse_norms(cols))
        raw = lax.dot_general(
            rows, cols, (((1,), (1,)), ((), ())), preferred_element_type=jnp.float32
        )
        weight = jnp.exp2(raw * scale * col_inv - beta_scale * math.log2(math.e))
        whole = size - size % LANES
        for lane in range(0, whole, LANES):
            dens += weight[:, lane : lane + LANES]
        if whole < size:
            part = jnp.sum(weight[:, whole:], axis=1, keepdims=True)
            dens += jnp.where(lax.broadcasted_iota(jnp.int32, dens.shape, 1) == 0, part, 0.0)
        coef = (weight * col_inv).astype(jnp.bfloat16)
        total += jnp.dot(coef, cols, preferred_element_type=jnp.float32)
    return total, dens


def add_kernel(n_blocks, rows_ref, *refs):
    col_refs, sum_refs, (total_ref, dens_ref) = (
        refs[:n_blocks],
        refs[n_blocks:-2],
        refs[-2:],
    )
    if sum_refs:
        total, dens = (ref[...] for ref in sum_refs)
    else:
        total = jnp.zeros(total_ref.shape, jnp.float32)
        dens = jnp.zeros(dens_ref.shape, jnp.float32)
    total, dens = add_columns(rows_ref[...], col_refs, total, dens)
    total_ref[...] = total
    dens_ref[...] = dens


def exponent(value):
    return jnp.floor(jnp.log2(jnp.maximum(value, 1e-30)))


def last_kernel(groups, rows_ref, total_ref, dens_ref, *refs):
    col_refs, out_refs = refs[:-groups], refs[-groups:]
    padded, width = out_refs[0].shape
    size = padded - EXTRA
    total, dens = add_columns(rows_ref[...], col_refs, total_ref[...], dens_ref[...])
    dens = jnp.sum(dens, axis=1, keepdims=True)
    power = exponent(jnp.max(jnp.abs(total), axis=1, keepdims=True))
    total = total * jnp.exp2(TOP - power)
    dens_power = exponent(dens)
    part = dens * jnp.exp2(-dens_power)
    aside = [power, dens_power]
    for k in range(3):
        piece = part.astype(jnp.bfloat16).astype(jnp.float32)
        aside.append(piece * 2.0 ** (8 * k))
        part = part - piece
    for k, out_ref in enumerate(out_refs[::-1]):
        rows = slice(k * size, (k + 1) * size)
        out_ref[:size, :] = total[rows, :]
        out_ref[size:, :] = jnp.zeros((EXTRA, width), jnp.float32)
        for line, column in enumerate(aside):
            out_ref[size + line : size + line + 1, :size] = as_row(column[rows, :])


def restore_kernel(chosen_ref, *refs):
    part_refs, (total_ref, dens_ref) = refs[:-2], refs[-2:]
    groups = len(part_refs)
    size = part_refs[0].shape[0] - EXTRA
    chosen = chosen_ref[...]
    sums, dens = [], []
    for part_ref in part_refs[::-1]:
        power, dens_power, *pieces = [
            as_column(part_ref[size + line : size + line + 1, :size])
            for line in range(5)
        ]
        sums.append(part_ref[:size, :] * jnp.exp2(power - TOP))
        part = sum(piece * 2.0 ** (-8 * j) for j, piece in enumerate(pieces))
        dens.append(part * jnp.exp2(dens_power))
    dens_ref[...] = jnp.sum(
        chosen.astype(jnp.float32) * jnp.concatenate(dens, axis=0), axis=0, keepdims=True
    )
    rest = jnp.concatenate(sums, axis=0)
    back = jnp.zeros(rest.shape, jnp.float32)
    for _ in range(2):
        piece = rest.astype(jnp.bfloat16)
        rest = rest - piece.astype(jnp.float32)
        back += lax.dot_general(
            chosen, piece, (((0,), (0,)), ((), ())), preferred_element_type=jnp.float32
        )
    total_ref[...] = back


def on_device(n_gr, n_gc, embeddings, cluster_ids):
    count, width = embeddings.shape
    size = count // n_gr
    own = lax.axis_index("gr").astype(jnp.int32).reshape(1)
    ids = cluster_ids.reshape(1, count)

    chosen, *parts = pl.pallas_call(
        sort_kernel,
        out_shape=[jax.ShapeDtypeStruct((count, count), jnp.bfloat16)]
        + [jax.ShapeDtypeStruct((size, width), jnp.bfloat16)] * n_gr,
        in_specs=[SMEM, HBM, HBM],
        out_specs=[VMEM] * (1 + n_gr),
        scratch_shapes=[
            pltpu.VMEM((1, count), jnp.int32),
            pltpu.VMEM((count, width), embeddings.dtype),
            pltpu.SemaphoreType.DMA,
            pltpu.SemaphoreType.DMA,
        ],
        compiler_params=GRANT,
        name="sort_rows",
    )(own, in_hbm(ids), in_hbm(embeddings))

    def along_gr(part, bits):
        return lax.ppermute(part, "gr", [(i, i ^ bits) for i in range(n_gr)])

    def along_gc(block, bits):
        return lax.ppermute(block, "gc", [(i, i ^ bits) for i in range(n_gc)])

    def other_core(block):
        return along_gc(block, 1)

    def cost(*blocks):
        pairs = count * sum(block.shape[0] for block in blocks)
        return pl.CostEstimate(
            flops=4 * pairs * width,
            bytes_accessed=0,
            transcendentals=pairs,
        )

    held = [parts[0]] + [along_gr(parts[k], k) for k in range(1, n_gr)]
    half = n_gr // 2
    early = jnp.concatenate(held[:half], axis=0)
    late = jnp.concatenate(held[half:], axis=0)
    first = [early] + [along_gc(early, k) for k in range(2, n_gc, 2)]
    second = [late] + [along_gc(late, k) for k in range(2, n_gc, 2)]
    if n_gc == 8:
        direct = early.shape[0] // 2
        split = (direct + early.shape[0]) // 2
        first[3] = along_gc(early[:direct], 6)
        second[1] = along_gc(jnp.concatenate([late, first[2][split:]], axis=0), 2)
        second[2] = along_gc(jnp.concatenate([late, first[1][direct:split]], axis=0), 4)
    first = jnp.concatenate(first, axis=0)
    rows = jnp.concatenate(held, axis=0)
    middle = len(second) // 2
    second, third = (
        jnp.concatenate(second[:middle], axis=0),
        jnp.concatenate(second[middle:], axis=0),
    )

    def add_sums(sums, name, *blocks):
        return pl.pallas_call(
            functools.partial(add_kernel, len(blocks)),
            out_shape=[
                jax.ShapeDtypeStruct((count, width), jnp.float32),
                jax.ShapeDtypeStruct((count, LANES), jnp.float32),
            ],
            in_specs=[VMEM] * (1 + len(blocks) + len(sums)),
            out_specs=[VMEM] * 2,
            compiler_params=GRANT,
            cost_estimate=cost(*blocks),
            name=name,
        )(rows, *blocks, *sums)

    total, dens = add_sums([], "early_sums", first, other_core(first))
    total, dens = add_sums([total, dens], "middle_sums", second, third)
    late = [other_core(second), other_core(third)]
    sums = pl.pallas_call(
        functools.partial(last_kernel, n_gr),
        out_shape=[jax.ShapeDtypeStruct((size + EXTRA, width), jnp.float32)] * n_gr,
        in_specs=[VMEM] * (3 + len(late)),
        out_specs=[VMEM] * n_gr,
        compiler_params=GRANT,
        cost_estimate=cost(*late),
        name="last_sums",
    )(rows, total, dens, *late)[::-1]

    sent = [part.astype(jnp.float16) for part in sums]
    back = [None] * n_gr
    back[0] = sent[0]
    for k in sorted(range(1, n_gr), reverse=True):
        back[k] = along_gr(sent[k], k)
    back = [part.astype(jnp.float32) for part in back]
    neighbour_sum, density = pl.pallas_call(
        restore_kernel,
        out_shape=[
            jax.ShapeDtypeStruct((count, width), jnp.float32),
            jax.ShapeDtypeStruct((1, count), jnp.float32),
        ],
        in_specs=[VMEM] * (1 + n_gr),
        out_specs=[VMEM, VMEM],
        compiler_params=GRANT,
        name="restore_rows",
    )(chosen, *back[::-1])
    return (neighbour_sum, density.reshape(count))


def solution(mesh):
    in_specs = (P(("gr", "gc"), None), P(("gr", "gc")))
    out_specs = (P(("gr", "gc"), None), P(("gr", "gc")))
    return jax.shard_map(
        functools.partial(on_device, mesh.shape["gr"], mesh.shape["gc"]),
        mesh=mesh,
        in_specs=in_specs,
        out_specs=out_specs,
        check_vma=False,
    )
```

```python
import functools
import math

import jax
import jax.numpy as jnp
from jax import lax
from jax.experimental import pallas as pl
from jax.experimental.pallas import tpu as pltpu
from jax.sharding import PartitionSpec as P

beta_scale = 16.0
LANES = 128
EXTRA = 8
TOP = 14.0
VMEM = pl.BlockSpec(memory_space=pltpu.VMEM)
HBM = pl.BlockSpec(memory_space=pltpu.HBM)
SMEM = pl.BlockSpec(memory_space=pltpu.SMEM)
GRANT = pltpu.CompilerParams(vmem_limit_bytes=40 * 1024 * 1024)


def in_hbm(array):
    return pltpu.with_memory_space_constraint(array, pltpu.HBM)


def diagonal(count):
    first = lax.broadcasted_iota(jnp.int32, (count, count), 0)
    second = lax.broadcasted_iota(jnp.int32, (count, count), 1)
    return first == second


def as_row(column):
    return jnp.sum(
        jnp.where(diagonal(column.shape[0]), column, jnp.zeros_like(column)),
        axis=0,
        keepdims=True,
    )


def as_column(row):
    return jnp.sum(
        jnp.where(diagonal(row.shape[1]), row, jnp.zeros_like(row)),
        axis=1,
        keepdims=True,
    )


def placement(own, ids, groups):
    count = ids.shape[1]
    first = lax.broadcasted_iota(jnp.int32, (count, count), 0)
    second = lax.broadcasted_iota(jnp.int32, (count, count), 1)
    earlier = jnp.where((as_column(ids) == ids) & (first < second), 1, 0)
    rank = jnp.sum(earlier, axis=0, keepdims=True)
    slot = (ids ^ own) * (count // groups) + rank
    return jnp.where(first == slot, 1.0, 0.0)


def sort_kernel(own_ref, ids_hbm, rows_hbm, *refs):
    chosen_ref, *out_refs = refs[:-4]
    ids_ref, rows_ref, ids_sem, rows_sem = refs[-4:]
    groups = len(out_refs)
    ids_copy = pltpu.make_async_copy(ids_hbm, ids_ref, ids_sem)
    rows_copy = pltpu.make_async_copy(rows_hbm, rows_ref, rows_sem)
    ids_copy.start()
    rows_copy.start()
    ids_copy.wait()
    chosen = placement(own_ref[0], ids_ref[...], groups).astype(jnp.bfloat16)
    chosen_ref[...] = chosen
    rows_copy.wait()
    ordered = jnp.dot(chosen, rows_ref[...], preferred_element_type=jnp.float32)
    ordered = ordered.astype(jnp.bfloat16)
    size = ordered.shape[0] // groups
    for k, out_ref in enumerate(out_refs):
        out_ref[...] = ordered[k * size : (k + 1) * size, :]


def inverse_norms(rows):
    wide = rows.astype(jnp.float32)
    return lax.rsqrt(jnp.sum(wide * wide, axis=1, keepdims=True) + 1e-06)


def add_columns(rows, col_refs, total, dens):
    count = rows.shape[0]
    scale = inverse_norms(rows) * (beta_scale * math.log2(math.e))
    blocks = [
        (col_ref, start)
        for col_ref in col_refs
        for start in range(0, col_ref.shape[0], count)
    ]
    for col_ref, start in blocks:
        cols = col_ref[start : min(start + count, col_ref.shape[0]), :]
        size = cols.shape[0]
        col_inv = as_row(inverse_norms(cols))
        raw = lax.dot_general(
            rows, cols, (((1,), (1,)), ((), ())), preferred_element_type=jnp.float32
        )
        weight = jnp.exp2(raw * scale * col_inv - beta_scale * math.log2(math.e))
        whole = size - size % LANES
        for lane in range(0, whole, LANES):
            dens += weight[:, lane : lane + LANES]
        if whole < size:
            part = jnp.sum(weight[:, whole:], axis=1, keepdims=True)
            dens += jnp.where(lax.broadcasted_iota(jnp.int32, dens.shape, 1) == 0, part, 0.0)
        coef = (weight * col_inv).astype(jnp.bfloat16)
        total += jnp.dot(coef, cols, preferred_element_type=jnp.float32)
    return total, dens


def add_kernel(n_blocks, rows_ref, *refs):
    col_refs, sum_refs, (total_ref, dens_ref) = (
        refs[:n_blocks],
        refs[n_blocks:-2],
        refs[-2:],
    )
    if sum_refs:
        total, dens = (ref[...] for ref in sum_refs)
    else:
        total = jnp.zeros(total_ref.shape, jnp.float32)
        dens = jnp.zeros(dens_ref.shape, jnp.float32)
    total, dens = add_columns(rows_ref[...], col_refs, total, dens)
    total_ref[...] = total
    dens_ref[...] = dens


def exponent(value):
    return jnp.floor(jnp.log2(jnp.maximum(value, 1e-30)))


def last_kernel(groups, rows_ref, total_ref, dens_ref, *refs):
    col_refs, out_refs = refs[:-groups], refs[-groups:]
    padded, width = out_refs[0].shape
    size = padded - EXTRA
    total, dens = add_columns(rows_ref[...], col_refs, total_ref[...], dens_ref[...])
    dens = jnp.sum(dens, axis=1, keepdims=True)
    power = exponent(jnp.max(jnp.abs(total), axis=1, keepdims=True))
    total = total * jnp.exp2(TOP - power)
    dens_power = exponent(dens)
    part = dens * jnp.exp2(-dens_power)
    aside = [power, dens_power]
    for k in range(3):
        piece = part.astype(jnp.bfloat16).astype(jnp.float32)
        aside.append(piece * 2.0 ** (8 * k))
        part = part - piece
    for k, out_ref in enumerate(out_refs[::-1]):
        rows = slice(k * size, (k + 1) * size)
        out_ref[:size, :] = total[rows, :]
        out_ref[size:, :] = jnp.zeros((EXTRA, width), jnp.float32)
        for line, column in enumerate(aside):
            out_ref[size + line : size + line + 1, :size] = as_row(column[rows, :])


def restore_kernel(chosen_ref, *refs):
    part_refs, (total_ref, dens_ref) = refs[:-2], refs[-2:]
    groups = len(part_refs)
    size = part_refs[0].shape[0] - EXTRA
    chosen = chosen_ref[...]
    sums, dens = [], []
    for part_ref in part_refs[::-1]:
        power, dens_power, *pieces = [
            as_column(part_ref[size + line : size + line + 1, :size])
            for line in range(5)
        ]
        sums.append(part_ref[:size, :] * jnp.exp2(power - TOP))
        part = sum(piece * 2.0 ** (-8 * j) for j, piece in enumerate(pieces))
        dens.append(part * jnp.exp2(dens_power))
    dens_ref[...] = jnp.sum(
        chosen.astype(jnp.float32) * jnp.concatenate(dens, axis=0), axis=0, keepdims=True
    )
    rest = jnp.concatenate(sums, axis=0)
    back = jnp.zeros(rest.shape, jnp.float32)
    for _ in range(2):
        piece = rest.astype(jnp.bfloat16)
        rest = rest - piece.astype(jnp.float32)
        back += lax.dot_general(
            chosen, piece, (((0,), (0,)), ((), ())), preferred_element_type=jnp.float32
        )
    total_ref[...] = back


def on_device(n_gr, n_gc, embeddings, cluster_ids):
    count, width = embeddings.shape
    size = count // n_gr
    own = lax.axis_index("gr").astype(jnp.int32).reshape(1)
    ids = cluster_ids.reshape(1, count)

    chosen, *parts = pl.pallas_call(
        sort_kernel,
        out_shape=[jax.ShapeDtypeStruct((count, count), jnp.bfloat16)]
        + [jax.ShapeDtypeStruct((size, width), jnp.bfloat16)] * n_gr,
        in_specs=[SMEM, HBM, HBM],
        out_specs=[VMEM] * (1 + n_gr),
        scratch_shapes=[
            pltpu.VMEM((1, count), jnp.int32),
            pltpu.VMEM((count, width), embeddings.dtype),
            pltpu.SemaphoreType.DMA,
            pltpu.SemaphoreType.DMA,
        ],
        compiler_params=GRANT,
        name="sort_rows",
    )(own, in_hbm(ids), in_hbm(embeddings))

    def along_gr(part, bits):
        return lax.ppermute(part, "gr", [(i, i ^ bits) for i in range(n_gr)])

    def along_gc(block, bits):
        return lax.ppermute(block, "gc", [(i, i ^ bits) for i in range(n_gc)])

    def other_core(block):
        return along_gc(block, 1)

    def cost(*blocks):
        pairs = count * sum(block.shape[0] for block in blocks)
        return pl.CostEstimate(
            flops=4 * pairs * width,
            bytes_accessed=0,
            transcendentals=pairs,
        )

    held = [parts[0]] + [along_gr(parts[k], k) for k in range(1, n_gr)]
    half = n_gr // 2
    sides = [k for k in range(2, n_gc, 2) if not k & (k - 1)]
    corners = [k for k in range(2, n_gc, 2) if k & (k - 1)]
    early = jnp.concatenate(held[:half], axis=0)
    late = jnp.concatenate(held[half:], axis=0)
    rest = jnp.concatenate(held[1:half], axis=0)
    filler = [along_gc(held[0], k) for k in corners]
    filler, rest = lax.optimization_barrier((filler, rest))
    first = [early] + [along_gc(early, k) for k in sides] + filler
    rests = [along_gc(rest, k) for k in corners]
    late_x = late_y = late_d = late
    late_d, rests = lax.optimization_barrier((late, rests))
    second = [late] + [along_gc(late_x, k) for k in sides[:1]] + [along_gc(late_y, k) for k in sides[1:]] + [along_gc(late_d, k) for k in corners]
    first = jnp.concatenate(first + rests, axis=0)
    rows = jnp.concatenate(held, axis=0)
    second = jnp.concatenate(second, axis=0)

    def add_sums(sums, name, *blocks):
        return pl.pallas_call(
            functools.partial(add_kernel, len(blocks)),
            out_shape=[
                jax.ShapeDtypeStruct((count, width), jnp.float32),
                jax.ShapeDtypeStruct((count, LANES), jnp.float32),
            ],
            in_specs=[VMEM] * (1 + len(blocks) + len(sums)),
            out_specs=[VMEM] * 2,
            compiler_params=GRANT,
            cost_estimate=cost(*blocks),
            name=name,
        )(rows, *blocks, *sums)

    total, dens = add_sums([], "early_sums", first, other_core(first))
    total, dens = add_sums([total, dens], "middle_sums", second)
    late = [other_core(second)]
    sums = pl.pallas_call(
        functools.partial(last_kernel, n_gr),
        out_shape=[jax.ShapeDtypeStruct((size + EXTRA, width), jnp.float32)] * n_gr,
        in_specs=[VMEM] * (3 + len(late)),
        out_specs=[VMEM] * n_gr,
        compiler_params=GRANT,
        cost_estimate=cost(*late),
        name="last_sums",
    )(rows, total, dens, *late)[::-1]

    sent = [part.astype(jnp.float16) for part in sums]
    back = [None] * n_gr
    back[0] = sent[0]
    for k in sorted(range(1, n_gr), reverse=True):
        back[k] = along_gr(sent[k], k)
    back = [part.astype(jnp.float32) for part in back]
    neighbour_sum, density = pl.pallas_call(
        restore_kernel,
        out_shape=[
            jax.ShapeDtypeStruct((count, width), jnp.float32),
            jax.ShapeDtypeStruct((1, count), jnp.float32),
        ],
        in_specs=[VMEM] * (1 + n_gr),
        out_specs=[VMEM, VMEM],
        compiler_params=GRANT,
        name="restore_rows",
    )(chosen, *back[::-1])
    return (neighbour_sum, density.reshape(count))


def solution(mesh):
    in_specs = (P(("gr", "gc"), None), P(("gr", "gc")))
    out_specs = (P(("gr", "gc"), None), P(("gr", "gc")))
    return jax.shard_map(
        functools.partial(on_device, mesh.shape["gr"], mesh.shape["gc"]),
        mesh=mesh,
        in_specs=in_specs,
        out_specs=out_specs,
        check_vma=False,
    )
```

```python
import functools
import math

import jax
import jax.numpy as jnp
from jax import lax
from jax.experimental import pallas as pl
from jax.experimental.pallas import tpu as pltpu
from jax.sharding import PartitionSpec as P

beta_scale = 16.0
floor_weight = math.exp(-beta_scale)
BLOCK = 256
LANES = 128
EXTRA = 8
TOP = 14.0
VMEM = pl.BlockSpec(memory_space=pltpu.VMEM)
HBM = pl.BlockSpec(memory_space=pltpu.HBM)
SMEM = pl.BlockSpec(memory_space=pltpu.SMEM)
GRANT = pltpu.CompilerParams(vmem_limit_bytes=40 * 1024 * 1024)


def in_hbm(array):
    return pltpu.with_memory_space_constraint(array, pltpu.HBM)


def diagonal(count):
    first = lax.broadcasted_iota(jnp.int32, (count, count), 0)
    second = lax.broadcasted_iota(jnp.int32, (count, count), 1)
    return first == second


def as_row(column):
    return jnp.sum(
        jnp.where(diagonal(column.shape[0]), column, jnp.zeros_like(column)),
        axis=0,
        keepdims=True,
    )


def as_column(row):
    return jnp.sum(
        jnp.where(diagonal(row.shape[1]), row, jnp.zeros_like(row)),
        axis=1,
        keepdims=True,
    )


def placement(own, ids, groups):
    count = ids.shape[1]
    first = lax.broadcasted_iota(jnp.int32, (count, count), 0)
    second = lax.broadcasted_iota(jnp.int32, (count, count), 1)
    earlier = jnp.where((as_column(ids) == ids) & (first < second), 1, 0)
    rank = jnp.sum(earlier, axis=0, keepdims=True)
    slot = (ids ^ own) * (count // groups) + rank
    return jnp.where(first == slot, 1.0, 0.0)


def sort_kernel(own_ref, ids_hbm, rows_hbm, *refs):
    chosen_ref, *out_refs = refs[:-4]
    ids_ref, rows_ref, ids_sem, rows_sem = refs[-4:]
    groups = len(out_refs)
    ids_copy = pltpu.make_async_copy(ids_hbm, ids_ref, ids_sem)
    rows_copy = pltpu.make_async_copy(rows_hbm, rows_ref, rows_sem)
    ids_copy.start()
    rows_copy.start()
    ids_copy.wait()
    chosen = placement(own_ref[0], ids_ref[...], groups).astype(jnp.bfloat16)
    chosen_ref[...] = chosen
    rows_copy.wait()
    ordered = jnp.dot(chosen, rows_ref[...], preferred_element_type=jnp.float32)
    ordered = ordered.astype(jnp.bfloat16)
    size = ordered.shape[0] // groups
    for k, out_ref in enumerate(out_refs):
        out_ref[...] = ordered[k * size : (k + 1) * size, :]


def product(left, right, dims):
    return lax.dot_general(
        left, right, (dims, ((), ())), preferred_element_type=jnp.float32
    )


def add_columns(rows, scale, col_refs, total, dens):
    for col_ref in col_refs:
        for start in range(0, col_ref.shape[0], BLOCK):
            cols = col_ref[start : min(start + BLOCK, col_ref.shape[0]), :]
            size = cols.shape[0]
            squares = jnp.where(diagonal(size), product(cols, cols, ((1,), (1,))), 0.0)
            col_inv = lax.rsqrt(jnp.sum(squares, axis=0, keepdims=True) + 1e-06)
            raw = product(rows, cols, ((1,), (1,)))
            weight = jnp.exp2(raw * scale * col_inv)
            whole = size - size % LANES
            for lane in range(0, whole, LANES):
                dens += weight[:, lane : lane + LANES]
            if whole < size:
                part = jnp.sum(weight[:, whole:], axis=1, keepdims=True)
                lanes = lax.broadcasted_iota(jnp.int32, dens.shape, 1)
                dens += jnp.where(lanes == 0, part, 0.0)
            coef = (weight * (col_inv * floor_weight)).astype(jnp.bfloat16)
            total += product(coef, cols, ((1,), (0,)))
    return total, dens


def early_kernel(rows_ref, *refs):
    col_refs, (scale_ref, total_ref, dens_ref) = refs[:-3], refs[-3:]
    wide = rows_ref[...].astype(jnp.float32)
    scale = lax.rsqrt(jnp.sum(wide * wide, axis=1, keepdims=True) + 1e-06)
    scale = scale * (beta_scale * math.log2(math.e))
    scale_ref[...] = jnp.broadcast_to(scale, scale_ref.shape)
    total = jnp.zeros(total_ref.shape, jnp.float32)
    dens = jnp.zeros(dens_ref.shape, jnp.float32)
    total, dens = add_columns(rows_ref[...], scale, col_refs, total, dens)
    total_ref[...] = total
    dens_ref[...] = dens


def middle_kernel(rows_ref, scale_ref, total_ref, dens_ref, *refs):
    col_refs, (total_out, dens_out) = refs[:-2], refs[-2:]
    total, dens = add_columns(
        rows_ref[...], scale_ref[:, 0:1], col_refs, total_ref[...], dens_ref[...]
    )
    total_out[...] = total
    dens_out[...] = dens


def exponent(value):
    return jnp.floor(jnp.log2(jnp.maximum(value, 1e-30)))


def last_kernel(groups, rows_ref, scale_ref, total_ref, dens_ref, *refs):
    col_refs, out_refs = refs[:-groups], refs[-groups:]
    padded, width = out_refs[0].shape
    size = padded - EXTRA
    total, dens = add_columns(
        rows_ref[...], scale_ref[:, 0:1], col_refs, total_ref[...], dens_ref[...]
    )
    dens = jnp.sum(dens, axis=1, keepdims=True) * floor_weight
    power = exponent(jnp.max(jnp.abs(total), axis=1, keepdims=True))
    total = total * jnp.exp2(TOP - power)
    dens_power = exponent(dens)
    part = dens * jnp.exp2(-dens_power)
    aside = [power, dens_power]
    for k in range(3):
        piece = part.astype(jnp.bfloat16).astype(jnp.float32)
        aside.append(piece * 2.0 ** (8 * k))
        part = part - piece
    for k, out_ref in enumerate(out_refs[::-1]):
        rows = slice(k * size, (k + 1) * size)
        out_ref[:size, :] = total[rows, :]
        out_ref[size:, :] = jnp.zeros((EXTRA, width), jnp.float32)
        for line, column in enumerate(aside):
            out_ref[size + line : size + line + 1, :size] = as_row(column[rows, :])


def restore_kernel(chosen_ref, *refs):
    part_refs, (total_ref, dens_ref) = refs[:-2], refs[-2:]
    groups = len(part_refs)
    size = part_refs[0].shape[0] - EXTRA
    chosen = chosen_ref[...]
    sums, dens = [], []
    for part_ref in part_refs[::-1]:
        power, dens_power, *pieces = [
            as_column(part_ref[size + line : size + line + 1, :size])
            for line in range(5)
        ]
        sums.append(part_ref[:size, :] * jnp.exp2(power - TOP))
        part = sum(piece * 2.0 ** (-8 * j) for j, piece in enumerate(pieces))
        dens.append(part * jnp.exp2(dens_power))
    dens_ref[...] = jnp.sum(
        chosen.astype(jnp.float32) * jnp.concatenate(dens, axis=0), axis=0, keepdims=True
    )
    rest = jnp.concatenate(sums, axis=0)
    back = jnp.zeros(rest.shape, jnp.float32)
    for _ in range(2):
        piece = rest.astype(jnp.bfloat16)
        rest = rest - piece.astype(jnp.float32)
        back += lax.dot_general(
            chosen, piece, (((0,), (0,)), ((), ())), preferred_element_type=jnp.float32
        )
    total_ref[...] = back


def on_device(n_gr, n_gc, embeddings, cluster_ids):
    count, width = embeddings.shape
    size = count // n_gr
    own = lax.axis_index("gr").astype(jnp.int32).reshape(1)
    ids = cluster_ids.reshape(1, count)

    chosen, *parts = pl.pallas_call(
        sort_kernel,
        out_shape=[jax.ShapeDtypeStruct((count, count), jnp.bfloat16)]
        + [jax.ShapeDtypeStruct((size, width), jnp.bfloat16)] * n_gr,
        in_specs=[SMEM, HBM, HBM],
        out_specs=[VMEM] * (1 + n_gr),
        scratch_shapes=[
            pltpu.VMEM((1, count), jnp.int32),
            pltpu.VMEM((count, width), embeddings.dtype),
            pltpu.SemaphoreType.DMA,
            pltpu.SemaphoreType.DMA,
        ],
        compiler_params=GRANT,
        name="sort_rows",
    )(own, in_hbm(ids), in_hbm(embeddings))

    def along_gr(part, bits):
        return lax.ppermute(part, "gr", [(i, i ^ bits) for i in range(n_gr)])

    def along_gc(block, bits):
        return lax.ppermute(block, "gc", [(i, i ^ bits) for i in range(n_gc)])

    def cost(*blocks):
        pairs = count * sum(block.shape[0] for block in blocks)
        return pl.CostEstimate(
            flops=4 * pairs * width,
            bytes_accessed=0,
            transcendentals=pairs,
        )

    held = [parts[0]] + [along_gr(parts[k], k) for k in range(1, n_gr)]
    half = n_gr // 2
    chunks = []
    for pieces in (held[:half], held[half:]):
        block = jnp.concatenate(pieces, axis=0)
        chunks.append([block] + [along_gc(block, k) for k in range(2, n_gc, 2)])
    rows = jnp.concatenate(held, axis=0)
    near = jnp.concatenate(chunks[0], axis=0)
    near, rows = lax.optimization_barrier((near, rows))
    late = jnp.concatenate(chunks[1], axis=0)
    early = [near, along_gc(near, 1)]

    scale, total, dens = pl.pallas_call(
        early_kernel,
        out_shape=[
            jax.ShapeDtypeStruct((count, LANES), jnp.float32),
            jax.ShapeDtypeStruct((count, width), jnp.float32),
            jax.ShapeDtypeStruct((count, LANES), jnp.float32),
        ],
        in_specs=[VMEM] * 3,
        out_specs=[VMEM] * 3,
        compiler_params=GRANT,
        cost_estimate=cost(*early),
        name="early_sums",
    )(rows, *early)
    total, dens = pl.pallas_call(
        middle_kernel,
        out_shape=[
            jax.ShapeDtypeStruct((count, width), jnp.float32),
            jax.ShapeDtypeStruct((count, LANES), jnp.float32),
        ],
        in_specs=[VMEM] * 5,
        out_specs=[VMEM] * 2,
        compiler_params=GRANT,
        cost_estimate=cost(late),
        name="middle_sums",
    )(rows, scale, total, dens, late)
    late = along_gc(late, 1)
    sums = pl.pallas_call(
        functools.partial(last_kernel, n_gr),
        out_shape=[jax.ShapeDtypeStruct((size + EXTRA, width), jnp.float32)] * n_gr,
        in_specs=[VMEM] * 5,
        out_specs=[VMEM] * n_gr,
        compiler_params=GRANT,
        cost_estimate=cost(late),
        name="last_sums",
    )(rows, scale, total, dens, late)[::-1]

    sent = [part.astype(jnp.float16) for part in sums]
    back = [None] * n_gr
    back[0] = sent[0]
    for k in sorted(range(1, n_gr), reverse=True):
        back[k] = along_gr(sent[k], k)
    back = [part.astype(jnp.float32) for part in back]
    neighbour_sum, density = pl.pallas_call(
        restore_kernel,
        out_shape=[
            jax.ShapeDtypeStruct((count, width), jnp.float32),
            jax.ShapeDtypeStruct((1, count), jnp.float32),
        ],
        in_specs=[VMEM] * (1 + n_gr),
        out_specs=[VMEM, VMEM],
        compiler_params=GRANT,
        name="restore_rows",
    )(chosen, *back[::-1])
    return (neighbour_sum, density.reshape(count))


def solution(mesh):
    in_specs = (P(("gr", "gc"), None), P(("gr", "gc")))
    out_specs = (P(("gr", "gc"), None), P(("gr", "gc")))
    return jax.shard_map(
        functools.partial(on_device, mesh.shape["gr"], mesh.shape["gc"]),
        mesh=mesh,
        in_specs=in_specs,
        out_specs=out_specs,
        check_vma=False,
    )
```

```python
import functools
import math

import jax
import jax.numpy as jnp
from jax import lax
from jax.experimental import pallas as pl
from jax.experimental.pallas import tpu as pltpu
from jax.sharding import PartitionSpec as P

beta_scale = 16.0
LANES = 128
EXTRA = 8
TOP = 14.0
VMEM = pl.BlockSpec(memory_space=pltpu.VMEM)
HBM = pl.BlockSpec(memory_space=pltpu.HBM)
SMEM = pl.BlockSpec(memory_space=pltpu.SMEM)
GRANT = pltpu.CompilerParams(vmem_limit_bytes=40 * 1024 * 1024)


def in_hbm(array):
    return pltpu.with_memory_space_constraint(array, pltpu.HBM)


def diagonal(count):
    first = lax.broadcasted_iota(jnp.int32, (count, count), 0)
    second = lax.broadcasted_iota(jnp.int32, (count, count), 1)
    return first == second


def as_row(column):
    return jnp.sum(
        jnp.where(diagonal(column.shape[0]), column, jnp.zeros_like(column)),
        axis=0,
        keepdims=True,
    )


def as_column(row):
    return jnp.sum(
        jnp.where(diagonal(row.shape[1]), row, jnp.zeros_like(row)),
        axis=1,
        keepdims=True,
    )


def placement(own, ids, groups):
    count = ids.shape[1]
    first = lax.broadcasted_iota(jnp.int32, (count, count), 0)
    second = lax.broadcasted_iota(jnp.int32, (count, count), 1)
    earlier = jnp.where((as_column(ids) == ids) & (first < second), 1, 0)
    rank = jnp.sum(earlier, axis=0, keepdims=True)
    slot = (ids ^ own) * (count // groups) + rank
    return jnp.where(first == slot, 1.0, 0.0)


def sort_kernel(own_ref, ids_hbm, rows_hbm, *refs):
    chosen_ref, *out_refs = refs[:-4]
    ids_ref, rows_ref, ids_sem, rows_sem = refs[-4:]
    groups = len(out_refs)
    ids_copy = pltpu.make_async_copy(ids_hbm, ids_ref, ids_sem)
    rows_copy = pltpu.make_async_copy(rows_hbm, rows_ref, rows_sem)
    ids_copy.start()
    rows_copy.start()
    ids_copy.wait()
    chosen = placement(own_ref[0], ids_ref[...], groups).astype(jnp.bfloat16)
    chosen_ref[...] = chosen
    rows_copy.wait()
    ordered = jnp.dot(chosen, rows_ref[...], preferred_element_type=jnp.float32)
    ordered = ordered.astype(jnp.bfloat16)
    size = ordered.shape[0] // groups
    for k, out_ref in enumerate(out_refs):
        out_ref[...] = ordered[k * size : (k + 1) * size, :]


def inverse_norms(rows):
    wide = rows.astype(jnp.float32)
    return lax.rsqrt(jnp.sum(wide * wide, axis=1, keepdims=True) + 1e-06)


def add_columns(rows, col_refs, total, dens):
    count = rows.shape[0]
    scale = inverse_norms(rows) * (beta_scale * math.log2(math.e))
    blocks = [
        (col_ref, start)
        for col_ref in col_refs
        for start in range(0, col_ref.shape[0], count)
    ]
    for col_ref, start in blocks:
        cols = col_ref[start : min(start + count, col_ref.shape[0]), :]
        size = cols.shape[0]
        col_inv = as_row(inverse_norms(cols))
        raw = lax.dot_general(
            rows, cols, (((1,), (1,)), ((), ())), preferred_element_type=jnp.float32
        )
        weight = jnp.exp2(raw * scale * col_inv - beta_scale * math.log2(math.e))
        whole = size - size % LANES
        for lane in range(0, whole, LANES):
            dens += weight[:, lane : lane + LANES]
        if whole < size:
            part = jnp.sum(weight[:, whole:], axis=1, keepdims=True)
            dens += jnp.where(lax.broadcasted_iota(jnp.int32, dens.shape, 1) == 0, part, 0.0)
        coef = (weight * col_inv).astype(jnp.bfloat16)
        total += jnp.dot(coef, cols, preferred_element_type=jnp.float32)
    return total, dens


def first_kernel(rows_ref, *refs):
    col_refs, (total_ref, dens_ref) = refs[:-2], refs[-2:]
    total = jnp.zeros(total_ref.shape, jnp.float32)
    dens = jnp.zeros(dens_ref.shape, jnp.float32)
    total, dens = add_columns(rows_ref[...], col_refs, total, dens)
    total_ref[...] = total
    dens_ref[...] = dens


def middle_kernel(rows_ref, total_ref, dens_ref, *refs):
    col_refs, (total_out, dens_out) = refs[:-2], refs[-2:]
    total, dens = add_columns(rows_ref[...], col_refs, total_ref[...], dens_ref[...])
    total_out[...] = total
    dens_out[...] = dens


def exponent(value):
    return jnp.floor(jnp.log2(jnp.maximum(value, 1e-30)))


def last_kernel(half, rows_ref, total_ref, dens_ref, cols_ref, *out_refs):
    groups = len(out_refs) - half
    size = out_refs[half].shape[0]
    total, dens = add_columns(
        rows_ref[...], [cols_ref], total_ref[...], dens_ref[...]
    )
    dens = jnp.sum(dens, axis=1, keepdims=True)
    power = exponent(jnp.max(jnp.abs(total), axis=1, keepdims=True))
    total = total * jnp.exp2(TOP - power)
    dens_power = exponent(dens)
    part = dens * jnp.exp2(-dens_power)
    aside = [power, dens_power]
    for k in range(3):
        piece = part.astype(jnp.bfloat16).astype(jnp.float32)
        aside.append(piece * 2.0 ** (8 * k))
        part = part - piece
    for k in range(groups):
        rows = slice(k * size, (k + 1) * size)
        out_refs[k][:size, :] = total[rows, :]
        if k < half:
            aside_ref, top = out_refs[k], size
            aside_ref[size:, :] = jnp.zeros((EXTRA, total.shape[1]), jnp.float32)
        else:
            aside_ref, top = out_refs[half + k], 0
            aside_ref[...] = jnp.zeros(aside_ref.shape, jnp.float32)
        for line, column in enumerate(aside):
            aside_ref[top + line : top + line + 1, :size] = as_row(column[rows, :])


def restore_kernel(half, chosen_ref, *refs):
    refs, (total_ref, dens_ref) = refs[:-2], refs[-2:]
    groups = len(refs) - half
    part_refs = refs[groups - 1 :: -1] + refs[: groups - 1 : -1]
    size = part_refs[half].shape[0]
    chosen = chosen_ref[...]
    sums, dens = [], []
    for k in range(groups):
        aside_ref, top = (part_refs[k], size) if k < half else (part_refs[half + k], 0)
        power, dens_power, *pieces = [
            as_column(aside_ref[top + line : top + line + 1, :size])
            for line in range(5)
        ]
        sums.append(part_refs[k][:size, :] * jnp.exp2(power - TOP))
        part = sum(piece * 2.0 ** (-8 * j) for j, piece in enumerate(pieces))
        dens.append(part * jnp.exp2(dens_power))
    dens_ref[...] = jnp.sum(
        chosen.astype(jnp.float32) * jnp.concatenate(dens, axis=0), axis=0, keepdims=True
    )
    rest = jnp.concatenate(sums, axis=0)
    back = jnp.zeros(rest.shape, jnp.float32)
    for _ in range(2):
        piece = rest.astype(jnp.bfloat16)
        rest = rest - piece.astype(jnp.float32)
        back += lax.dot_general(
            chosen, piece, (((0,), (0,)), ((), ())), preferred_element_type=jnp.float32
        )
    total_ref[...] = back


def on_device(n_gr, n_gc, embeddings, cluster_ids):
    count, width = embeddings.shape
    size = count // n_gr
    own = lax.axis_index("gr").astype(jnp.int32).reshape(1)
    ids = cluster_ids.reshape(1, count)

    chosen, *parts = pl.pallas_call(
        sort_kernel,
        out_shape=[jax.ShapeDtypeStruct((count, count), jnp.bfloat16)]
        + [jax.ShapeDtypeStruct((size, width), jnp.bfloat16)] * n_gr,
        in_specs=[SMEM, HBM, HBM],
        out_specs=[VMEM] * (1 + n_gr),
        scratch_shapes=[
            pltpu.VMEM((1, count), jnp.int32),
            pltpu.VMEM((count, width), embeddings.dtype),
            pltpu.SemaphoreType.DMA,
            pltpu.SemaphoreType.DMA,
        ],
        compiler_params=GRANT,
        name="sort_rows",
    )(own, in_hbm(ids), in_hbm(embeddings))

    def along_gr(part, bits):
        return lax.ppermute(part, "gr", [(i, i ^ bits) for i in range(n_gr)])

    def along_gc(block, bits):
        return lax.ppermute(block, "gc", [(i, i ^ bits) for i in range(n_gc)])

    def other_core(block):
        return along_gc(block, 1)

    def cost(*blocks):
        pairs = count * sum(block.shape[0] for block in blocks)
        return pl.CostEstimate(
            flops=4 * pairs * width,
            bytes_accessed=0,
            transcendentals=pairs,
        )

    held = [parts[0]] + [along_gr(parts[k], k) for k in range(1, n_gr)]
    half = n_gr // 2
    chunks = []
    for pieces in (held[:half], held[half:]):
        block = jnp.concatenate(pieces, axis=0)
        near = [block] + [along_gc(block, k) for k in range(2, n_gc, 2)]
        chunks.append(jnp.concatenate(near, axis=0))
    rows = jnp.concatenate(held, axis=0)
    chunks[0], rows = lax.optimization_barrier((chunks[0], rows))
    early = [chunks[0], other_core(chunks[0])]

    total, dens = pl.pallas_call(
        first_kernel,
        out_shape=[
            jax.ShapeDtypeStruct((count, width), jnp.float32),
            jax.ShapeDtypeStruct((count, LANES), jnp.float32),
        ],
        in_specs=[VMEM] * (1 + len(early)),
        out_specs=[VMEM] * 2,
        compiler_params=GRANT,
        cost_estimate=cost(*early),
        name="early_sums",
    )(rows, *early)
    total, dens = pl.pallas_call(
        middle_kernel,
        out_shape=[
            jax.ShapeDtypeStruct((count, width), jnp.float32),
            jax.ShapeDtypeStruct((count, LANES), jnp.float32),
        ],
        in_specs=[VMEM] * 4,
        out_specs=[VMEM] * 2,
        compiler_params=GRANT,
        cost_estimate=cost(chunks[1]),
        name="middle_sums",
    )(rows, total, dens, chunks[1])
    late = [other_core(chunks[1])]
    sums = pl.pallas_call(
        functools.partial(last_kernel, half),
        out_shape=[jax.ShapeDtypeStruct((size + EXTRA, width), jnp.float32)] * half
        + [jax.ShapeDtypeStruct((size, width), jnp.float32)] * (n_gr - half)
        + [jax.ShapeDtypeStruct((EXTRA, LANES), jnp.float32)] * (n_gr - half),
        in_specs=[VMEM] * 4,
        out_specs=[VMEM] * (2 * n_gr - half),
        compiler_params=GRANT,
        cost_estimate=cost(*late),
        name="last_sums",
    )(rows, total, dens, *late)

    sent = [part.astype(jnp.float16) for part in sums[:n_gr]]
    back = [sent[0]] + [along_gr(sent[k], k) for k in range(1, n_gr)]
    back = [part.astype(jnp.float32) for part in back]
    back += [along_gr(sums[half + k], k) for k in range(half, n_gr)]
    neighbour_sum, density = pl.pallas_call(
        functools.partial(restore_kernel, half),
        out_shape=[
            jax.ShapeDtypeStruct((count, width), jnp.float32),
            jax.ShapeDtypeStruct((1, count), jnp.float32),
        ],
        in_specs=[VMEM] * (1 + len(back)),
        out_specs=[VMEM, VMEM],
        compiler_params=GRANT,
        name="restore_rows",
    )(chosen, *back[n_gr - 1 :: -1], *back[:n_gr - 1 : -1])
    return (neighbour_sum, density.reshape(count))


def solution(mesh):
    in_specs = (P(("gr", "gc"), None), P(("gr", "gc")))
    out_specs = (P(("gr", "gc"), None), P(("gr", "gc")))
    return jax.shard_map(
        functools.partial(on_device, mesh.shape["gr"], mesh.shape["gc"]),
        mesh=mesh,
        in_specs=in_specs,
        out_specs=out_specs,
        check_vma=False,
    )
```

```python
import functools
import math

import jax
import jax.numpy as jnp
from jax import lax
from jax.experimental import pallas as pl
from jax.experimental.pallas import tpu as pltpu
from jax.sharding import PartitionSpec as P

beta_scale = 16.0
LANES = 128
EXTRA = 8
TOP = 14.0
VMEM = pl.BlockSpec(memory_space=pltpu.VMEM)
HBM = pl.BlockSpec(memory_space=pltpu.HBM)
SMEM = pl.BlockSpec(memory_space=pltpu.SMEM)
GRANT = pltpu.CompilerParams(vmem_limit_bytes=40 * 1024 * 1024)


def in_hbm(array):
    return pltpu.with_memory_space_constraint(array, pltpu.HBM)


def diagonal(count):
    first = lax.broadcasted_iota(jnp.int32, (count, count), 0)
    second = lax.broadcasted_iota(jnp.int32, (count, count), 1)
    return first == second


def as_row(column):
    return jnp.sum(
        jnp.where(diagonal(column.shape[0]), column, jnp.zeros_like(column)),
        axis=0,
        keepdims=True,
    )


def as_column(row):
    return jnp.sum(
        jnp.where(diagonal(row.shape[1]), row, jnp.zeros_like(row)),
        axis=1,
        keepdims=True,
    )


def placement(own, ids, groups):
    count = ids.shape[1]
    first = lax.broadcasted_iota(jnp.int32, (count, count), 0)
    second = lax.broadcasted_iota(jnp.int32, (count, count), 1)
    earlier = jnp.where((as_column(ids) == ids) & (first < second), 1, 0)
    rank = jnp.sum(earlier, axis=0, keepdims=True)
    slot = (ids ^ own) * (count // groups) + rank
    return jnp.where(first == slot, 1.0, 0.0)


def sort_kernel(own_ref, ids_hbm, rows_hbm, *refs):
    chosen_ref, *out_refs = refs[:-4]
    ids_ref, rows_ref, ids_sem, rows_sem = refs[-4:]
    groups = len(out_refs)
    ids_copy = pltpu.make_async_copy(ids_hbm, ids_ref, ids_sem)
    rows_copy = pltpu.make_async_copy(rows_hbm, rows_ref, rows_sem)
    ids_copy.start()
    rows_copy.start()
    ids_copy.wait()
    chosen = placement(own_ref[0], ids_ref[...], groups).astype(jnp.bfloat16)
    chosen_ref[...] = chosen
    rows_copy.wait()
    ordered = jnp.dot(chosen, rows_ref[...], preferred_element_type=jnp.float32)
    ordered = ordered.astype(jnp.bfloat16)
    size = ordered.shape[0] // groups
    for k, out_ref in enumerate(out_refs):
        out_ref[...] = ordered[k * size : (k + 1) * size, :]


def inverse_norms(rows):
    wide = rows.astype(jnp.float32)
    return lax.rsqrt(jnp.sum(wide * wide, axis=1, keepdims=True) + 1e-06)


def add_columns(rows, col_refs, total, dens):
    count = rows.shape[0]
    scale = inverse_norms(rows) * (beta_scale * math.log2(math.e))
    blocks = [
        (col_ref, start)
        for col_ref in col_refs
        for start in range(0, col_ref.shape[0], count)
    ]
    for col_ref, start in blocks:
        cols = col_ref[start : min(start + count, col_ref.shape[0]), :]
        size = cols.shape[0]
        col_inv = as_row(inverse_norms(cols))
        raw = lax.dot_general(
            rows, cols, (((1,), (1,)), ((), ())), preferred_element_type=jnp.float32
        )
        weight = jnp.exp2(raw * scale * col_inv - beta_scale * math.log2(math.e))
        whole = size - size % LANES
        for lane in range(0, whole, LANES):
            dens += weight[:, lane : lane + LANES]
        if whole < size:
            part = jnp.sum(weight[:, whole:], axis=1, keepdims=True)
            dens += jnp.where(lax.broadcasted_iota(jnp.int32, dens.shape, 1) == 0, part, 0.0)
        coef = (weight * col_inv).astype(jnp.bfloat16)
        total += jnp.dot(coef, cols, preferred_element_type=jnp.float32)
    return total, dens


def first_kernel(rows_ref, *refs):
    col_refs, (total_ref, dens_ref) = refs[:-2], refs[-2:]
    total = jnp.zeros(total_ref.shape, jnp.float32)
    dens = jnp.zeros(dens_ref.shape, jnp.float32)
    total, dens = add_columns(rows_ref[...], col_refs, total, dens)
    total_ref[...] = total
    dens_ref[...] = dens


def middle_kernel(rows_ref, total_ref, dens_ref, *refs):
    col_refs, (total_out, dens_out) = refs[:-2], refs[-2:]
    total, dens = add_columns(rows_ref[...], col_refs, total_ref[...], dens_ref[...])
    total_out[...] = total
    dens_out[...] = dens


def exponent(value):
    return jnp.floor(jnp.log2(jnp.maximum(value, 1e-30)))


def last_kernel(half, rows_ref, total_ref, dens_ref, cols_ref, *out_refs):
    groups = len(out_refs) - half
    size = out_refs[half].shape[0]
    total, dens = add_columns(
        rows_ref[...], [cols_ref], total_ref[...], dens_ref[...]
    )
    dens = jnp.sum(dens, axis=1, keepdims=True)
    power = exponent(jnp.max(jnp.abs(total), axis=1, keepdims=True))
    total = total * jnp.exp2(TOP - power)
    dens_power = exponent(dens)
    part = dens * jnp.exp2(-dens_power)
    aside = [power, dens_power]
    for k in range(3):
        piece = part.astype(jnp.bfloat16).astype(jnp.float32)
        aside.append(piece * 2.0 ** (8 * k))
        part = part - piece
    for k in range(groups):
        rows = slice(k * size, (k + 1) * size)
        out_refs[k][:size, :] = total[rows, :]
        if k < half:
            aside_ref, top = out_refs[k], size
            aside_ref[size:, :] = jnp.zeros((EXTRA, total.shape[1]), jnp.float32)
        else:
            aside_ref, top = out_refs[half + k], 0
            aside_ref[...] = jnp.zeros(aside_ref.shape, jnp.float32)
        for line, column in enumerate(aside):
            aside_ref[top + line : top + line + 1, :size] = as_row(column[rows, :])


def restore_kernel(half, chosen_ref, *refs):
    refs, (total_ref, dens_ref) = refs[:-2], refs[-2:]
    groups = len(refs) - half
    part_refs = refs[groups - 1 :: -1] + refs[: groups - 1 : -1]
    size = part_refs[half].shape[0]
    chosen = chosen_ref[...]
    sums, dens = [], []
    for k in range(groups):
        aside_ref, top = (part_refs[k], size) if k < half else (part_refs[half + k], 0)
        power, dens_power, *pieces = [
            as_column(aside_ref[top + line : top + line + 1, :size])
            for line in range(5)
        ]
        sums.append(part_refs[k][:size, :] * jnp.exp2(power - TOP))
        part = sum(piece * 2.0 ** (-8 * j) for j, piece in enumerate(pieces))
        dens.append(part * jnp.exp2(dens_power))
    dens_ref[...] = jnp.sum(
        chosen.astype(jnp.float32) * jnp.concatenate(dens, axis=0), axis=0, keepdims=True
    )
    rest = jnp.concatenate(sums, axis=0)
    back = jnp.zeros(rest.shape, jnp.float32)
    for _ in range(2):
        piece = rest.astype(jnp.bfloat16)
        rest = rest - piece.astype(jnp.float32)
        back += lax.dot_general(
            chosen, piece, (((0,), (0,)), ((), ())), preferred_element_type=jnp.float32
        )
    total_ref[...] = back


def on_device(n_gr, n_gc, embeddings, cluster_ids):
    count, width = embeddings.shape
    size = count // n_gr
    own = lax.axis_index("gr").astype(jnp.int32).reshape(1)
    ids = cluster_ids.reshape(1, count)

    chosen, *parts = pl.pallas_call(
        sort_kernel,
        out_shape=[jax.ShapeDtypeStruct((count, count), jnp.bfloat16)]
        + [jax.ShapeDtypeStruct((size, width), jnp.bfloat16)] * n_gr,
        in_specs=[SMEM, HBM, HBM],
        out_specs=[VMEM] * (1 + n_gr),
        scratch_shapes=[
            pltpu.VMEM((1, count), jnp.int32),
            pltpu.VMEM((count, width), embeddings.dtype),
            pltpu.SemaphoreType.DMA,
            pltpu.SemaphoreType.DMA,
        ],
        compiler_params=GRANT,
        name="sort_rows",
    )(own, in_hbm(ids), in_hbm(embeddings))

    def along_gr(part, bits):
        return lax.ppermute(part, "gr", [(i, i ^ bits) for i in range(n_gr)])

    def along_gc(block, bits):
        return lax.ppermute(block, "gc", [(i, i ^ bits) for i in range(n_gc)])

    def other_core(block):
        return along_gc(block, 1)

    def cost(*blocks):
        pairs = count * sum(block.shape[0] for block in blocks)
        return pl.CostEstimate(
            flops=4 * pairs * width,
            bytes_accessed=0,
            transcendentals=pairs,
        )

    held = [parts[0]] + [along_gr(parts[k], k) for k in range(1, n_gr)]
    half = n_gr // 2
    sides = [k for k in range(2, n_gc, 2) if not k & (k - 1)]
    pair = jnp.concatenate(held[1:half], axis=0)
    block = jnp.concatenate(held[:half], axis=0)
    late = jnp.concatenate(held[half:], axis=0)
    own_near = [along_gc(held[0], k) for k in sides]
    own_near, pair = lax.optimization_barrier((own_near, pair))
    pair_near = [along_gc(pair, k) for k in sides]
    both_near = [along_gc(block, k) for k in range(2, n_gc, 2) if k not in sides]
    rows = jnp.concatenate(held, axis=0)
    late_near = [along_gc(late, k) for k in range(2, n_gc, 2)]
    chunks = [jnp.concatenate(both_near + pair_near + own_near + [block], axis=0), jnp.concatenate([late] + late_near, axis=0)]
    chunks[0], rows = lax.optimization_barrier((chunks[0], rows))
    early = [chunks[0], other_core(chunks[0])]

    total, dens = pl.pallas_call(
        first_kernel,
        out_shape=[
            jax.ShapeDtypeStruct((count, width), jnp.float32),
            jax.ShapeDtypeStruct((count, LANES), jnp.float32),
        ],
        in_specs=[VMEM] * (1 + len(early)),
        out_specs=[VMEM] * 2,
        compiler_params=GRANT,
        cost_estimate=cost(*early),
        name="early_sums",
    )(rows, *early)
    total, dens = pl.pallas_call(
        middle_kernel,
        out_shape=[
            jax.ShapeDtypeStruct((count, width), jnp.float32),
            jax.ShapeDtypeStruct((count, LANES), jnp.float32),
        ],
        in_specs=[VMEM] * 4,
        out_specs=[VMEM] * 2,
        compiler_params=GRANT,
        cost_estimate=cost(chunks[1]),
        name="middle_sums",
    )(rows, total, dens, chunks[1])
    late = [other_core(chunks[1])]
    sums = pl.pallas_call(
        functools.partial(last_kernel, half),
        out_shape=[jax.ShapeDtypeStruct((size + EXTRA, width), jnp.float32)] * half
        + [jax.ShapeDtypeStruct((size, width), jnp.float32)] * (n_gr - half)
        + [jax.ShapeDtypeStruct((EXTRA, LANES), jnp.float32)] * (n_gr - half),
        in_specs=[VMEM] * 4,
        out_specs=[VMEM] * (2 * n_gr - half),
        compiler_params=GRANT,
        cost_estimate=cost(*late),
        name="last_sums",
    )(rows, total, dens, *late)

    sent = [part.astype(jnp.float16) for part in sums[:n_gr]]
    back = [sent[0]] + [along_gr(sent[k], k) for k in range(1, n_gr)]
    back = [part.astype(jnp.float32) for part in back]
    back += [along_gr(sums[half + k], k) for k in range(half, n_gr)]
    neighbour_sum, density = pl.pallas_call(
        functools.partial(restore_kernel, half),
        out_shape=[
            jax.ShapeDtypeStruct((count, width), jnp.float32),
            jax.ShapeDtypeStruct((1, count), jnp.float32),
        ],
        in_specs=[VMEM] * (1 + len(back)),
        out_specs=[VMEM, VMEM],
        compiler_params=GRANT,
        name="restore_rows",
    )(chosen, *back[n_gr - 1 :: -1], *back[:n_gr - 1 : -1])
    return (neighbour_sum, density.reshape(count))


def solution(mesh):
    in_specs = (P(("gr", "gc"), None), P(("gr", "gc")))
    out_specs = (P(("gr", "gc"), None), P(("gr", "gc")))
    return jax.shard_map(
        functools.partial(on_device, mesh.shape["gr"], mesh.shape["gc"]),
        mesh=mesh,
        in_specs=in_specs,
        out_specs=out_specs,
        check_vma=False,
    )
```

```python
import functools
import math

import jax
import jax.numpy as jnp
from jax import lax
from jax.experimental import pallas as pl
from jax.experimental.pallas import tpu as pltpu
from jax.sharding import PartitionSpec as P

beta_scale = 16.0
LANES = 128
EXTRA = 8
TOP = 14.0
VMEM = pl.BlockSpec(memory_space=pltpu.VMEM)
HBM = pl.BlockSpec(memory_space=pltpu.HBM)
SMEM = pl.BlockSpec(memory_space=pltpu.SMEM)
GRANT = pltpu.CompilerParams(vmem_limit_bytes=40 * 1024 * 1024)


def in_hbm(array):
    return pltpu.with_memory_space_constraint(array, pltpu.HBM)


def diagonal(count):
    first = lax.broadcasted_iota(jnp.int32, (count, count), 0)
    second = lax.broadcasted_iota(jnp.int32, (count, count), 1)
    return first == second


def as_row(column):
    return jnp.sum(
        jnp.where(diagonal(column.shape[0]), column, jnp.zeros_like(column)),
        axis=0,
        keepdims=True,
    )


def as_column(row):
    return jnp.sum(
        jnp.where(diagonal(row.shape[1]), row, jnp.zeros_like(row)),
        axis=1,
        keepdims=True,
    )


def placement(own, ids, groups):
    count = ids.shape[1]
    first = lax.broadcasted_iota(jnp.int32, (count, count), 0)
    second = lax.broadcasted_iota(jnp.int32, (count, count), 1)
    earlier = jnp.where((as_column(ids) == ids) & (first < second), 1, 0)
    rank = jnp.sum(earlier, axis=0, keepdims=True)
    slot = (ids ^ own) * (count // groups) + rank
    return jnp.where(first == slot, 1.0, 0.0)


def sort_kernel(own_ref, ids_hbm, rows_hbm, *refs):
    chosen_ref, *out_refs = refs[:-4]
    ids_ref, rows_ref, ids_sem, rows_sem = refs[-4:]
    groups = len(out_refs)
    ids_copy = pltpu.make_async_copy(ids_hbm, ids_ref, ids_sem)
    rows_copy = pltpu.make_async_copy(rows_hbm, rows_ref, rows_sem)
    ids_copy.start()
    rows_copy.start()
    ids_copy.wait()
    chosen = placement(own_ref[0], ids_ref[...], groups).astype(jnp.bfloat16)
    chosen_ref[...] = chosen
    rows_copy.wait()
    ordered = jnp.dot(chosen, rows_ref[...], preferred_element_type=jnp.float32)
    ordered = ordered.astype(jnp.bfloat16)
    size = ordered.shape[0] // groups
    for k, out_ref in enumerate(out_refs):
        out_ref[...] = ordered[k * size : (k + 1) * size, :]


def inverse_norms(rows):
    wide = rows.astype(jnp.float32)
    return lax.rsqrt(jnp.sum(wide * wide, axis=1, keepdims=True) + 1e-06)


def add_columns(rows, col_refs, total, dens):
    count = rows.shape[0]
    scale = inverse_norms(rows) * (beta_scale * math.log2(math.e))
    blocks = [
        (col_ref, start)
        for col_ref in col_refs
        for start in range(0, col_ref.shape[0], count)
    ]
    for col_ref, start in blocks:
        cols = col_ref[start : min(start + count, col_ref.shape[0]), :]
        size = cols.shape[0]
        col_inv = as_row(inverse_norms(cols))
        raw = lax.dot_general(
            rows, cols, (((1,), (1,)), ((), ())), preferred_element_type=jnp.float32
        )
        weight = jnp.exp2(raw * scale * col_inv - beta_scale * math.log2(math.e))
        whole = size - size % LANES
        for lane in range(0, whole, LANES):
            dens += weight[:, lane : lane + LANES]
        if whole < size:
            part = jnp.sum(weight[:, whole:], axis=1, keepdims=True)
            dens += jnp.where(lax.broadcasted_iota(jnp.int32, dens.shape, 1) == 0, part, 0.0)
        coef = (weight * col_inv).astype(jnp.bfloat16)
        total += jnp.dot(coef, cols, preferred_element_type=jnp.float32)
    return total, dens


def first_kernel(rows_ref, *refs):
    col_refs, (total_ref, dens_ref) = refs[:-2], refs[-2:]
    total = jnp.zeros(total_ref.shape, jnp.float32)
    dens = jnp.zeros(dens_ref.shape, jnp.float32)
    total, dens = add_columns(rows_ref[...], col_refs, total, dens)
    total_ref[...] = total
    dens_ref[...] = dens


def middle_kernel(rows_ref, total_ref, dens_ref, *refs):
    col_refs, (total_out, dens_out) = refs[:-2], refs[-2:]
    total, dens = add_columns(rows_ref[...], col_refs, total_ref[...], dens_ref[...])
    total_out[...] = total
    dens_out[...] = dens


def exponent(value):
    return jnp.floor(jnp.log2(jnp.maximum(value, 1e-30)))


def last_kernel(half, rows_ref, total_ref, dens_ref, cols_ref, *out_refs):
    groups = len(out_refs) - half
    size = out_refs[half].shape[0]
    total, dens = add_columns(
        rows_ref[...], [cols_ref], total_ref[...], dens_ref[...]
    )
    dens = jnp.sum(dens, axis=1, keepdims=True)
    power = exponent(jnp.max(jnp.abs(total), axis=1, keepdims=True))
    total = total * jnp.exp2(TOP - power)
    dens_power = exponent(dens)
    part = dens * jnp.exp2(-dens_power)
    aside = [power, dens_power]
    for k in range(3):
        piece = part.astype(jnp.bfloat16).astype(jnp.float32)
        aside.append(piece * 2.0 ** (8 * k))
        part = part - piece
    for k in range(groups):
        rows = slice(k * size, (k + 1) * size)
        out_refs[k][:size, :] = total[rows, :]
        if k < half:
            aside_ref, top = out_refs[k], size
            aside_ref[size:, :] = jnp.zeros((EXTRA, total.shape[1]), jnp.float32)
        else:
            aside_ref, top = out_refs[half + k], 0
            aside_ref[...] = jnp.zeros(aside_ref.shape, jnp.float32)
        for line, column in enumerate(aside):
            aside_ref[top + line : top + line + 1, :size] = as_row(column[rows, :])


def restore_kernel(half, chosen_ref, *refs):
    refs, (total_ref, dens_ref) = refs[:-2], refs[-2:]
    groups = len(refs) - half
    part_refs = refs[groups - 1 :: -1] + refs[: groups - 1 : -1]
    size = part_refs[half].shape[0]
    chosen = chosen_ref[...]
    sums, dens = [], []
    for k in range(groups):
        aside_ref, top = (part_refs[k], size) if k < half else (part_refs[half + k], 0)
        power, dens_power, *pieces = [
            as_column(aside_ref[top + line : top + line + 1, :size])
            for line in range(5)
        ]
        sums.append(part_refs[k][:size, :] * jnp.exp2(power - TOP))
        part = sum(piece * 2.0 ** (-8 * j) for j, piece in enumerate(pieces))
        dens.append(part * jnp.exp2(dens_power))
    dens_ref[...] = jnp.sum(
        chosen.astype(jnp.float32) * jnp.concatenate(dens, axis=0), axis=0, keepdims=True
    )
    rest = jnp.concatenate(sums, axis=0)
    back = jnp.zeros(rest.shape, jnp.float32)
    for _ in range(2):
        piece = rest.astype(jnp.bfloat16)
        rest = rest - piece.astype(jnp.float32)
        back += lax.dot_general(
            chosen, piece, (((0,), (0,)), ((), ())), preferred_element_type=jnp.float32
        )
    total_ref[...] = back


def on_device(n_gr, n_gc, embeddings, cluster_ids):
    count, width = embeddings.shape
    size = count // n_gr
    own = lax.axis_index("gr").astype(jnp.int32).reshape(1)
    ids = cluster_ids.reshape(1, count)

    chosen, *parts = pl.pallas_call(
        sort_kernel,
        out_shape=[jax.ShapeDtypeStruct((count, count), jnp.bfloat16)]
        + [jax.ShapeDtypeStruct((size, width), jnp.bfloat16)] * n_gr,
        in_specs=[SMEM, HBM, HBM],
        out_specs=[VMEM] * (1 + n_gr),
        scratch_shapes=[
            pltpu.VMEM((1, count), jnp.int32),
            pltpu.VMEM((count, width), embeddings.dtype),
            pltpu.SemaphoreType.DMA,
            pltpu.SemaphoreType.DMA,
        ],
        compiler_params=GRANT,
        name="sort_rows",
    )(own, in_hbm(ids), in_hbm(embeddings))

    def along_gr(part, bits):
        return lax.ppermute(part, "gr", [(i, i ^ bits) for i in range(n_gr)])

    def along_gc(block, bits):
        return lax.ppermute(block, "gc", [(i, i ^ bits) for i in range(n_gc)])

    def other_core(block):
        return along_gc(block, 1)

    def cost(*blocks):
        pairs = count * sum(block.shape[0] for block in blocks)
        return pl.CostEstimate(
            flops=4 * pairs * width,
            bytes_accessed=0,
            transcendentals=pairs,
        )

    held = [parts[0]] + [along_gr(parts[k], k) for k in range(1, n_gr)]
    half = n_gr // 2
    sides = [k for k in range(2, n_gc, 2) if not k & (k - 1)]
    corners = [k for k in range(2, n_gc, 2) if k & (k - 1)]

    def to_side(block, step):
        pairs = [(i, i ^ sides[(step + i % 2) % len(sides)]) for i in range(n_gc)]
        return lax.ppermute(block, "gc", pairs)

    chunks = []
    for pieces in (held[:half], held[half:]):
        block = jnp.concatenate(pieces, axis=0)
        near = [block] + [to_side(block, step) for step in range(len(sides))]
        near += [along_gc(block, k) for k in corners]
        chunks.append(jnp.concatenate(near, axis=0))
    rows = jnp.concatenate(held, axis=0)
    chunks[0], rows = lax.optimization_barrier((chunks[0], rows))
    early = [chunks[0], other_core(chunks[0])]

    total, dens = pl.pallas_call(
        first_kernel,
        out_shape=[
            jax.ShapeDtypeStruct((count, width), jnp.float32),
            jax.ShapeDtypeStruct((count, LANES), jnp.float32),
        ],
        in_specs=[VMEM] * (1 + len(early)),
        out_specs=[VMEM] * 2,
        compiler_params=GRANT,
        cost_estimate=cost(*early),
        name="early_sums",
    )(rows, *early)
    total, dens = pl.pallas_call(
        middle_kernel,
        out_shape=[
            jax.ShapeDtypeStruct((count, width), jnp.float32),
            jax.ShapeDtypeStruct((count, LANES), jnp.float32),
        ],
        in_specs=[VMEM] * 4,
        out_specs=[VMEM] * 2,
        compiler_params=GRANT,
        cost_estimate=cost(chunks[1]),
        name="middle_sums",
    )(rows, total, dens, chunks[1])
    late = [other_core(chunks[1])]
    sums = pl.pallas_call(
        functools.partial(last_kernel, half),
        out_shape=[jax.ShapeDtypeStruct((size + EXTRA, width), jnp.float32)] * half
        + [jax.ShapeDtypeStruct((size, width), jnp.float32)] * (n_gr - half)
        + [jax.ShapeDtypeStruct((EXTRA, LANES), jnp.float32)] * (n_gr - half),
        in_specs=[VMEM] * 4,
        out_specs=[VMEM] * (2 * n_gr - half),
        compiler_params=GRANT,
        cost_estimate=cost(*late),
        name="last_sums",
    )(rows, total, dens, *late)

    sent = [part.astype(jnp.float16) for part in sums[:n_gr]]
    back = [sent[0]] + [along_gr(sent[k], k) for k in range(1, n_gr)]
    back = [part.astype(jnp.float32) for part in back]
    back += [along_gr(sums[half + k], k) for k in range(half, n_gr)]
    neighbour_sum, density = pl.pallas_call(
        functools.partial(restore_kernel, half),
        out_shape=[
            jax.ShapeDtypeStruct((count, width), jnp.float32),
            jax.ShapeDtypeStruct((1, count), jnp.float32),
        ],
        in_specs=[VMEM] * (1 + len(back)),
        out_specs=[VMEM, VMEM],
        compiler_params=GRANT,
        name="restore_rows",
    )(chosen, *back[n_gr - 1 :: -1], *back[:n_gr - 1 : -1])
    return (neighbour_sum, density.reshape(count))


def solution(mesh):
    in_specs = (P(("gr", "gc"), None), P(("gr", "gc")))
    out_specs = (P(("gr", "gc"), None), P(("gr", "gc")))
    return jax.shard_map(
        functools.partial(on_device, mesh.shape["gr"], mesh.shape["gc"]),
        mesh=mesh,
        in_specs=in_specs,
        out_specs=out_specs,
        check_vma=False,
    )
```

```python
import functools
import math

import jax
import jax.numpy as jnp
from jax import lax
from jax.experimental import pallas as pl
from jax.experimental.pallas import tpu as pltpu
from jax.sharding import PartitionSpec as P

beta_scale = 16.0
LANES = 128
EXTRA = 8
TOP = 14.0
VMEM = pl.BlockSpec(memory_space=pltpu.VMEM)
HBM = pl.BlockSpec(memory_space=pltpu.HBM)
SMEM = pl.BlockSpec(memory_space=pltpu.SMEM)
GRANT = pltpu.CompilerParams(vmem_limit_bytes=40 * 1024 * 1024)


def in_hbm(array):
    return pltpu.with_memory_space_constraint(array, pltpu.HBM)


def diagonal(count):
    first = lax.broadcasted_iota(jnp.int32, (count, count), 0)
    second = lax.broadcasted_iota(jnp.int32, (count, count), 1)
    return first == second


def as_row(column):
    return jnp.sum(
        jnp.where(diagonal(column.shape[0]), column, jnp.zeros_like(column)),
        axis=0,
        keepdims=True,
    )


def as_column(row):
    return jnp.sum(
        jnp.where(diagonal(row.shape[1]), row, jnp.zeros_like(row)),
        axis=1,
        keepdims=True,
    )


def placement(own, ids, groups):
    count = ids.shape[1]
    first = lax.broadcasted_iota(jnp.int32, (count, count), 0)
    second = lax.broadcasted_iota(jnp.int32, (count, count), 1)
    earlier = jnp.where((as_column(ids) == ids) & (first < second), 1, 0)
    rank = jnp.sum(earlier, axis=0, keepdims=True)
    slot = (ids ^ own) * (count // groups) + rank
    return jnp.where(first == slot, 1.0, 0.0)


def sort_kernel(own_ref, ids_hbm, rows_hbm, *refs):
    chosen_ref, *out_refs = refs[:-4]
    ids_ref, rows_ref, ids_sem, rows_sem = refs[-4:]
    groups = len(out_refs)
    ids_copy = pltpu.make_async_copy(ids_hbm, ids_ref, ids_sem)
    rows_copy = pltpu.make_async_copy(rows_hbm, rows_ref, rows_sem)
    ids_copy.start()
    rows_copy.start()
    ids_copy.wait()
    chosen = placement(own_ref[0], ids_ref[...], groups).astype(jnp.bfloat16)
    chosen_ref[...] = chosen
    rows_copy.wait()
    ordered = jnp.dot(chosen, rows_ref[...], preferred_element_type=jnp.float32)
    ordered = ordered.astype(jnp.bfloat16)
    size = ordered.shape[0] // groups
    for k, out_ref in enumerate(out_refs):
        out_ref[...] = ordered[k * size : (k + 1) * size, :]


def inverse_norms(rows):
    wide = rows.astype(jnp.float32)
    return lax.rsqrt(jnp.sum(wide * wide, axis=1, keepdims=True) + 1e-06)


def add_columns(rows, col_refs, total, dens):
    count = rows.shape[0]
    scale = inverse_norms(rows) * (beta_scale * math.log2(math.e))
    blocks = [
        (col_ref, start)
        for col_ref in col_refs
        for start in range(0, col_ref.shape[0], count)
    ]
    for col_ref, start in blocks:
        cols = col_ref[start : min(start + count, col_ref.shape[0]), :]
        size = cols.shape[0]
        col_inv = as_row(inverse_norms(cols))
        raw = lax.dot_general(
            rows, cols, (((1,), (1,)), ((), ())), preferred_element_type=jnp.float32
        )
        weight = jnp.exp2(raw * scale * col_inv - beta_scale * math.log2(math.e))
        whole = size - size % LANES
        for lane in range(0, whole, LANES):
            dens += weight[:, lane : lane + LANES]
        if whole < size:
            part = jnp.sum(weight[:, whole:], axis=1, keepdims=True)
            dens += jnp.where(lax.broadcasted_iota(jnp.int32, dens.shape, 1) == 0, part, 0.0)
        coef = (weight * col_inv).astype(jnp.bfloat16)
        total += jnp.dot(coef, cols, preferred_element_type=jnp.float32)
    return total, dens


def first_kernel(rows_ref, *refs):
    col_refs, (total_ref, dens_ref) = refs[:-2], refs[-2:]
    total = jnp.zeros(total_ref.shape, jnp.float32)
    dens = jnp.zeros(dens_ref.shape, jnp.float32)
    total, dens = add_columns(rows_ref[...], col_refs, total, dens)
    total_ref[...] = total
    dens_ref[...] = dens


def middle_kernel(rows_ref, total_ref, dens_ref, *refs):
    col_refs, (total_out, dens_out) = refs[:-2], refs[-2:]
    total, dens = add_columns(rows_ref[...], col_refs, total_ref[...], dens_ref[...])
    total_out[...] = total
    dens_out[...] = dens


def exponent(value):
    return jnp.floor(jnp.log2(jnp.maximum(value, 1e-30)))


def last_kernel(half, rows_ref, total_ref, dens_ref, cols_ref, *out_refs):
    groups = len(out_refs) - half
    size = out_refs[half].shape[0]
    total, dens = add_columns(
        rows_ref[...], [cols_ref], total_ref[...], dens_ref[...]
    )
    dens = jnp.sum(dens, axis=1, keepdims=True)
    power = exponent(jnp.max(jnp.abs(total), axis=1, keepdims=True))
    total = total * jnp.exp2(TOP - power)
    dens_power = exponent(dens)
    part = dens * jnp.exp2(-dens_power)
    aside = [power, dens_power]
    for k in range(3):
        piece = part.astype(jnp.bfloat16).astype(jnp.float32)
        aside.append(piece * 2.0 ** (8 * k))
        part = part - piece
    for k in range(groups):
        rows = slice(k * size, (k + 1) * size)
        out_refs[k][:size, :] = total[rows, :]
        if k < half:
            aside_ref, top = out_refs[k], size
            aside_ref[size:, :] = jnp.zeros((EXTRA, total.shape[1]), jnp.float32)
        else:
            aside_ref, top = out_refs[half + k], 0
            aside_ref[...] = jnp.zeros(aside_ref.shape, jnp.float32)
        for line, column in enumerate(aside):
            aside_ref[top + line : top + line + 1, :size] = as_row(column[rows, :])


def restore_kernel(half, chosen_ref, *refs):
    refs, (total_ref, dens_ref) = refs[:-2], refs[-2:]
    groups = len(refs) - half
    part_refs = refs[groups - 1 :: -1] + refs[: groups - 1 : -1]
    size = part_refs[half].shape[0]
    chosen = chosen_ref[...]
    sums, dens = [], []
    for k in range(groups):
        aside_ref, top = (part_refs[k], size) if k < half else (part_refs[half + k], 0)
        power, dens_power, *pieces = [
            as_column(aside_ref[top + line : top + line + 1, :size])
            for line in range(5)
        ]
        sums.append(part_refs[k][:size, :] * jnp.exp2(power - TOP))
        part = sum(piece * 2.0 ** (-8 * j) for j, piece in enumerate(pieces))
        dens.append(part * jnp.exp2(dens_power))
    dens_ref[...] = jnp.sum(
        chosen.astype(jnp.float32) * jnp.concatenate(dens, axis=0), axis=0, keepdims=True
    )
    rest = jnp.concatenate(sums, axis=0)
    back = jnp.zeros(rest.shape, jnp.float32)
    for _ in range(2):
        piece = rest.astype(jnp.bfloat16)
        rest = rest - piece.astype(jnp.float32)
        back += lax.dot_general(
            chosen, piece, (((0,), (0,)), ((), ())), preferred_element_type=jnp.float32
        )
    total_ref[...] = back


def on_device(n_gr, n_gc, embeddings, cluster_ids):
    count, width = embeddings.shape
    size = count // n_gr
    own = lax.axis_index("gr").astype(jnp.int32).reshape(1)
    ids = cluster_ids.reshape(1, count)

    chosen, *parts = pl.pallas_call(
        sort_kernel,
        out_shape=[jax.ShapeDtypeStruct((count, count), jnp.bfloat16)]
        + [jax.ShapeDtypeStruct((size, width), jnp.bfloat16)] * n_gr,
        in_specs=[SMEM, HBM, HBM],
        out_specs=[VMEM] * (1 + n_gr),
        scratch_shapes=[
            pltpu.VMEM((1, count), jnp.int32),
            pltpu.VMEM((count, width), embeddings.dtype),
            pltpu.SemaphoreType.DMA,
            pltpu.SemaphoreType.DMA,
        ],
        compiler_params=GRANT,
        name="sort_rows",
    )(own, in_hbm(ids), in_hbm(embeddings))

    def along_gr(part, bits):
        return lax.ppermute(part, "gr", [(i, i ^ bits) for i in range(n_gr)])

    def along_gc(block, bits):
        return lax.ppermute(block, "gc", [(i, i ^ bits) for i in range(n_gc)])

    def other_core(block):
        return along_gc(block, 1)

    def cost(*blocks):
        pairs = count * sum(block.shape[0] for block in blocks)
        return pl.CostEstimate(
            flops=4 * pairs * width,
            bytes_accessed=0,
            transcendentals=pairs,
        )

    held = [parts[0]] + [along_gr(parts[k], k) for k in range(1, n_gr)]
    half = n_gr // 2
    sides = [k for k in range(2, n_gc, 2) if not k & (k - 1)]
    corners = [k for k in range(2, n_gc, 2) if k & (k - 1)]

    def to_side(block, step):
        pairs = [(i, i ^ sides[(step + i % 2) % len(sides)]) for i in range(n_gc)]
        return lax.ppermute(block, "gc", pairs)

    early = jnp.concatenate(held[:half], axis=0)
    late = jnp.concatenate(held[half:], axis=0)
    rest = jnp.concatenate(held[1:half], axis=0)
    filler = [along_gc(held[0], k) for k in corners]
    filler, rest = lax.optimization_barrier((filler, rest))
    rest_corners = [along_gc(rest, k) for k in corners]
    early_sides = [to_side(early, step) for step in range(len(sides))]
    late_near = [to_side(late, 0)] + [along_gc(late, k) for k in corners]
    rest_corners, late = lax.optimization_barrier((rest_corners, late))
    late_near += [to_side(late, step) for step in range(1, len(sides))]
    rows = jnp.concatenate(held, axis=0)
    chunks = [jnp.concatenate(early_sides + rest_corners + filler + [early], axis=0), jnp.concatenate([late] + late_near, axis=0)]
    early = [chunks[0], other_core(chunks[0])]

    total, dens = pl.pallas_call(
        first_kernel,
        out_shape=[
            jax.ShapeDtypeStruct((count, width), jnp.float32),
            jax.ShapeDtypeStruct((count, LANES), jnp.float32),
        ],
        in_specs=[VMEM] * (1 + len(early)),
        out_specs=[VMEM] * 2,
        compiler_params=GRANT,
        cost_estimate=cost(*early),
        name="early_sums",
    )(rows, *early)
    total, dens = pl.pallas_call(
        middle_kernel,
        out_shape=[
            jax.ShapeDtypeStruct((count, width), jnp.float32),
            jax.ShapeDtypeStruct((count, LANES), jnp.float32),
        ],
        in_specs=[VMEM] * 4,
        out_specs=[VMEM] * 2,
        compiler_params=GRANT,
        cost_estimate=cost(chunks[1]),
        name="middle_sums",
    )(rows, total, dens, chunks[1])
    late = [other_core(chunks[1])]
    sums = pl.pallas_call(
        functools.partial(last_kernel, half),
        out_shape=[jax.ShapeDtypeStruct((size + EXTRA, width), jnp.float32)] * half
        + [jax.ShapeDtypeStruct((size, width), jnp.float32)] * (n_gr - half)
        + [jax.ShapeDtypeStruct((EXTRA, LANES), jnp.float32)] * (n_gr - half),
        in_specs=[VMEM] * 4,
        out_specs=[VMEM] * (2 * n_gr - half),
        compiler_params=GRANT,
        cost_estimate=cost(*late),
        name="last_sums",
    )(rows, total, dens, *late)

    sent = [part.astype(jnp.float16) for part in sums[:n_gr]]
    back = [sent[0]] + [along_gr(sent[k], k) for k in range(1, n_gr)]
    back = [part.astype(jnp.float32) for part in back]
    back += [along_gr(sums[half + k], k) for k in range(half, n_gr)]
    neighbour_sum, density = pl.pallas_call(
        functools.partial(restore_kernel, half),
        out_shape=[
            jax.ShapeDtypeStruct((count, width), jnp.float32),
            jax.ShapeDtypeStruct((1, count), jnp.float32),
        ],
        in_specs=[VMEM] * (1 + len(back)),
        out_specs=[VMEM, VMEM],
        compiler_params=GRANT,
        name="restore_rows",
    )(chosen, *back[n_gr - 1 :: -1], *back[:n_gr - 1 : -1])
    return (neighbour_sum, density.reshape(count))


def solution(mesh):
    in_specs = (P(("gr", "gc"), None), P(("gr", "gc")))
    out_specs = (P(("gr", "gc"), None), P(("gr", "gc")))
    return jax.shard_map(
        functools.partial(on_device, mesh.shape["gr"], mesh.shape["gc"]),
        mesh=mesh,
        in_specs=in_specs,
        out_specs=out_specs,
        check_vma=False,
    )
```

```python
import functools
import math

import jax
import jax.numpy as jnp
from jax import lax
from jax.experimental import pallas as pl
from jax.experimental.pallas import tpu as pltpu
from jax.sharding import PartitionSpec as P

beta_scale = 16.0
LANES = 128
EXTRA = 8
TOP = 14.0
VMEM = pl.BlockSpec(memory_space=pltpu.VMEM)
HBM = pl.BlockSpec(memory_space=pltpu.HBM)
SMEM = pl.BlockSpec(memory_space=pltpu.SMEM)
GRANT = pltpu.CompilerParams(vmem_limit_bytes=40 * 1024 * 1024)


def in_hbm(array):
    return pltpu.with_memory_space_constraint(array, pltpu.HBM)


def diagonal(count):
    first = lax.broadcasted_iota(jnp.int32, (count, count), 0)
    second = lax.broadcasted_iota(jnp.int32, (count, count), 1)
    return first == second


def as_row(column):
    return jnp.sum(
        jnp.where(diagonal(column.shape[0]), column, jnp.zeros_like(column)),
        axis=0,
        keepdims=True,
    )


def as_column(row):
    return jnp.sum(
        jnp.where(diagonal(row.shape[1]), row, jnp.zeros_like(row)),
        axis=1,
        keepdims=True,
    )


def placement(own, ids, groups):
    count = ids.shape[1]
    first = lax.broadcasted_iota(jnp.int32, (count, count), 0)
    second = lax.broadcasted_iota(jnp.int32, (count, count), 1)
    earlier = jnp.where((as_column(ids) == ids) & (first < second), 1, 0)
    rank = jnp.sum(earlier, axis=0, keepdims=True)
    slot = (ids ^ own) * (count // groups) + rank
    return jnp.where(first == slot, 1.0, 0.0)


def sort_kernel(own_ref, ids_hbm, rows_hbm, *refs):
    chosen_ref, *out_refs = refs[:-4]
    ids_ref, rows_ref, ids_sem, rows_sem = refs[-4:]
    groups = len(out_refs)
    ids_copy = pltpu.make_async_copy(ids_hbm, ids_ref, ids_sem)
    rows_copy = pltpu.make_async_copy(rows_hbm, rows_ref, rows_sem)
    ids_copy.start()
    rows_copy.start()
    ids_copy.wait()
    chosen = placement(own_ref[0], ids_ref[...], groups).astype(jnp.bfloat16)
    chosen_ref[...] = chosen
    rows_copy.wait()
    ordered = jnp.dot(chosen, rows_ref[...], preferred_element_type=jnp.float32)
    ordered = ordered.astype(jnp.bfloat16)
    size = ordered.shape[0] // groups
    for k, out_ref in enumerate(out_refs):
        out_ref[...] = ordered[k * size : (k + 1) * size, :]


def inverse_norms(rows):
    wide = rows.astype(jnp.float32)
    return lax.rsqrt(jnp.sum(wide * wide, axis=1, keepdims=True) + 1e-06)


def add_columns(rows, col_refs, total, dens):
    count = rows.shape[0]
    scale = inverse_norms(rows) * (beta_scale * math.log2(math.e))
    blocks = [
        (col_ref, start)
        for col_ref in col_refs
        for start in range(0, col_ref.shape[0], count)
    ]
    for col_ref, start in blocks:
        cols = col_ref[start : min(start + count, col_ref.shape[0]), :]
        size = cols.shape[0]
        col_inv = as_row(inverse_norms(cols))
        raw = lax.dot_general(
            rows, cols, (((1,), (1,)), ((), ())), preferred_element_type=jnp.float32
        )
        weight = jnp.exp2(raw * scale * col_inv - beta_scale * math.log2(math.e))
        whole = size - size % LANES
        for lane in range(0, whole, LANES):
            dens += weight[:, lane : lane + LANES]
        if whole < size:
            part = jnp.sum(weight[:, whole:], axis=1, keepdims=True)
            dens += jnp.where(lax.broadcasted_iota(jnp.int32, dens.shape, 1) == 0, part, 0.0)
        coef = (weight * col_inv).astype(jnp.bfloat16)
        total += jnp.dot(coef, cols, preferred_element_type=jnp.float32)
    return total, dens


def first_kernel(rows_ref, *refs):
    col_refs, (total_ref, dens_ref) = refs[:-2], refs[-2:]
    total = jnp.zeros(total_ref.shape, jnp.float32)
    dens = jnp.zeros(dens_ref.shape, jnp.float32)
    total, dens = add_columns(rows_ref[...], col_refs, total, dens)
    total_ref[...] = total
    dens_ref[...] = dens


def middle_kernel(rows_ref, total_ref, dens_ref, *refs):
    col_refs, (total_out, dens_out) = refs[:-2], refs[-2:]
    total, dens = add_columns(rows_ref[...], col_refs, total_ref[...], dens_ref[...])
    total_out[...] = total
    dens_out[...] = dens


def exponent(value):
    return jnp.floor(jnp.log2(jnp.maximum(value, 1e-30)))


def last_kernel(half, rows_ref, total_ref, dens_ref, cols_ref, *out_refs):
    groups = len(out_refs) - half
    size = out_refs[half].shape[0]
    total, dens = add_columns(
        rows_ref[...], [cols_ref], total_ref[...], dens_ref[...]
    )
    dens = jnp.sum(dens, axis=1, keepdims=True)
    power = exponent(jnp.max(jnp.abs(total), axis=1, keepdims=True))
    total = total * jnp.exp2(TOP - power)
    dens_power = exponent(dens)
    part = dens * jnp.exp2(-dens_power)
    aside = [power, dens_power]
    for k in range(3):
        piece = part.astype(jnp.bfloat16).astype(jnp.float32)
        aside.append(piece * 2.0 ** (8 * k))
        part = part - piece
    for k in range(groups):
        rows = slice(k * size, (k + 1) * size)
        out_refs[k][:size, :] = total[rows, :]
        if k < half:
            aside_ref, top = out_refs[k], size
            aside_ref[size:, :] = jnp.zeros((EXTRA, total.shape[1]), jnp.float32)
        else:
            aside_ref, top = out_refs[half + k], 0
            aside_ref[...] = jnp.zeros(aside_ref.shape, jnp.float32)
        for line, column in enumerate(aside):
            aside_ref[top + line : top + line + 1, :size] = as_row(column[rows, :])


def restore_kernel(half, chosen_ref, *refs):
    refs, (total_ref, dens_ref) = refs[:-2], refs[-2:]
    groups = len(refs) - half
    part_refs = refs[groups - 1 :: -1] + refs[: groups - 1 : -1]
    size = part_refs[half].shape[0]
    chosen = chosen_ref[...]
    sums, dens = [], []
    for k in range(groups):
        aside_ref, top = (part_refs[k], size) if k < half else (part_refs[half + k], 0)
        power, dens_power, *pieces = [
            as_column(aside_ref[top + line : top + line + 1, :size])
            for line in range(5)
        ]
        sums.append(part_refs[k][:size, :] * jnp.exp2(power - TOP))
        part = sum(piece * 2.0 ** (-8 * j) for j, piece in enumerate(pieces))
        dens.append(part * jnp.exp2(dens_power))
    dens_ref[...] = jnp.sum(
        chosen.astype(jnp.float32) * jnp.concatenate(dens, axis=0), axis=0, keepdims=True
    )
    rest = jnp.concatenate(sums, axis=0)
    back = jnp.zeros(rest.shape, jnp.float32)
    for _ in range(2):
        piece = rest.astype(jnp.bfloat16)
        rest = rest - piece.astype(jnp.float32)
        back += lax.dot_general(
            chosen, piece, (((0,), (0,)), ((), ())), preferred_element_type=jnp.float32
        )
    total_ref[...] = back


def on_device(n_gr, n_gc, embeddings, cluster_ids):
    count, width = embeddings.shape
    size = count // n_gr
    own = lax.axis_index("gr").astype(jnp.int32).reshape(1)
    ids = cluster_ids.reshape(1, count)

    chosen, *parts = pl.pallas_call(
        sort_kernel,
        out_shape=[jax.ShapeDtypeStruct((count, count), jnp.bfloat16)]
        + [jax.ShapeDtypeStruct((size, width), jnp.bfloat16)] * n_gr,
        in_specs=[SMEM, HBM, HBM],
        out_specs=[VMEM] * (1 + n_gr),
        scratch_shapes=[
            pltpu.VMEM((1, count), jnp.int32),
            pltpu.VMEM((count, width), embeddings.dtype),
            pltpu.SemaphoreType.DMA,
            pltpu.SemaphoreType.DMA,
        ],
        compiler_params=GRANT,
        name="sort_rows",
    )(own, in_hbm(ids), in_hbm(embeddings))

    def along_gr(part, bits):
        return lax.ppermute(part, "gr", [(i, i ^ bits) for i in range(n_gr)])

    def along_gc(block, bits):
        return lax.ppermute(block, "gc", [(i, i ^ bits) for i in range(n_gc)])

    def other_core(block):
        return along_gc(block, 1)

    def cost(*blocks):
        pairs = count * sum(block.shape[0] for block in blocks)
        return pl.CostEstimate(
            flops=4 * pairs * width,
            bytes_accessed=0,
            transcendentals=pairs,
        )

    held = [parts[0]] + [along_gr(parts[k], k) for k in range(1, n_gr)]
    half = n_gr // 2
    sides = [k for k in range(2, n_gc, 2) if not k & (k - 1)]
    corners = [k for k in range(2, n_gc, 2) if k & (k - 1)]

    def to_side(block, step):
        pairs = [(i, i ^ sides[(step + i % 2) % len(sides)]) for i in range(n_gc)]
        return lax.ppermute(block, "gc", pairs)

    chunks = []
    for pieces in (held[:half], held[half:]):
        block = jnp.concatenate(pieces, axis=0)
        near = [block] + [along_gc(block, k) for k in corners]
        near += [to_side(block, step) for step in range(len(sides))]
        chunks.append(jnp.concatenate(near, axis=0))
    rows = jnp.concatenate(held, axis=0)
    chunks[0], rows = lax.optimization_barrier((chunks[0], rows))
    early = [chunks[0], other_core(chunks[0])]

    total, dens = pl.pallas_call(
        first_kernel,
        out_shape=[
            jax.ShapeDtypeStruct((count, width), jnp.float32),
            jax.ShapeDtypeStruct((count, LANES), jnp.float32),
        ],
        in_specs=[VMEM] * (1 + len(early)),
        out_specs=[VMEM] * 2,
        compiler_params=GRANT,
        cost_estimate=cost(*early),
        name="early_sums",
    )(rows, *early)
    total, dens = pl.pallas_call(
        middle_kernel,
        out_shape=[
            jax.ShapeDtypeStruct((count, width), jnp.float32),
            jax.ShapeDtypeStruct((count, LANES), jnp.float32),
        ],
        in_specs=[VMEM] * 4,
        out_specs=[VMEM] * 2,
        compiler_params=GRANT,
        cost_estimate=cost(chunks[1]),
        name="middle_sums",
    )(rows, total, dens, chunks[1])
    late = [other_core(chunks[1])]
    sums = pl.pallas_call(
        functools.partial(last_kernel, half),
        out_shape=[jax.ShapeDtypeStruct((size + EXTRA, width), jnp.float32)] * half
        + [jax.ShapeDtypeStruct((size, width), jnp.float32)] * (n_gr - half)
        + [jax.ShapeDtypeStruct((EXTRA, LANES), jnp.float32)] * (n_gr - half),
        in_specs=[VMEM] * 4,
        out_specs=[VMEM] * (2 * n_gr - half),
        compiler_params=GRANT,
        cost_estimate=cost(*late),
        name="last_sums",
    )(rows, total, dens, *late)

    sent = [part.astype(jnp.float16) for part in sums[:n_gr]]
    back = [sent[0]] + [along_gr(sent[k], k) for k in range(1, n_gr)]
    back = [part.astype(jnp.float32) for part in back]
    back += [along_gr(sums[half + k], k) for k in range(half, n_gr)]
    neighbour_sum, density = pl.pallas_call(
        functools.partial(restore_kernel, half),
        out_shape=[
            jax.ShapeDtypeStruct((count, width), jnp.float32),
            jax.ShapeDtypeStruct((1, count), jnp.float32),
        ],
        in_specs=[VMEM] * (1 + len(back)),
        out_specs=[VMEM, VMEM],
        compiler_params=GRANT,
        name="restore_rows",
    )(chosen, *back[n_gr - 1 :: -1], *back[:n_gr - 1 : -1])
    return (neighbour_sum, density.reshape(count))


def solution(mesh):
    in_specs = (P(("gr", "gc"), None), P(("gr", "gc")))
    out_specs = (P(("gr", "gc"), None), P(("gr", "gc")))
    return jax.shard_map(
        functools.partial(on_device, mesh.shape["gr"], mesh.shape["gc"]),
        mesh=mesh,
        in_specs=in_specs,
        out_specs=out_specs,
        check_vma=False,
    )
```

```python
import functools
import math

import jax
import jax.numpy as jnp
from jax import lax
from jax.experimental import pallas as pl
from jax.experimental.pallas import tpu as pltpu
from jax.sharding import PartitionSpec as P

beta_scale = 16.0
LANES = 128
EXTRA = 8
TOP = 14.0
COPIES = 4
VMEM = pl.BlockSpec(memory_space=pltpu.VMEM)
HBM = pl.BlockSpec(memory_space=pltpu.HBM)
SMEM = pl.BlockSpec(memory_space=pltpu.SMEM)
GRANT = pltpu.CompilerParams(vmem_limit_bytes=40 * 1024 * 1024)


def in_hbm(array):
    return pltpu.with_memory_space_constraint(array, pltpu.HBM)


def diagonal(count):
    first = lax.broadcasted_iota(jnp.int32, (count, count), 0)
    second = lax.broadcasted_iota(jnp.int32, (count, count), 1)
    return first == second


def as_row(column):
    return jnp.sum(
        jnp.where(diagonal(column.shape[0]), column, jnp.zeros_like(column)),
        axis=0,
        keepdims=True,
    )


def as_column(row):
    return jnp.sum(
        jnp.where(diagonal(row.shape[1]), row, jnp.zeros_like(row)),
        axis=1,
        keepdims=True,
    )


def placement(own, ids, groups):
    count = ids.shape[1]
    first = lax.broadcasted_iota(jnp.int32, (count, count), 0)
    second = lax.broadcasted_iota(jnp.int32, (count, count), 1)
    earlier = jnp.where((as_column(ids) == ids) & (first < second), 1, 0)
    rank = jnp.sum(earlier, axis=0, keepdims=True)
    slot = (ids ^ own) * (count // groups) + rank
    return jnp.where(first == slot, 1.0, 0.0)


def row_blocks(count):
    size = count // COPIES
    return [pl.ds(k * size, size) for k in range(COPIES)]


def sort_kernel(own_ref, ids_hbm, rows_hbm, *refs):
    chosen_ref, *out_refs = refs[:-4]
    ids_ref, rows_ref, ids_sem, rows_sem = refs[-4:]
    groups = len(out_refs)
    ids_copy = pltpu.make_async_copy(ids_hbm, ids_ref, ids_sem)
    ids_copy.start()
    row_copies = []
    for k, rows in enumerate(row_blocks(rows_hbm.shape[0])):
        row_copies.append(
            pltpu.make_async_copy(rows_hbm.at[rows], rows_ref.at[rows], rows_sem.at[k])
        )
        row_copies[-1].start()
    ids_copy.wait()
    chosen = placement(own_ref[0], ids_ref[...], groups).astype(jnp.bfloat16)
    chosen_ref[...] = chosen
    for row_copy in row_copies:
        row_copy.wait()
    ordered = jnp.dot(chosen, rows_ref[...], preferred_element_type=jnp.float32)
    ordered = ordered.astype(jnp.bfloat16)
    size = ordered.shape[0] // groups
    for k, out_ref in enumerate(out_refs):
        out_ref[...] = ordered[k * size : (k + 1) * size, :]


def inverse_norms(rows):
    wide = rows.astype(jnp.float32)
    return lax.rsqrt(jnp.sum(wide * wide, axis=1, keepdims=True) + 1e-06)


def add_columns(rows, col_refs, total, dens):
    count = rows.shape[0]
    scale = inverse_norms(rows) * (beta_scale * math.log2(math.e))
    blocks = [
        (col_ref, start)
        for col_ref in col_refs
        for start in range(0, col_ref.shape[0], count)
    ]
    for col_ref, start in blocks:
        cols = col_ref[start : min(start + count, col_ref.shape[0]), :]
        size = cols.shape[0]
        col_inv = as_row(inverse_norms(cols))
        raw = lax.dot_general(
            rows, cols, (((1,), (1,)), ((), ())), preferred_element_type=jnp.float32
        )
        weight = jnp.exp2(raw * scale * col_inv - beta_scale * math.log2(math.e))
        whole = size - size % LANES
        for lane in range(0, whole, LANES):
            dens += weight[:, lane : lane + LANES]
        if whole < size:
            part = jnp.sum(weight[:, whole:], axis=1, keepdims=True)
            dens += jnp.where(lax.broadcasted_iota(jnp.int32, dens.shape, 1) == 0, part, 0.0)
        coef = (weight * col_inv).astype(jnp.bfloat16)
        total += jnp.dot(coef, cols, preferred_element_type=jnp.float32)
    return total, dens


def first_kernel(rows_ref, *refs):
    col_refs, (total_ref, dens_ref) = refs[:-2], refs[-2:]
    total = jnp.zeros(total_ref.shape, jnp.float32)
    dens = jnp.zeros(dens_ref.shape, jnp.float32)
    total, dens = add_columns(rows_ref[...], col_refs, total, dens)
    total_ref[...] = total
    dens_ref[...] = dens


def middle_kernel(rows_ref, total_ref, dens_ref, *refs):
    col_refs, (total_out, dens_out) = refs[:-2], refs[-2:]
    total, dens = add_columns(rows_ref[...], col_refs, total_ref[...], dens_ref[...])
    total_out[...] = total
    dens_out[...] = dens


def exponent(value):
    return jnp.floor(jnp.log2(jnp.maximum(value, 1e-30)))


def last_kernel(half, rows_ref, total_ref, dens_ref, cols_ref, *out_refs):
    groups = len(out_refs) - half
    size = out_refs[half].shape[0]
    total, dens = add_columns(
        rows_ref[...], [cols_ref], total_ref[...], dens_ref[...]
    )
    dens = jnp.sum(dens, axis=1, keepdims=True)
    power = exponent(jnp.max(jnp.abs(total), axis=1, keepdims=True))
    total = total * jnp.exp2(TOP - power)
    dens_power = exponent(dens)
    part = dens * jnp.exp2(-dens_power)
    aside = [power, dens_power]
    for k in range(3):
        piece = part.astype(jnp.bfloat16).astype(jnp.float32)
        aside.append(piece * 2.0 ** (8 * k))
        part = part - piece
    for k in range(groups):
        rows = slice(k * size, (k + 1) * size)
        out_refs[k][:size, :] = total[rows, :]
        if k < half:
            aside_ref, top = out_refs[k], size
            aside_ref[size:, :] = jnp.zeros((EXTRA, total.shape[1]), jnp.float32)
        else:
            aside_ref, top = out_refs[half + k], 0
            aside_ref[...] = jnp.zeros(aside_ref.shape, jnp.float32)
        for line, column in enumerate(aside):
            aside_ref[top + line : top + line + 1, :size] = as_row(column[rows, :])


def turn_kernel(chosen_ref, turned_ref):
    turned_ref[...] = chosen_ref[...].astype(jnp.float32).T.astype(jnp.bfloat16)


def restore_kernel(half, chosen_ref, turned_ref, *refs):
    refs, (total_hbm, dens_hbm, total_ref, dens_ref, total_sem, dens_sem) = (
        refs[:-6],
        refs[-6:],
    )
    groups = len(refs) - half
    part_refs = refs[groups - 1 :: -1] + refs[: groups - 1 : -1]
    size = part_refs[half].shape[0]
    sums, dens = [], []
    for k in range(groups):
        aside_ref, top = (part_refs[k], size) if k < half else (part_refs[half + k], 0)
        power, dens_power, *pieces = [
            as_column(aside_ref[top + line : top + line + 1, :size])
            for line in range(5)
        ]
        sums.append(part_refs[k][:size, :] * jnp.exp2(power - TOP))
        part = sum(piece * 2.0 ** (-8 * j) for j, piece in enumerate(pieces))
        dens.append(part * jnp.exp2(dens_power))
    dens_ref[...] = jnp.sum(
        chosen_ref[...].astype(jnp.float32) * jnp.concatenate(dens, axis=0),
        axis=0,
        keepdims=True,
    )
    copies = [pltpu.make_async_copy(dens_ref, dens_hbm, dens_sem)]
    copies[0].start()
    rest = jnp.concatenate(sums, axis=0)
    high = rest.astype(jnp.bfloat16)
    low = (rest - high.astype(jnp.float32)).astype(jnp.bfloat16)
    for k, rows in enumerate(row_blocks(total_ref.shape[0])):
        turned = turned_ref[rows, :]
        total_ref[rows, :] = jnp.dot(
            turned, high, preferred_element_type=jnp.float32
        ) + jnp.dot(turned, low, preferred_element_type=jnp.float32)
        copies.append(
            pltpu.make_async_copy(
                total_ref.at[rows], total_hbm.at[rows], total_sem.at[k]
            )
        )
        copies[-1].start()
    for copy in copies:
        copy.wait()


def on_device(n_gr, n_gc, embeddings, cluster_ids):
    count, width = embeddings.shape
    size = count // n_gr
    own = lax.axis_index("gr").astype(jnp.int32).reshape(1)
    ids = cluster_ids.reshape(1, count)

    chosen, *parts = pl.pallas_call(
        sort_kernel,
        out_shape=[jax.ShapeDtypeStruct((count, count), jnp.bfloat16)]
        + [jax.ShapeDtypeStruct((size, width), jnp.bfloat16)] * n_gr,
        in_specs=[SMEM, HBM, HBM],
        out_specs=[VMEM] * (1 + n_gr),
        scratch_shapes=[
            pltpu.VMEM((1, count), jnp.int32),
            pltpu.VMEM((count, width), embeddings.dtype),
            pltpu.SemaphoreType.DMA,
            pltpu.SemaphoreType.DMA((COPIES,)),
        ],
        compiler_params=GRANT,
        name="sort_rows",
    )(own, in_hbm(ids), in_hbm(embeddings))

    def along_gr(part, bits):
        return lax.ppermute(part, "gr", [(i, i ^ bits) for i in range(n_gr)])

    def along_gc(block, bits):
        return lax.ppermute(block, "gc", [(i, i ^ bits) for i in range(n_gc)])

    def other_core(block):
        return along_gc(block, 1)

    def cost(*blocks):
        pairs = count * sum(block.shape[0] for block in blocks)
        return pl.CostEstimate(
            flops=4 * pairs * width,
            bytes_accessed=0,
            transcendentals=pairs,
        )

    held = [parts[0]] + [along_gr(parts[k], k) for k in range(1, n_gr)]
    half = n_gr // 2
    sides = [k for k in range(2, n_gc, 2) if not k & (k - 1)]
    corners = [k for k in range(2, n_gc, 2) if k & (k - 1)]

    def to_side(block, step):
        pairs = [(i, i ^ sides[(step + i % 2) % len(sides)]) for i in range(n_gc)]
        return lax.ppermute(block, "gc", pairs)

    chunks = []
    for pieces in (held[:half], held[half:]):
        block = jnp.concatenate(pieces, axis=0)
        near = [block] + [along_gc(block, k) for k in corners]
        near += [to_side(block, step) for step in range(len(sides))]
        chunks.append(jnp.concatenate(near, axis=0))
    rows = jnp.concatenate(held, axis=0)
    chunks[0], rows = lax.optimization_barrier((chunks[0], rows))
    early = [chunks[0], other_core(chunks[0])]

    total, dens = pl.pallas_call(
        first_kernel,
        out_shape=[
            jax.ShapeDtypeStruct((count, width), jnp.float32),
            jax.ShapeDtypeStruct((count, LANES), jnp.float32),
        ],
        in_specs=[VMEM] * (1 + len(early)),
        out_specs=[VMEM] * 2,
        compiler_params=GRANT,
        cost_estimate=cost(*early),
        name="early_sums",
    )(rows, *early)
    total, dens = pl.pallas_call(
        middle_kernel,
        out_shape=[
            jax.ShapeDtypeStruct((count, width), jnp.float32),
            jax.ShapeDtypeStruct((count, LANES), jnp.float32),
        ],
        in_specs=[VMEM] * 4,
        out_specs=[VMEM] * 2,
        compiler_params=GRANT,
        cost_estimate=cost(chunks[1]),
        name="middle_sums",
    )(rows, total, dens, chunks[1])
    late = [other_core(chunks[1])]
    sums = pl.pallas_call(
        functools.partial(last_kernel, half),
        out_shape=[jax.ShapeDtypeStruct((size + EXTRA, width), jnp.float32)] * half
        + [jax.ShapeDtypeStruct((size, width), jnp.float32)] * (n_gr - half)
        + [jax.ShapeDtypeStruct((EXTRA, LANES), jnp.float32)] * (n_gr - half),
        in_specs=[VMEM] * 4,
        out_specs=[VMEM] * (2 * n_gr - half),
        compiler_params=GRANT,
        cost_estimate=cost(*late),
        name="last_sums",
    )(rows, total, dens, *late)

    sent = [part.astype(jnp.float16) for part in sums[:n_gr]]
    back = [sent[0]] + [along_gr(sent[k], k) for k in range(1, n_gr)]
    back = [part.astype(jnp.float32) for part in back]
    chosen, back[0] = lax.optimization_barrier((chosen, back[0]))
    back += [along_gr(sums[half + k], k) for k in range(half, n_gr)]
    turned = pl.pallas_call(
        turn_kernel,
        out_shape=jax.ShapeDtypeStruct((count, count), jnp.bfloat16),
        in_specs=[VMEM],
        out_specs=VMEM,
        compiler_params=GRANT,
        name="turn_matrix",
    )(chosen)
    neighbour_sum, density = pl.pallas_call(
        functools.partial(restore_kernel, half),
        out_shape=[
            jax.ShapeDtypeStruct((count, width), jnp.float32),
            jax.ShapeDtypeStruct((1, count), jnp.float32),
        ],
        in_specs=[VMEM] * (2 + len(back)),
        out_specs=[HBM, HBM],
        scratch_shapes=[
            pltpu.VMEM((count, width), jnp.float32),
            pltpu.VMEM((1, count), jnp.float32),
            pltpu.SemaphoreType.DMA((COPIES,)),
            pltpu.SemaphoreType.DMA,
        ],
        compiler_params=GRANT,
        name="restore_rows",
    )(chosen, turned, *back[n_gr - 1 :: -1], *back[:n_gr - 1 : -1])
    return (neighbour_sum, density.reshape(count))


def solution(mesh):
    in_specs = (P(("gr", "gc"), None), P(("gr", "gc")))
    out_specs = (P(("gr", "gc"), None), P(("gr", "gc")))
    return jax.shard_map(
        functools.partial(on_device, mesh.shape["gr"], mesh.shape["gc"]),
        mesh=mesh,
        in_specs=in_specs,
        out_specs=out_specs,
        check_vma=False,
    )
```

```python
import functools
import math

import jax
import jax.numpy as jnp
from jax import lax
from jax.experimental import pallas as pl
from jax.experimental.pallas import tpu as pltpu
from jax.sharding import PartitionSpec as P

beta_scale = 16.0
floor_weight = math.exp(-beta_scale)
BLOCK = 512
LANES = 128
EXTRA = 8
TOP = 14.0
VMEM = pl.BlockSpec(memory_space=pltpu.VMEM)
HBM = pl.BlockSpec(memory_space=pltpu.HBM)
SMEM = pl.BlockSpec(memory_space=pltpu.SMEM)
GRANT = pltpu.CompilerParams(vmem_limit_bytes=40 * 1024 * 1024)


def in_hbm(array):
    return pltpu.with_memory_space_constraint(array, pltpu.HBM)


def diagonal(count):
    first = lax.broadcasted_iota(jnp.int32, (count, count), 0)
    second = lax.broadcasted_iota(jnp.int32, (count, count), 1)
    return first == second


def as_row(column):
    return jnp.sum(
        jnp.where(diagonal(column.shape[0]), column, jnp.zeros_like(column)),
        axis=0,
        keepdims=True,
    )


def as_column(row):
    return jnp.sum(
        jnp.where(diagonal(row.shape[1]), row, jnp.zeros_like(row)),
        axis=1,
        keepdims=True,
    )


def placement(own, ids, groups):
    count = ids.shape[1]
    first = lax.broadcasted_iota(jnp.int32, (count, count), 0)
    second = lax.broadcasted_iota(jnp.int32, (count, count), 1)
    earlier = jnp.where((as_column(ids) == ids) & (first < second), 1, 0)
    rank = jnp.sum(earlier, axis=0, keepdims=True)
    slot = (ids ^ own) * (count // groups) + rank
    return jnp.where(first == slot, 1.0, 0.0)


def sort_kernel(own_ref, ids_hbm, rows_hbm, *refs):
    chosen_ref, *out_refs = refs[:-4]
    ids_ref, rows_ref, ids_sem, rows_sem = refs[-4:]
    groups = len(out_refs)
    ids_copy = pltpu.make_async_copy(ids_hbm, ids_ref, ids_sem)
    rows_copy = pltpu.make_async_copy(rows_hbm, rows_ref, rows_sem)
    ids_copy.start()
    rows_copy.start()
    ids_copy.wait()
    chosen = placement(own_ref[0], ids_ref[...], groups).astype(jnp.bfloat16)
    chosen_ref[...] = chosen
    rows_copy.wait()
    ordered = jnp.dot(chosen, rows_ref[...], preferred_element_type=jnp.float32)
    ordered = ordered.astype(jnp.bfloat16)
    size = ordered.shape[0] // groups
    for k, out_ref in enumerate(out_refs):
        out_ref[...] = ordered[k * size : (k + 1) * size, :]


def folded_squares(rows):
    total = 0.0
    for lane in range(0, rows.shape[1], LANES):
        wide = rows[:, lane : lane + LANES].astype(jnp.float32)
        total += wide * wide
    return total


def add_columns(rows, scale, col_refs, total, dens):
    for col_ref in col_refs:
        for start in range(0, col_ref.shape[0], BLOCK):
            cols = col_ref[start : min(start + BLOCK, col_ref.shape[0]), :]
            squares = jnp.sum(folded_squares(cols).T, axis=0, keepdims=True)
            col_inv = lax.rsqrt(squares + 1e-06)
            raw = lax.dot_general(
                rows, cols, (((1,), (1,)), ((), ())), preferred_element_type=jnp.float32
            )
            weight = jnp.exp2(raw * scale * col_inv)
            for lane in range(0, cols.shape[0], LANES):
                dens += weight[:, lane : lane + LANES]
            coef = (weight * (col_inv * floor_weight)).astype(jnp.bfloat16)
            total += jnp.dot(coef, cols, preferred_element_type=jnp.float32)
    return total, dens


def early_kernel(rows_ref, *refs):
    col_refs, (scale_ref, total_ref, dens_ref) = refs[:-3], refs[-3:]
    squares = jnp.sum(folded_squares(rows_ref[...]), axis=1, keepdims=True)
    scale = lax.rsqrt(squares + 1e-06) * (beta_scale * math.log2(math.e))
    scale_ref[...] = jnp.broadcast_to(scale, scale_ref.shape)
    total = jnp.zeros(total_ref.shape, jnp.float32)
    dens = jnp.zeros(dens_ref.shape, jnp.float32)
    total, dens = add_columns(rows_ref[...], scale, col_refs, total, dens)
    total_ref[...] = total
    dens_ref[...] = dens


def middle_kernel(rows_ref, scale_ref, total_ref, dens_ref, *refs):
    col_refs, (total_out, dens_out) = refs[:-2], refs[-2:]
    total, dens = add_columns(
        rows_ref[...], scale_ref[:, 0:1], col_refs, total_ref[...], dens_ref[...]
    )
    total_out[...] = total
    dens_out[...] = dens


def exponent(value):
    return jnp.floor(jnp.log2(jnp.maximum(value, 1e-30)))


def last_kernel(half, rows_ref, scale_ref, total_ref, dens_ref, cols_ref, *out_refs):
    groups = len(out_refs) - half
    size = out_refs[half].shape[0]
    total, dens = add_columns(
        rows_ref[...], scale_ref[:, 0:1], [cols_ref], total_ref[...], dens_ref[...]
    )
    dens = jnp.sum(dens, axis=1, keepdims=True) * floor_weight
    power = exponent(jnp.max(jnp.abs(total), axis=1, keepdims=True))
    total = total * jnp.exp2(TOP - power)
    dens_power = exponent(dens)
    part = dens * jnp.exp2(-dens_power)
    aside = [power, dens_power]
    for k in range(3):
        piece = part.astype(jnp.bfloat16).astype(jnp.float32)
        aside.append(piece * 2.0 ** (8 * k))
        part = part - piece
    for k in range(groups):
        rows = slice(k * size, (k + 1) * size)
        out_refs[k][:size, :] = total[rows, :]
        if k < half:
            aside_ref, top = out_refs[k], size
            aside_ref[size:, :] = jnp.zeros((EXTRA, total.shape[1]), jnp.float32)
        else:
            aside_ref, top = out_refs[half + k], 0
            aside_ref[...] = jnp.zeros(aside_ref.shape, jnp.float32)
        for line, column in enumerate(aside):
            aside_ref[top + line : top + line + 1, :size] = as_row(column[rows, :])


def restore_kernel(half, chosen_ref, *refs):
    refs, (total_ref, dens_ref) = refs[:-2], refs[-2:]
    groups = len(refs) - half
    part_refs = refs[groups - 1 :: -1] + refs[: groups - 1 : -1]
    size = part_refs[half].shape[0]
    chosen = chosen_ref[...]
    sums, dens = [], []
    for k in range(groups):
        aside_ref, top = (part_refs[k], size) if k < half else (part_refs[half + k], 0)
        power, dens_power, *pieces = [
            as_column(aside_ref[top + line : top + line + 1, :size])
            for line in range(5)
        ]
        sums.append(part_refs[k][:size, :] * jnp.exp2(power - TOP))
        part = sum(piece * 2.0 ** (-8 * j) for j, piece in enumerate(pieces))
        dens.append(part * jnp.exp2(dens_power))
    dens_ref[...] = jnp.sum(
        chosen.astype(jnp.float32) * jnp.concatenate(dens, axis=0), axis=0, keepdims=True
    )
    rest = jnp.concatenate(sums, axis=0)
    back = jnp.zeros(rest.shape, jnp.float32)
    for _ in range(2):
        piece = rest.astype(jnp.bfloat16)
        rest = rest - piece.astype(jnp.float32)
        back += lax.dot_general(
            chosen, piece, (((0,), (0,)), ((), ())), preferred_element_type=jnp.float32
        )
    total_ref[...] = back


def on_device(n_gr, n_gc, embeddings, cluster_ids):
    count, width = embeddings.shape
    size = count // n_gr
    own = lax.axis_index("gr").astype(jnp.int32).reshape(1)
    ids = cluster_ids.reshape(1, count)

    chosen, *parts = pl.pallas_call(
        sort_kernel,
        out_shape=[jax.ShapeDtypeStruct((count, count), jnp.bfloat16)]
        + [jax.ShapeDtypeStruct((size, width), jnp.bfloat16)] * n_gr,
        in_specs=[SMEM, HBM, HBM],
        out_specs=[VMEM] * (1 + n_gr),
        scratch_shapes=[
            pltpu.VMEM((1, count), jnp.int32),
            pltpu.VMEM((count, width), embeddings.dtype),
            pltpu.SemaphoreType.DMA,
            pltpu.SemaphoreType.DMA,
        ],
        compiler_params=GRANT,
        name="sort_rows",
    )(own, in_hbm(ids), in_hbm(embeddings))

    def along_gr(part, bits):
        return lax.ppermute(part, "gr", [(i, i ^ bits) for i in range(n_gr)])

    def along_gc(block, bits):
        return lax.ppermute(block, "gc", [(i, i ^ bits) for i in range(n_gc)])

    def other_core(block):
        return along_gc(block, 1)

    def cost(*blocks):
        pairs = count * sum(block.shape[0] for block in blocks)
        return pl.CostEstimate(
            flops=4 * pairs * width,
            bytes_accessed=0,
            transcendentals=pairs,
        )

    held = [parts[0]] + [along_gr(parts[k], k) for k in range(1, n_gr)]
    half = n_gr // 2
    sides = [k for k in range(2, n_gc, 2) if not k & (k - 1)]
    corners = [k for k in range(2, n_gc, 2) if k & (k - 1)]

    def to_side(block, step):
        pairs = [(i, i ^ sides[(step + i % 2) % len(sides)]) for i in range(n_gc)]
        return lax.ppermute(block, "gc", pairs)

    chunks = []
    for pieces in (held[:half], held[half:]):
        block = jnp.concatenate(pieces, axis=0)
        near = [block] + [along_gc(block, k) for k in corners]
        near += [to_side(block, step) for step in range(len(sides))]
        chunks.append(jnp.concatenate(near, axis=0))
    rows = jnp.concatenate(held, axis=0)
    chunks[0], rows = lax.optimization_barrier((chunks[0], rows))
    early = [chunks[0], other_core(chunks[0]), chunks[1]]

    scale, total, dens = pl.pallas_call(
        early_kernel,
        out_shape=[
            jax.ShapeDtypeStruct((count, LANES), jnp.float32),
            jax.ShapeDtypeStruct((count, width), jnp.float32),
            jax.ShapeDtypeStruct((count, LANES), jnp.float32),
        ],
        in_specs=[VMEM] * (1 + len(early)),
        out_specs=[VMEM] * 3,
        compiler_params=GRANT,
        cost_estimate=cost(*early),
        name="early_sums",
    )(rows, *early)
    late = other_core(chunks[1])
    sums = pl.pallas_call(
        functools.partial(last_kernel, half),
        out_shape=[jax.ShapeDtypeStruct((size + EXTRA, width), jnp.float32)] * half
        + [jax.ShapeDtypeStruct((size, width), jnp.float32)] * (n_gr - half)
        + [jax.ShapeDtypeStruct((EXTRA, LANES), jnp.float32)] * (n_gr - half),
        in_specs=[VMEM] * 5,
        out_specs=[VMEM] * (2 * n_gr - half),
        compiler_params=GRANT,
        cost_estimate=cost(late),
        name="last_sums",
    )(rows, scale, total, dens, late)

    sent = [part.astype(jnp.float16) for part in sums[:n_gr]]
    back = [sent[0]] + [along_gr(sent[k], k) for k in range(1, n_gr)]
    back = [part.astype(jnp.float32) for part in back]
    back += [along_gr(sums[half + k], k) for k in range(half, n_gr)]
    neighbour_sum, density = pl.pallas_call(
        functools.partial(restore_kernel, half),
        out_shape=[
            jax.ShapeDtypeStruct((count, width), jnp.float32),
            jax.ShapeDtypeStruct((1, count), jnp.float32),
        ],
        in_specs=[VMEM] * (1 + len(back)),
        out_specs=[VMEM, VMEM],
        compiler_params=GRANT,
        name="restore_rows",
    )(chosen, *back[n_gr - 1 :: -1], *back[:n_gr - 1 : -1])
    return (neighbour_sum, density.reshape(count))


def solution(mesh):
    in_specs = (P(("gr", "gc"), None), P(("gr", "gc")))
    out_specs = (P(("gr", "gc"), None), P(("gr", "gc")))
    return jax.shard_map(
        functools.partial(on_device, mesh.shape["gr"], mesh.shape["gc"]),
        mesh=mesh,
        in_specs=in_specs,
        out_specs=out_specs,
        check_vma=False,
    )
```

```python
import functools
import math

import jax
import jax.numpy as jnp
from jax import lax
from jax.experimental import pallas as pl
from jax.experimental.pallas import tpu as pltpu
from jax.sharding import PartitionSpec as P

beta_scale = 16.0
floor_weight = math.exp(-beta_scale)
BLOCK = 512
LANES = 128
EXTRA = 8
TOP = 14.0
VMEM = pl.BlockSpec(memory_space=pltpu.VMEM)
HBM = pl.BlockSpec(memory_space=pltpu.HBM)
SMEM = pl.BlockSpec(memory_space=pltpu.SMEM)
GRANT = pltpu.CompilerParams(vmem_limit_bytes=40 * 1024 * 1024)


def in_hbm(array):
    return pltpu.with_memory_space_constraint(array, pltpu.HBM)


def diagonal(count):
    first = lax.broadcasted_iota(jnp.int32, (count, count), 0)
    second = lax.broadcasted_iota(jnp.int32, (count, count), 1)
    return first == second


def as_row(column):
    return jnp.sum(
        jnp.where(diagonal(column.shape[0]), column, jnp.zeros_like(column)),
        axis=0,
        keepdims=True,
    )


def as_column(row):
    return jnp.sum(
        jnp.where(diagonal(row.shape[1]), row, jnp.zeros_like(row)),
        axis=1,
        keepdims=True,
    )


def placement(own, ids, groups):
    count = ids.shape[1]
    first = lax.broadcasted_iota(jnp.int32, (count, count), 0)
    second = lax.broadcasted_iota(jnp.int32, (count, count), 1)
    earlier = jnp.where((as_column(ids) == ids) & (first < second), 1, 0)
    rank = jnp.sum(earlier, axis=0, keepdims=True)
    slot = (ids ^ own) * (count // groups) + rank
    return jnp.where(first == slot, 1.0, 0.0)


def sort_kernel(own_ref, ids_hbm, rows_hbm, *refs):
    chosen_ref, *out_refs = refs[:-4]
    ids_ref, rows_ref, ids_sem, rows_sem = refs[-4:]
    groups = len(out_refs)
    ids_copy = pltpu.make_async_copy(ids_hbm, ids_ref, ids_sem)
    rows_copy = pltpu.make_async_copy(rows_hbm, rows_ref, rows_sem)
    ids_copy.start()
    rows_copy.start()
    ids_copy.wait()
    chosen = placement(own_ref[0], ids_ref[...], groups).astype(jnp.bfloat16)
    chosen_ref[...] = chosen
    rows_copy.wait()
    ordered = jnp.dot(chosen, rows_ref[...], preferred_element_type=jnp.float32)
    ordered = ordered.astype(jnp.bfloat16)
    size = ordered.shape[0] // groups
    for k, out_ref in enumerate(out_refs):
        out_ref[...] = ordered[k * size : (k + 1) * size, :]


def folded_squares(rows):
    total = 0.0
    for lane in range(0, rows.shape[1], LANES):
        wide = rows[:, lane : lane + LANES].astype(jnp.float32)
        total += wide * wide
    return total


def add_columns(rows, scale, col_refs, total, dens):
    for col_ref in col_refs:
        for start in range(0, col_ref.shape[0], BLOCK):
            cols = col_ref[start : min(start + BLOCK, col_ref.shape[0]), :]
            squares = jnp.sum(folded_squares(cols).T, axis=0, keepdims=True)
            col_inv = lax.rsqrt(squares + 1e-06)
            raw = lax.dot_general(
                rows, cols, (((1,), (1,)), ((), ())), preferred_element_type=jnp.float32
            )
            weight = jnp.exp2(raw * scale * col_inv)
            for lane in range(0, cols.shape[0], LANES):
                dens += weight[:, lane : lane + LANES]
            coef = (weight * (col_inv * floor_weight)).astype(jnp.bfloat16)
            total += jnp.dot(coef, cols, preferred_element_type=jnp.float32)
    return total, dens


def early_kernel(rows_ref, *refs):
    col_refs, (scale_ref, total_ref, dens_ref) = refs[:-3], refs[-3:]
    squares = jnp.sum(folded_squares(rows_ref[...]), axis=1, keepdims=True)
    scale = lax.rsqrt(squares + 1e-06) * (beta_scale * math.log2(math.e))
    scale_ref[...] = jnp.broadcast_to(scale, scale_ref.shape)
    total = jnp.zeros(total_ref.shape, jnp.float32)
    dens = jnp.zeros(dens_ref.shape, jnp.float32)
    total, dens = add_columns(rows_ref[...], scale, col_refs, total, dens)
    total_ref[...] = total
    dens_ref[...] = dens


def middle_kernel(rows_ref, scale_ref, total_ref, dens_ref, *refs):
    col_refs, (total_out, dens_out) = refs[:-2], refs[-2:]
    total, dens = add_columns(
        rows_ref[...], scale_ref[:, 0:1], col_refs, total_ref[...], dens_ref[...]
    )
    total_out[...] = total
    dens_out[...] = dens


def exponent(value):
    return jnp.floor(jnp.log2(jnp.maximum(value, 1e-30)))


def last_kernel(half, rows_ref, scale_ref, total_ref, dens_ref, cols_ref, *out_refs):
    groups = len(out_refs) - half
    size = out_refs[half].shape[0]
    total, dens = add_columns(
        rows_ref[...], scale_ref[:, 0:1], [cols_ref], total_ref[...], dens_ref[...]
    )
    dens = jnp.sum(dens, axis=1, keepdims=True) * floor_weight
    power = exponent(jnp.max(jnp.abs(total), axis=1, keepdims=True))
    total = total * jnp.exp2(TOP - power)
    dens_power = exponent(dens)
    part = dens * jnp.exp2(-dens_power)
    aside = [power, dens_power]
    for k in range(3):
        piece = part.astype(jnp.bfloat16).astype(jnp.float32)
        aside.append(piece * 2.0 ** (8 * k))
        part = part - piece
    lanes = lax.broadcasted_iota(jnp.int32, (total.shape[0], LANES), 1)
    table = jnp.zeros(lanes.shape, jnp.float32)
    for line, column in enumerate(aside):
        table = jnp.where(lanes == line, column, table)
    for k in range(groups):
        rows = slice(k * size, (k + 1) * size)
        out_refs[k][:size, :] = total[rows, :]
        if k < half:
            aside_ref, top = out_refs[k], size
        else:
            aside_ref, top = out_refs[half + k], 0
        aside_ref[top:, :] = jnp.zeros((EXTRA, aside_ref.shape[1]), jnp.float32)
        aside_ref[top:, :size] = table[rows, :].T[:EXTRA, :]


def restore_kernel(groups, chosen_ref, *refs):
    high_refs, low_refs, aside_refs, (total_ref, dens_ref) = (
        refs[:groups],
        refs[groups : 2 * groups],
        refs[2 * groups : -2],
        refs[-2:],
    )
    size = high_refs[0].shape[0]
    scales, dens = [], []
    for aside_ref in aside_refs[::-1]:
        table = aside_ref[...].T[:size, :]
        scales.append(jnp.exp2(table[:, 0:1] - TOP))
        part = table[:, 2:3] + table[:, 3:4] * 2.0**-8 + table[:, 4:5] * 2.0**-16
        dens.append(part * jnp.exp2(table[:, 1:2]))
    chosen = chosen_ref[...].astype(jnp.float32)
    dens_ref[...] = jnp.sum(
        chosen * jnp.concatenate(dens, axis=0), axis=0, keepdims=True
    )
    scaled = (chosen * jnp.concatenate(scales, axis=0)).astype(jnp.bfloat16)
    back = 0.0
    for part_refs in (high_refs, low_refs):
        parts = jnp.concatenate([ref[...] for ref in part_refs[::-1]], axis=0)
        back += lax.dot_general(
            scaled, parts, (((0,), (0,)), ((), ())), preferred_element_type=jnp.float32
        )
    total_ref[...] = back


def on_device(n_gr, n_gc, embeddings, cluster_ids):
    count, width = embeddings.shape
    size = count // n_gr
    own = lax.axis_index("gr").astype(jnp.int32).reshape(1)
    ids = cluster_ids.reshape(1, count)

    chosen, *parts = pl.pallas_call(
        sort_kernel,
        out_shape=[jax.ShapeDtypeStruct((count, count), jnp.bfloat16)]
        + [jax.ShapeDtypeStruct((size, width), jnp.bfloat16)] * n_gr,
        in_specs=[SMEM, HBM, HBM],
        out_specs=[VMEM] * (1 + n_gr),
        scratch_shapes=[
            pltpu.VMEM((1, count), jnp.int32),
            pltpu.VMEM((count, width), embeddings.dtype),
            pltpu.SemaphoreType.DMA,
            pltpu.SemaphoreType.DMA,
        ],
        compiler_params=GRANT,
        name="sort_rows",
    )(own, in_hbm(ids), in_hbm(embeddings))

    def along_gr(part, bits):
        return lax.ppermute(part, "gr", [(i, i ^ bits) for i in range(n_gr)])

    def along_gc(block, bits):
        return lax.ppermute(block, "gc", [(i, i ^ bits) for i in range(n_gc)])

    def other_core(block):
        return along_gc(block, 1)

    def cost(*blocks):
        pairs = count * sum(block.shape[0] for block in blocks)
        return pl.CostEstimate(
            flops=4 * pairs * width,
            bytes_accessed=0,
            transcendentals=pairs,
        )

    held = [parts[0]] + [along_gr(parts[k], k) for k in range(1, n_gr)]
    half = n_gr // 2
    sides = [k for k in range(2, n_gc, 2) if not k & (k - 1)]
    corners = [k for k in range(2, n_gc, 2) if k & (k - 1)]

    def to_side(block, step):
        pairs = [(i, i ^ sides[(step + i % 2) % len(sides)]) for i in range(n_gc)]
        return lax.ppermute(block, "gc", pairs)

    chunks = []
    for pieces in (held[:half], held[half:]):
        block = jnp.concatenate(pieces, axis=0)
        near = [block] + [along_gc(block, k) for k in corners]
        near += [to_side(block, step) for step in range(len(sides))]
        chunks.append(jnp.concatenate(near, axis=0))
    rows = jnp.concatenate(held, axis=0)
    chunks[0], rows = lax.optimization_barrier((chunks[0], rows))
    early = [chunks[0], other_core(chunks[0]), chunks[1]]

    scale, total, dens = pl.pallas_call(
        early_kernel,
        out_shape=[
            jax.ShapeDtypeStruct((count, LANES), jnp.float32),
            jax.ShapeDtypeStruct((count, width), jnp.float32),
            jax.ShapeDtypeStruct((count, LANES), jnp.float32),
        ],
        in_specs=[VMEM] * (1 + len(early)),
        out_specs=[VMEM] * 3,
        compiler_params=GRANT,
        cost_estimate=cost(*early),
        name="early_sums",
    )(rows, *early)
    late = other_core(chunks[1])
    sums = pl.pallas_call(
        functools.partial(last_kernel, half),
        out_shape=[jax.ShapeDtypeStruct((size + EXTRA, width), jnp.float32)] * half
        + [jax.ShapeDtypeStruct((size, width), jnp.float32)] * (n_gr - half)
        + [jax.ShapeDtypeStruct((EXTRA, LANES), jnp.float32)] * (n_gr - half),
        in_specs=[VMEM] * 5,
        out_specs=[VMEM] * (2 * n_gr - half),
        compiler_params=GRANT,
        cost_estimate=cost(late),
        name="last_sums",
    )(rows, scale, total, dens, late)

    sent = [part.astype(jnp.float16) for part in sums[:n_gr]]
    back = [sent[0]] + [along_gr(sent[k], k) for k in range(1, n_gr)]
    beside = [part[size:, :LANES].astype(jnp.float32) for part in back[:half]]
    beside += [along_gr(sums[half + k], k) for k in range(half, n_gr)]
    back = [part[:size].astype(jnp.float32) for part in back]
    high = [lax.reduce_precision(part, 8, 7) for part in back]
    low = [(part - top).astype(jnp.bfloat16) for part, top in zip(back, high)]
    high = [part.astype(jnp.bfloat16) for part in high]
    neighbour_sum, density = pl.pallas_call(
        functools.partial(restore_kernel, n_gr),
        out_shape=[
            jax.ShapeDtypeStruct((count, width), jnp.float32),
            jax.ShapeDtypeStruct((1, count), jnp.float32),
        ],
        in_specs=[VMEM] * (1 + 3 * n_gr),
        out_specs=[VMEM, VMEM],
        compiler_params=GRANT,
        name="restore_rows",
    )(chosen, *high[::-1], *low[::-1], *beside[::-1])
    return (neighbour_sum, density.reshape(count))


def solution(mesh):
    in_specs = (P(("gr", "gc"), None), P(("gr", "gc")))
    out_specs = (P(("gr", "gc"), None), P(("gr", "gc")))
    return jax.shard_map(
        functools.partial(on_device, mesh.shape["gr"], mesh.shape["gc"]),
        mesh=mesh,
        in_specs=in_specs,
        out_specs=out_specs,
        check_vma=False,
    )
```

```python
import functools
import math

import jax
import jax.numpy as jnp
from jax import lax
from jax.experimental import pallas as pl
from jax.experimental.pallas import tpu as pltpu
from jax.sharding import PartitionSpec as P

beta_scale = 16.0
floor_weight = math.exp(-beta_scale)
BLOCK = 512
LANES = 128
EXTRA = 8
TOP = 14.0
VMEM = pl.BlockSpec(memory_space=pltpu.VMEM)
HBM = pl.BlockSpec(memory_space=pltpu.HBM)
SMEM = pl.BlockSpec(memory_space=pltpu.SMEM)
GRANT = pltpu.CompilerParams(vmem_limit_bytes=40 * 1024 * 1024)


def in_hbm(array):
    return pltpu.with_memory_space_constraint(array, pltpu.HBM)


def diagonal(count):
    first = lax.broadcasted_iota(jnp.int32, (count, count), 0)
    second = lax.broadcasted_iota(jnp.int32, (count, count), 1)
    return first == second


def as_row(column):
    return jnp.sum(
        jnp.where(diagonal(column.shape[0]), column, jnp.zeros_like(column)),
        axis=0,
        keepdims=True,
    )


def as_column(row):
    return jnp.sum(
        jnp.where(diagonal(row.shape[1]), row, jnp.zeros_like(row)),
        axis=1,
        keepdims=True,
    )


def placement(own, ids, groups):
    count = ids.shape[1]
    first = lax.broadcasted_iota(jnp.int32, (count, count), 0)
    second = lax.broadcasted_iota(jnp.int32, (count, count), 1)
    earlier = jnp.where((as_column(ids) == ids) & (first < second), 1, 0)
    rank = jnp.sum(earlier, axis=0, keepdims=True)
    slot = (ids ^ own) * (count // groups) + rank
    return jnp.where(first == slot, 1.0, 0.0)


def sort_kernel(own_ref, ids_hbm, rows_hbm, *refs):
    chosen_ref, *out_refs = refs[:-4]
    ids_ref, rows_ref, ids_sem, rows_sem = refs[-4:]
    groups = len(out_refs)
    ids_copy = pltpu.make_async_copy(ids_hbm, ids_ref, ids_sem)
    rows_copy = pltpu.make_async_copy(rows_hbm, rows_ref, rows_sem)
    ids_copy.start()
    rows_copy.start()
    ids_copy.wait()
    chosen = placement(own_ref[0], ids_ref[...], groups).astype(jnp.bfloat16)
    chosen_ref[...] = chosen
    rows_copy.wait()
    ordered = jnp.dot(chosen, rows_ref[...], preferred_element_type=jnp.float32)
    ordered = ordered.astype(jnp.bfloat16)
    size = ordered.shape[0] // groups
    for k, out_ref in enumerate(out_refs):
        out_ref[...] = ordered[k * size : (k + 1) * size, :]


def folded_squares(rows):
    total = 0.0
    for lane in range(0, rows.shape[1], LANES):
        wide = rows[:, lane : lane + LANES].astype(jnp.float32)
        total += wide * wide
    return total


def add_columns(rows, scale, col_refs, total, dens):
    for col_ref in col_refs:
        for start in range(0, col_ref.shape[0], BLOCK):
            cols = col_ref[start : min(start + BLOCK, col_ref.shape[0]), :]
            squares = jnp.sum(folded_squares(cols).T, axis=0, keepdims=True)
            col_inv = lax.rsqrt(squares + 1e-06)
            raw = lax.dot_general(
                rows, cols, (((1,), (1,)), ((), ())), preferred_element_type=jnp.float32
            )
            weight = jnp.exp2(raw * scale * col_inv)
            for lane in range(0, cols.shape[0], LANES):
                dens += weight[:, lane : lane + LANES]
            coef = (weight * (col_inv * floor_weight)).astype(jnp.bfloat16)
            total += jnp.dot(coef, cols, preferred_element_type=jnp.float32)
    return total, dens


def early_kernel(rows_ref, *refs):
    col_refs, (scale_ref, total_ref, dens_ref) = refs[:-3], refs[-3:]
    squares = jnp.sum(folded_squares(rows_ref[...]), axis=1, keepdims=True)
    scale = lax.rsqrt(squares + 1e-06) * (beta_scale * math.log2(math.e))
    scale_ref[...] = jnp.broadcast_to(scale, scale_ref.shape)
    total = jnp.zeros(total_ref.shape, jnp.float32)
    dens = jnp.zeros(dens_ref.shape, jnp.float32)
    total, dens = add_columns(rows_ref[...], scale, col_refs, total, dens)
    total_ref[...] = total
    dens_ref[...] = dens


def middle_kernel(rows_ref, scale_ref, total_ref, dens_ref, *refs):
    col_refs, (total_out, dens_out) = refs[:-2], refs[-2:]
    total, dens = add_columns(
        rows_ref[...], scale_ref[:, 0:1], col_refs, total_ref[...], dens_ref[...]
    )
    total_out[...] = total
    dens_out[...] = dens


def exponent(value):
    return jnp.floor(jnp.log2(jnp.maximum(value, 1e-30)))


def last_kernel(half, rows_ref, scale_ref, total_ref, dens_ref, cols_ref, *out_refs):
    groups = len(out_refs) - half
    size = out_refs[half].shape[0]
    total, dens = add_columns(
        rows_ref[...], scale_ref[:, 0:1], [cols_ref], total_ref[...], dens_ref[...]
    )
    dens = jnp.sum(dens, axis=1, keepdims=True) * floor_weight
    power = exponent(jnp.max(jnp.abs(total), axis=1, keepdims=True))
    total = total * jnp.exp2(TOP - power)
    dens_power = exponent(dens)
    part = dens * jnp.exp2(-dens_power)
    aside = [power, dens_power]
    for k in range(3):
        piece = part.astype(jnp.bfloat16).astype(jnp.float32)
        aside.append(piece * 2.0 ** (8 * k))
        part = part - piece
    for k in range(groups):
        rows = slice(k * size, (k + 1) * size)
        out_refs[k][:size, :] = total[rows, :]
        if k < half:
            aside_ref, top = out_refs[k], size
            aside_ref[size:, :] = jnp.zeros((EXTRA, total.shape[1]), jnp.float32)
        else:
            aside_ref, top = out_refs[half + k], 0
            aside_ref[...] = jnp.zeros(aside_ref.shape, jnp.float32)
        for line, column in enumerate(aside):
            aside_ref[top + line : top + line + 1, :size] = as_row(column[rows, :])


def restore_kernel(half, chosen_ref, *refs):
    refs, (total_ref, dens_ref) = refs[:-2], refs[-2:]
    groups = len(refs) - half
    part_refs = refs[:groups][::-1][:half] + refs[: groups - half] + refs[groups:]
    size = part_refs[half].shape[0]
    chosen = chosen_ref[...]
    sums, dens = [], []
    for k in range(groups):
        aside_ref, top = (part_refs[k], size) if k < half else (part_refs[half + k], 0)
        power, dens_power, *pieces = [
            as_column(aside_ref[top + line : top + line + 1, :size])
            for line in range(5)
        ]
        sums.append(part_refs[k][:size, :] * jnp.exp2(power - TOP))
        part = sum(piece * 2.0 ** (-8 * j) for j, piece in enumerate(pieces))
        dens.append(part * jnp.exp2(dens_power))
    dens_ref[...] = jnp.sum(
        chosen.astype(jnp.float32) * jnp.concatenate(dens, axis=0), axis=0, keepdims=True
    )
    rest = jnp.concatenate(sums, axis=0)
    back = jnp.zeros(rest.shape, jnp.float32)
    for _ in range(2):
        piece = rest.astype(jnp.bfloat16)
        rest = rest - piece.astype(jnp.float32)
        back += lax.dot_general(
            chosen, piece, (((0,), (0,)), ((), ())), preferred_element_type=jnp.float32
        )
    total_ref[...] = back


def on_device(n_gr, n_gc, embeddings, cluster_ids):
    count, width = embeddings.shape
    size = count // n_gr
    own = lax.axis_index("gr").astype(jnp.int32).reshape(1)
    ids = cluster_ids.reshape(1, count)

    chosen, *parts = pl.pallas_call(
        sort_kernel,
        out_shape=[jax.ShapeDtypeStruct((count, count), jnp.bfloat16)]
        + [jax.ShapeDtypeStruct((size, width), jnp.bfloat16)] * n_gr,
        in_specs=[SMEM, HBM, HBM],
        out_specs=[VMEM] * (1 + n_gr),
        scratch_shapes=[
            pltpu.VMEM((1, count), jnp.int32),
            pltpu.VMEM((count, width), embeddings.dtype),
            pltpu.SemaphoreType.DMA,
            pltpu.SemaphoreType.DMA,
        ],
        compiler_params=GRANT,
        name="sort_rows",
    )(own, in_hbm(ids), in_hbm(embeddings))

    def along_gr(part, bits):
        return lax.ppermute(part, "gr", [(i, i ^ bits) for i in range(n_gr)])

    def along_gc(block, bits):
        return lax.ppermute(block, "gc", [(i, i ^ bits) for i in range(n_gc)])

    def other_core(block):
        return along_gc(block, 1)

    def cost(*blocks):
        pairs = count * sum(block.shape[0] for block in blocks)
        return pl.CostEstimate(
            flops=4 * pairs * width,
            bytes_accessed=0,
            transcendentals=pairs,
        )

    held = [parts[0]] + [along_gr(parts[k], k) for k in range(1, n_gr)]
    half = n_gr // 2
    sides = [k for k in range(2, n_gc, 2) if not k & (k - 1)]
    corners = [k for k in range(2, n_gc, 2) if k & (k - 1)]

    def to_side(block, step):
        pairs = [(i, i ^ sides[(step + i % 2) % len(sides)]) for i in range(n_gc)]
        return lax.ppermute(block, "gc", pairs)

    chunks = []
    for pieces in (held[:half], held[half:]):
        block = jnp.concatenate(pieces, axis=0)
        near = [block] + [along_gc(block, k) for k in corners]
        near += [to_side(block, step) for step in range(len(sides))]
        chunks.append(jnp.concatenate(near, axis=0))
    rows = jnp.concatenate(held, axis=0)
    chunks[0], rows = lax.optimization_barrier((chunks[0], rows))
    early = [chunks[0], other_core(chunks[0]), chunks[1]]

    scale, total, dens = pl.pallas_call(
        early_kernel,
        out_shape=[
            jax.ShapeDtypeStruct((count, LANES), jnp.float32),
            jax.ShapeDtypeStruct((count, width), jnp.float32),
            jax.ShapeDtypeStruct((count, LANES), jnp.float32),
        ],
        in_specs=[VMEM] * (1 + len(early)),
        out_specs=[VMEM] * 3,
        compiler_params=GRANT,
        cost_estimate=cost(*early),
        name="early_sums",
    )(rows, *early)
    late = other_core(chunks[1])
    sums = pl.pallas_call(
        functools.partial(last_kernel, half),
        out_shape=[jax.ShapeDtypeStruct((size + EXTRA, width), jnp.float32)] * half
        + [jax.ShapeDtypeStruct((size, width), jnp.float32)] * (n_gr - half)
        + [jax.ShapeDtypeStruct((EXTRA, LANES), jnp.float32)] * (n_gr - half),
        in_specs=[VMEM] * 5,
        out_specs=[VMEM] * (2 * n_gr - half),
        compiler_params=GRANT,
        cost_estimate=cost(late),
        name="last_sums",
    )(rows, scale, total, dens, late)

    sent = [part.astype(jnp.float16) for part in sums[:n_gr]]
    back = [sent[0]] + [along_gr(sent[k], k) for k in range(1, n_gr)]
    back = [part.astype(jnp.float32) for part in back]
    back += [along_gr(sums[half + k], k) for k in range(half, n_gr)]
    order = [*range(half, n_gr), *range(half)[::-1]]
    neighbour_sum, density = pl.pallas_call(
        functools.partial(restore_kernel, half),
        out_shape=[
            jax.ShapeDtypeStruct((count, width), jnp.float32),
            jax.ShapeDtypeStruct((1, count), jnp.float32),
        ],
        in_specs=[VMEM] * (1 + len(back)),
        out_specs=[VMEM, VMEM],
        compiler_params=GRANT,
        name="restore_rows",
    )(chosen, *[back[k] for k in order], *back[n_gr:])
    return (neighbour_sum, density.reshape(count))


def solution(mesh):
    in_specs = (P(("gr", "gc"), None), P(("gr", "gc")))
    out_specs = (P(("gr", "gc"), None), P(("gr", "gc")))
    return jax.shard_map(
        functools.partial(on_device, mesh.shape["gr"], mesh.shape["gc"]),
        mesh=mesh,
        in_specs=in_specs,
        out_specs=out_specs,
        check_vma=False,
    )
```

```python
import functools
import math

import jax
import jax.numpy as jnp
from jax import lax
from jax.experimental import pallas as pl
from jax.experimental.pallas import tpu as pltpu
from jax.sharding import PartitionSpec as P

beta_scale = 16.0
floor_weight = math.exp(-beta_scale)
BLOCK = 512
LANES = 128
EXTRA = 8
TOP = 14.0
VMEM = pl.BlockSpec(memory_space=pltpu.VMEM)
HBM = pl.BlockSpec(memory_space=pltpu.HBM)
SMEM = pl.BlockSpec(memory_space=pltpu.SMEM)
GRANT = pltpu.CompilerParams(vmem_limit_bytes=40 * 1024 * 1024)


def in_hbm(array):
    return pltpu.with_memory_space_constraint(array, pltpu.HBM)


def diagonal(count):
    first = lax.broadcasted_iota(jnp.int32, (count, count), 0)
    second = lax.broadcasted_iota(jnp.int32, (count, count), 1)
    return first == second


def as_row(column):
    return jnp.sum(
        jnp.where(diagonal(column.shape[0]), column, jnp.zeros_like(column)),
        axis=0,
        keepdims=True,
    )


def as_column(row):
    return jnp.sum(
        jnp.where(diagonal(row.shape[1]), row, jnp.zeros_like(row)),
        axis=1,
        keepdims=True,
    )


def placement(own, ids, groups):
    count = ids.shape[1]
    first = lax.broadcasted_iota(jnp.int32, (count, count), 0)
    second = lax.broadcasted_iota(jnp.int32, (count, count), 1)
    earlier = jnp.where((as_column(ids) == ids) & (first < second), 1, 0)
    rank = jnp.sum(earlier, axis=0, keepdims=True)
    slot = (ids ^ own) * (count // groups) + rank
    return jnp.where(first == slot, 1.0, 0.0)


def sort_kernel(own_ref, ids_hbm, rows_hbm, *refs):
    chosen_ref, *out_refs = refs[:-4]
    ids_ref, rows_ref, ids_sem, rows_sem = refs[-4:]
    groups = len(out_refs)
    ids_copy = pltpu.make_async_copy(ids_hbm, ids_ref, ids_sem)
    rows_copy = pltpu.make_async_copy(rows_hbm, rows_ref, rows_sem)
    ids_copy.start()
    rows_copy.start()
    ids_copy.wait()
    chosen = placement(own_ref[0], ids_ref[...], groups).astype(jnp.bfloat16)
    chosen_ref[...] = chosen
    rows_copy.wait()
    ordered = jnp.dot(chosen, rows_ref[...], preferred_element_type=jnp.float32)
    ordered = ordered.astype(jnp.bfloat16)
    size = ordered.shape[0] // groups
    for k, out_ref in enumerate(out_refs):
        out_ref[...] = ordered[k * size : (k + 1) * size, :]


def folded_squares(rows):
    total = 0.0
    for lane in range(0, rows.shape[1], LANES):
        wide = rows[:, lane : lane + LANES].astype(jnp.float32)
        total += wide * wide
    return total


def add_columns(rows, scale, col_refs, total, dens):
    for col_ref in col_refs:
        for start in range(0, col_ref.shape[0], BLOCK):
            cols = col_ref[start : min(start + BLOCK, col_ref.shape[0]), :]
            squares = jnp.sum(folded_squares(cols).T, axis=0, keepdims=True)
            col_inv = lax.rsqrt(squares + 1e-06)
            raw = lax.dot_general(
                rows, cols, (((1,), (1,)), ((), ())), preferred_element_type=jnp.float32
            )
            weight = jnp.exp2(raw * scale * col_inv)
            for lane in range(0, cols.shape[0], LANES):
                dens += weight[:, lane : lane + LANES]
            coef = (weight * (col_inv * floor_weight)).astype(jnp.bfloat16)
            total += jnp.dot(coef, cols, preferred_element_type=jnp.float32)
    return total, dens


def early_kernel(rows_ref, *refs):
    col_refs, (scale_ref, total_ref, dens_ref) = refs[:-3], refs[-3:]
    squares = jnp.sum(folded_squares(rows_ref[...]), axis=1, keepdims=True)
    scale = lax.rsqrt(squares + 1e-06) * (beta_scale * math.log2(math.e))
    scale_ref[...] = jnp.broadcast_to(scale, scale_ref.shape)
    total = jnp.zeros(total_ref.shape, jnp.float32)
    dens = jnp.zeros(dens_ref.shape, jnp.float32)
    total, dens = add_columns(rows_ref[...], scale, col_refs, total, dens)
    total_ref[...] = total
    dens_ref[...] = dens


def middle_kernel(rows_ref, scale_ref, total_ref, dens_ref, *refs):
    col_refs, (total_out, dens_out) = refs[:-2], refs[-2:]
    total, dens = add_columns(
        rows_ref[...], scale_ref[:, 0:1], col_refs, total_ref[...], dens_ref[...]
    )
    total_out[...] = total
    dens_out[...] = dens


def exponent(value):
    return jnp.floor(jnp.log2(jnp.maximum(value, 1e-30)))


def last_kernel(half, rows_ref, scale_ref, total_ref, dens_ref, cols_ref, *out_refs):
    groups = len(out_refs) - half
    size = out_refs[half].shape[0]
    total, dens = add_columns(
        rows_ref[...], scale_ref[:, 0:1], [cols_ref], total_ref[...], dens_ref[...]
    )
    dens = jnp.sum(dens, axis=1, keepdims=True) * floor_weight
    power = exponent(jnp.max(jnp.abs(total), axis=1, keepdims=True))
    total = total * jnp.exp2(TOP - power)
    dens_power = exponent(dens)
    part = dens * jnp.exp2(-dens_power)
    aside = [power, dens_power]
    for k in range(3):
        piece = part.astype(jnp.bfloat16).astype(jnp.float32)
        aside.append(piece * 2.0 ** (8 * k))
        part = part - piece
    for k in range(groups):
        rows = slice(k * size, (k + 1) * size)
        out_refs[k][:size, :] = total[rows, :]
        if k < half:
            aside_ref, top = out_refs[k], size
            aside_ref[size:, :] = jnp.zeros((EXTRA, total.shape[1]), jnp.float32)
        else:
            aside_ref, top = out_refs[half + k], 0
            aside_ref[...] = jnp.zeros(aside_ref.shape, jnp.float32)
        for line, column in enumerate(aside):
            aside_ref[top + line : top + line + 1, :size] = as_row(column[rows, :])


def restore_kernel(half, chosen_ref, *refs):
    refs, (total_ref, dens_ref) = refs[:-2], refs[-2:]
    groups = len(refs) - half
    part_refs = refs[groups - 1 :: -1] + refs[: groups - 1 : -1]
    size = part_refs[half].shape[0]
    chosen = chosen_ref[...]
    sums, dens = [], []
    for k in range(groups):
        aside_ref, top = (part_refs[k], size) if k < half else (part_refs[half + k], 0)
        power, dens_power, *pieces = [
            as_column(aside_ref[top + line : top + line + 1, :size])
            for line in range(5)
        ]
        sums.append(part_refs[k][:size, :] * jnp.exp2(power - TOP))
        part = sum(piece * 2.0 ** (-8 * j) for j, piece in enumerate(pieces))
        dens.append(part * jnp.exp2(dens_power))
    dens_ref[...] = jnp.sum(
        chosen.astype(jnp.float32) * jnp.concatenate(dens, axis=0), axis=0, keepdims=True
    )
    rest = jnp.concatenate(sums, axis=0)
    back = jnp.zeros(rest.shape, jnp.float32)
    for _ in range(2):
        piece = rest.astype(jnp.bfloat16)
        rest = rest - piece.astype(jnp.float32)
        back += lax.dot_general(
            chosen, piece, (((0,), (0,)), ((), ())), preferred_element_type=jnp.float32
        )
    total_ref[...] = back


def on_device(n_gr, n_gc, embeddings, cluster_ids):
    count, width = embeddings.shape
    size = count // n_gr
    own = lax.axis_index("gr").astype(jnp.int32).reshape(1)
    ids = cluster_ids.reshape(1, count)

    chosen, *parts = pl.pallas_call(
        sort_kernel,
        out_shape=[jax.ShapeDtypeStruct((count, count), jnp.bfloat16)]
        + [jax.ShapeDtypeStruct((size, width), jnp.bfloat16)] * n_gr,
        in_specs=[SMEM, HBM, HBM],
        out_specs=[VMEM] * (1 + n_gr),
        scratch_shapes=[
            pltpu.VMEM((1, count), jnp.int32),
            pltpu.VMEM((count, width), embeddings.dtype),
            pltpu.SemaphoreType.DMA,
            pltpu.SemaphoreType.DMA,
        ],
        compiler_params=GRANT,
        name="sort_rows",
    )(own, in_hbm(ids), in_hbm(embeddings))

    def along_gr(part, bits):
        return lax.ppermute(part, "gr", [(i, i ^ bits) for i in range(n_gr)])

    def along_gc(block, bits):
        return lax.ppermute(block, "gc", [(i, i ^ bits) for i in range(n_gc)])

    def other_core(block):
        return along_gc(block, 1)

    def cost(*blocks):
        pairs = count * sum(block.shape[0] for block in blocks)
        return pl.CostEstimate(
            flops=4 * pairs * width,
            bytes_accessed=0,
            transcendentals=pairs,
        )

    held = [parts[0]] + [along_gr(parts[k], k) for k in range(1, n_gr)]
    half = n_gr // 2
    sides = [k for k in range(2, n_gc, 2) if not k & (k - 1)]
    corners = [k for k in range(2, n_gc, 2) if k & (k - 1)]

    def to_side(block, step):
        pairs = [(i, i ^ sides[(step + i % 2) % len(sides)]) for i in range(n_gc)]
        return lax.ppermute(block, "gc", pairs)

    early = jnp.concatenate(held[:half], axis=0)
    late = jnp.concatenate(held[half:], axis=0)
    rest = jnp.concatenate(held[1:half], axis=0)
    filler = [along_gc(held[0], k) for k in corners]
    filler, rest = lax.optimization_barrier((filler, rest))
    rest_corners = [along_gc(rest, k) for k in corners]
    early_sides = [to_side(early, step) for step in range(len(sides))]
    late_near = [along_gc(late, k) for k in corners] + [to_side(late, step) for step in range(1)]
    rest_corners, late = lax.optimization_barrier((rest_corners, late))
    late_near += [to_side(late, step) for step in range(1, len(sides))]
    rows = jnp.concatenate(held, axis=0)
    chunks = [jnp.concatenate([early] + early_sides + filler + rest_corners, axis=0), jnp.concatenate(late_near + [late], axis=0)]
    early = [chunks[0], other_core(chunks[0]), chunks[1]]

    scale, total, dens = pl.pallas_call(
        early_kernel,
        out_shape=[
            jax.ShapeDtypeStruct((count, LANES), jnp.float32),
            jax.ShapeDtypeStruct((count, width), jnp.float32),
            jax.ShapeDtypeStruct((count, LANES), jnp.float32),
        ],
        in_specs=[VMEM] * (1 + len(early)),
        out_specs=[VMEM] * 3,
        compiler_params=GRANT,
        cost_estimate=cost(*early),
        name="early_sums",
    )(rows, *early)
    late = other_core(chunks[1])
    sums = pl.pallas_call(
        functools.partial(last_kernel, half),
        out_shape=[jax.ShapeDtypeStruct((size + EXTRA, width), jnp.float32)] * half
        + [jax.ShapeDtypeStruct((size, width), jnp.float32)] * (n_gr - half)
        + [jax.ShapeDtypeStruct((EXTRA, LANES), jnp.float32)] * (n_gr - half),
        in_specs=[VMEM] * 5,
        out_specs=[VMEM] * (2 * n_gr - half),
        compiler_params=GRANT,
        cost_estimate=cost(late),
        name="last_sums",
    )(rows, scale, total, dens, late)

    sent = [part.astype(jnp.float16) for part in sums[:n_gr]]
    back = [sent[0]] + [along_gr(sent[k], k) for k in range(1, n_gr)]
    back = [part.astype(jnp.float32) for part in back]
    back += [along_gr(sums[half + k], k) for k in range(half, n_gr)]
    neighbour_sum, density = pl.pallas_call(
        functools.partial(restore_kernel, half),
        out_shape=[
            jax.ShapeDtypeStruct((count, width), jnp.float32),
            jax.ShapeDtypeStruct((1, count), jnp.float32),
        ],
        in_specs=[VMEM] * (1 + len(back)),
        out_specs=[VMEM, VMEM],
        compiler_params=GRANT,
        name="restore_rows",
    )(chosen, *back[n_gr - 1 :: -1], *back[:n_gr - 1 : -1])
    return (neighbour_sum, density.reshape(count))


def solution(mesh):
    in_specs = (P(("gr", "gc"), None), P(("gr", "gc")))
    out_specs = (P(("gr", "gc"), None), P(("gr", "gc")))
    return jax.shard_map(
        functools.partial(on_device, mesh.shape["gr"], mesh.shape["gc"]),
        mesh=mesh,
        in_specs=in_specs,
        out_specs=out_specs,
        check_vma=False,
    )
```

```python
import functools
import math

import jax
import jax.numpy as jnp
from jax import lax
from jax.experimental import pallas as pl
from jax.experimental.pallas import tpu as pltpu
from jax.sharding import PartitionSpec as P

beta_scale = 16.0
floor_weight = math.exp(-beta_scale)
BLOCK = 512
LANES = 128
EXTRA = 8
TOP = 14.0
VMEM = pl.BlockSpec(memory_space=pltpu.VMEM)
HBM = pl.BlockSpec(memory_space=pltpu.HBM)
SMEM = pl.BlockSpec(memory_space=pltpu.SMEM)
GRANT = pltpu.CompilerParams(vmem_limit_bytes=40 * 1024 * 1024)


def in_hbm(array):
    return pltpu.with_memory_space_constraint(array, pltpu.HBM)


def diagonal(count):
    first = lax.broadcasted_iota(jnp.int32, (count, count), 0)
    second = lax.broadcasted_iota(jnp.int32, (count, count), 1)
    return first == second


def as_row(column):
    return jnp.sum(
        jnp.where(diagonal(column.shape[0]), column, jnp.zeros_like(column)),
        axis=0,
        keepdims=True,
    )


def as_column(row):
    return jnp.sum(
        jnp.where(diagonal(row.shape[1]), row, jnp.zeros_like(row)),
        axis=1,
        keepdims=True,
    )


def placement(own, ids, groups):
    count = ids.shape[1]
    first = lax.broadcasted_iota(jnp.int32, (count, count), 0)
    second = lax.broadcasted_iota(jnp.int32, (count, count), 1)
    earlier = jnp.where((as_column(ids) == ids) & (first < second), 1, 0)
    rank = jnp.sum(earlier, axis=0, keepdims=True)
    slot = (ids ^ own) * (count // groups) + rank
    return jnp.where(first == slot, 1.0, 0.0)


def sort_kernel(own_ref, ids_hbm, rows_hbm, *refs):
    chosen_ref, *out_refs = refs[:-4]
    ids_ref, rows_ref, ids_sem, rows_sem = refs[-4:]
    groups = len(out_refs)
    ids_copy = pltpu.make_async_copy(ids_hbm, ids_ref, ids_sem)
    rows_copy = pltpu.make_async_copy(rows_hbm, rows_ref, rows_sem)
    ids_copy.start()
    rows_copy.start()
    ids_copy.wait()
    chosen = placement(own_ref[0], ids_ref[...], groups).astype(jnp.bfloat16)
    size = chosen.shape[0] // groups
    for k in range(groups):
        chosen_ref[(groups - 1 - k) * size : (groups - k) * size, :] = chosen[
            k * size : (k + 1) * size, :
        ]
    rows_copy.wait()
    ordered = jnp.dot(chosen, rows_ref[...], preferred_element_type=jnp.float32)
    ordered = ordered.astype(jnp.bfloat16)
    size = ordered.shape[0] // groups
    for k, out_ref in enumerate(out_refs):
        out_ref[...] = ordered[k * size : (k + 1) * size, :]


def folded_squares(rows):
    total = 0.0
    for lane in range(0, rows.shape[1], LANES):
        wide = rows[:, lane : lane + LANES].astype(jnp.float32)
        total += wide * wide
    return total


def add_columns(rows, scale, col_refs, total, dens):
    for col_ref in col_refs:
        for start in range(0, col_ref.shape[0], BLOCK):
            cols = col_ref[start : min(start + BLOCK, col_ref.shape[0]), :]
            squares = jnp.sum(folded_squares(cols).T, axis=0, keepdims=True)
            col_inv = lax.rsqrt(squares + 1e-06)
            raw = lax.dot_general(
                rows, cols, (((1,), (1,)), ((), ())), preferred_element_type=jnp.float32
            )
            weight = jnp.exp2(raw * scale * col_inv)
            for lane in range(0, cols.shape[0], LANES):
                dens += weight[:, lane : lane + LANES]
            coef = (weight * (col_inv * floor_weight)).astype(jnp.bfloat16)
            total += jnp.dot(coef, cols, preferred_element_type=jnp.float32)
    return total, dens


def early_kernel(rows_ref, *refs):
    col_refs, (scale_ref, total_ref, dens_ref) = refs[:-3], refs[-3:]
    squares = jnp.sum(folded_squares(rows_ref[...]), axis=1, keepdims=True)
    scale = lax.rsqrt(squares + 1e-06) * (beta_scale * math.log2(math.e))
    scale_ref[...] = jnp.broadcast_to(scale, scale_ref.shape)
    total = jnp.zeros(total_ref.shape, jnp.float32)
    dens = jnp.zeros(dens_ref.shape, jnp.float32)
    total, dens = add_columns(rows_ref[...], scale, col_refs, total, dens)
    total_ref[...] = total
    dens_ref[...] = dens


def middle_kernel(rows_ref, scale_ref, total_ref, dens_ref, *refs):
    col_refs, (total_out, dens_out) = refs[:-2], refs[-2:]
    total, dens = add_columns(
        rows_ref[...], scale_ref[:, 0:1], col_refs, total_ref[...], dens_ref[...]
    )
    total_out[...] = total
    dens_out[...] = dens


def exponent(value):
    return jnp.floor(jnp.log2(jnp.maximum(value, 1e-30)))


def last_kernel(half, rows_ref, scale_ref, total_ref, dens_ref, cols_ref, *out_refs):
    groups = len(out_refs) - half
    size = out_refs[half].shape[0]
    total, dens = add_columns(
        rows_ref[...], scale_ref[:, 0:1], [cols_ref], total_ref[...], dens_ref[...]
    )
    dens = jnp.sum(dens, axis=1, keepdims=True) * floor_weight
    power = exponent(jnp.max(jnp.abs(total), axis=1, keepdims=True))
    total = total * jnp.exp2(TOP - power)
    dens_power = exponent(dens)
    part = dens * jnp.exp2(-dens_power)
    aside = [power, dens_power]
    for k in range(3):
        piece = part.astype(jnp.bfloat16).astype(jnp.float32)
        aside.append(piece * 2.0 ** (8 * k))
        part = part - piece
    for k in range(groups):
        rows = slice(k * size, (k + 1) * size)
        out_refs[k][:size, :] = total[rows, :]
        if k < half:
            aside_ref, top = out_refs[k], size
            aside_ref[size:, :] = jnp.zeros((EXTRA, total.shape[1]), jnp.float32)
        else:
            aside_ref, top = out_refs[half + k], 0
            aside_ref[...] = jnp.zeros(aside_ref.shape, jnp.float32)
        for line, column in enumerate(aside):
            aside_ref[top + line : top + line + 1, :size] = as_row(column[rows, :])


def on_device(n_gr, n_gc, embeddings, cluster_ids):
    count, width = embeddings.shape
    size = count // n_gr
    own = lax.axis_index("gr").astype(jnp.int32).reshape(1)
    ids = cluster_ids.reshape(1, count)

    chosen, *parts = pl.pallas_call(
        sort_kernel,
        out_shape=[jax.ShapeDtypeStruct((count, count), jnp.bfloat16)]
        + [jax.ShapeDtypeStruct((size, width), jnp.bfloat16)] * n_gr,
        in_specs=[SMEM, HBM, HBM],
        out_specs=[VMEM] * (1 + n_gr),
        scratch_shapes=[
            pltpu.VMEM((1, count), jnp.int32),
            pltpu.VMEM((count, width), embeddings.dtype),
            pltpu.SemaphoreType.DMA,
            pltpu.SemaphoreType.DMA,
        ],
        compiler_params=GRANT,
        name="sort_rows",
    )(own, in_hbm(ids), in_hbm(embeddings))

    def along_gr(part, bits):
        return lax.ppermute(part, "gr", [(i, i ^ bits) for i in range(n_gr)])

    def along_gc(block, bits):
        return lax.ppermute(block, "gc", [(i, i ^ bits) for i in range(n_gc)])

    def other_core(block):
        return along_gc(block, 1)

    def cost(*blocks):
        pairs = count * sum(block.shape[0] for block in blocks)
        return pl.CostEstimate(
            flops=4 * pairs * width,
            bytes_accessed=0,
            transcendentals=pairs,
        )

    held = [parts[0]] + [along_gr(parts[k], k) for k in range(1, n_gr)]
    half = n_gr // 2
    sides = [k for k in range(2, n_gc, 2) if not k & (k - 1)]
    corners = [k for k in range(2, n_gc, 2) if k & (k - 1)]

    def to_side(block, step):
        pairs = [(i, i ^ sides[(step + i % 2) % len(sides)]) for i in range(n_gc)]
        return lax.ppermute(block, "gc", pairs)

    chunks = []
    for pieces in (held[:half], held[half:]):
        block = jnp.concatenate(pieces, axis=0)
        near = [block] + [along_gc(block, k) for k in corners]
        near += [to_side(block, step) for step in range(len(sides))]
        chunks.append(jnp.concatenate(near, axis=0))
    rows = jnp.concatenate(held, axis=0)
    chunks[0], rows = lax.optimization_barrier((chunks[0], rows))
    early = [chunks[0], other_core(chunks[0]), chunks[1]]

    scale, total, dens = pl.pallas_call(
        early_kernel,
        out_shape=[
            jax.ShapeDtypeStruct((count, LANES), jnp.float32),
            jax.ShapeDtypeStruct((count, width), jnp.float32),
            jax.ShapeDtypeStruct((count, LANES), jnp.float32),
        ],
        in_specs=[VMEM] * (1 + len(early)),
        out_specs=[VMEM] * 3,
        compiler_params=GRANT,
        cost_estimate=cost(*early),
        name="early_sums",
    )(rows, *early)
    late = other_core(chunks[1])
    sums = pl.pallas_call(
        functools.partial(last_kernel, half),
        out_shape=[jax.ShapeDtypeStruct((size + EXTRA, width), jnp.float32)] * half
        + [jax.ShapeDtypeStruct((size, width), jnp.float32)] * (n_gr - half)
        + [jax.ShapeDtypeStruct((EXTRA, LANES), jnp.float32)] * (n_gr - half),
        in_specs=[VMEM] * 5,
        out_specs=[VMEM] * (2 * n_gr - half),
        compiler_params=GRANT,
        cost_estimate=cost(late),
        name="last_sums",
    )(rows, scale, total, dens, late)

    sent = [part.astype(jnp.float16) for part in sums[:n_gr]]
    back = [sent[0]] + [along_gr(sent[k], k) for k in range(1, n_gr)]
    asides = [along_gr(sums[half + k], k) for k in range(half, n_gr)]
    far, asides = lax.optimization_barrier((back[half:][::-1], asides[::-1]))
    back, asides = back[:half] + far[::-1], asides[::-1]
    wide = [part[:size].astype(jnp.float32) for part in back[::-1]]
    high = [lax.reduce_precision(part, 8, 7) for part in wide]
    low = [(part - top).astype(jnp.bfloat16) for part, top in zip(wide, high)]
    high = [part.astype(jnp.bfloat16) for part in high]
    beside = [part[size:, :size].astype(jnp.float32) for part in back[:half]]
    beside += [part[:, :size] for part in asides]
    beside = jnp.concatenate(beside[::-1], axis=1)
    scale = jnp.exp2(beside[0] - TOP).astype(jnp.bfloat16)
    part = beside[2] + beside[3] * 2.0**-8 + beside[4] * 2.0**-16
    dens = part * jnp.exp2(beside[1])
    density = jnp.sum(chosen.astype(jnp.float32) * dens[:, None], axis=0)
    scaled = chosen * scale[:, None]
    neighbour_sum = lax.dot_general(
        jnp.concatenate([scaled, scaled], axis=0),
        jnp.concatenate(high + low, axis=0),
        (((0,), (0,)), ((), ())),
        preferred_element_type=jnp.float32,
    )
    return (neighbour_sum, density)


def solution(mesh):
    in_specs = (P(("gr", "gc"), None), P(("gr", "gc")))
    out_specs = (P(("gr", "gc"), None), P(("gr", "gc")))
    return jax.shard_map(
        functools.partial(on_device, mesh.shape["gr"], mesh.shape["gc"]),
        mesh=mesh,
        in_specs=in_specs,
        out_specs=out_specs,
        check_vma=False,
    )
```

```python
import functools
import math

import jax
import jax.numpy as jnp
from jax import lax
from jax.experimental import pallas as pl
from jax.experimental.pallas import tpu as pltpu
from jax.sharding import PartitionSpec as P

beta_scale = 16.0
floor_weight = math.exp(-beta_scale)
BLOCK = 512
LANES = 128
EXTRA = 8
TOP = 14.0
VMEM = pl.BlockSpec(memory_space=pltpu.VMEM)
HBM = pl.BlockSpec(memory_space=pltpu.HBM)
SMEM = pl.BlockSpec(memory_space=pltpu.SMEM)
GRANT = pltpu.CompilerParams(vmem_limit_bytes=40 * 1024 * 1024)


def in_hbm(array):
    return pltpu.with_memory_space_constraint(array, pltpu.HBM)


def diagonal(count):
    first = lax.broadcasted_iota(jnp.int32, (count, count), 0)
    second = lax.broadcasted_iota(jnp.int32, (count, count), 1)
    return first == second


def as_row(column):
    return jnp.sum(
        jnp.where(diagonal(column.shape[0]), column, jnp.zeros_like(column)),
        axis=0,
        keepdims=True,
    )


def as_column(row):
    return jnp.sum(
        jnp.where(diagonal(row.shape[1]), row, jnp.zeros_like(row)),
        axis=1,
        keepdims=True,
    )


def placement(own, ids, groups):
    count = ids.shape[1]
    first = lax.broadcasted_iota(jnp.int32, (count, count), 0)
    second = lax.broadcasted_iota(jnp.int32, (count, count), 1)
    earlier = jnp.where((as_column(ids) == ids) & (first < second), 1, 0)
    rank = jnp.sum(earlier, axis=0, keepdims=True)
    slot = (ids ^ own) * (count // groups) + rank
    return jnp.where(first == slot, 1.0, 0.0)


def sort_kernel(own_ref, ids_hbm, rows_hbm, *refs):
    chosen_ref, *out_refs = refs[:-4]
    ids_ref, rows_ref, ids_sem, rows_sem = refs[-4:]
    groups = len(out_refs)
    ids_copy = pltpu.make_async_copy(ids_hbm, ids_ref, ids_sem)
    rows_copy = pltpu.make_async_copy(rows_hbm, rows_ref, rows_sem)
    ids_copy.start()
    rows_copy.start()
    ids_copy.wait()
    chosen = placement(own_ref[0], ids_ref[...], groups).astype(jnp.bfloat16)
    chosen_ref[...] = chosen
    rows_copy.wait()
    ordered = jnp.dot(chosen, rows_ref[...], preferred_element_type=jnp.float32)
    ordered = ordered.astype(jnp.bfloat16)
    size = ordered.shape[0] // groups
    for k, out_ref in enumerate(out_refs):
        out_ref[...] = ordered[k * size : (k + 1) * size, :]


def folded_squares(rows):
    total = 0.0
    for lane in range(0, rows.shape[1], LANES):
        wide = rows[:, lane : lane + LANES].astype(jnp.float32)
        total += wide * wide
    return total


def add_columns(rows, scale, col_refs, total, dens):
    for col_ref in col_refs:
        for start in range(0, col_ref.shape[0], BLOCK):
            cols = col_ref[start : min(start + BLOCK, col_ref.shape[0]), :]
            squares = jnp.sum(folded_squares(cols).T, axis=0, keepdims=True)
            col_inv = lax.rsqrt(squares + 1e-06)
            raw = lax.dot_general(
                rows, cols, (((1,), (1,)), ((), ())), preferred_element_type=jnp.float32
            )
            weight = jnp.exp2(raw * scale * col_inv)
            for lane in range(0, cols.shape[0], LANES):
                dens += weight[:, lane : lane + LANES]
            coef = (weight * (col_inv * floor_weight)).astype(jnp.bfloat16)
            total += jnp.dot(coef, cols, preferred_element_type=jnp.float32)
    return total, dens


def early_kernel(rows_ref, *refs):
    col_refs, (scale_ref, total_ref, dens_ref) = refs[:-3], refs[-3:]
    squares = jnp.sum(folded_squares(rows_ref[...]), axis=1, keepdims=True)
    scale = lax.rsqrt(squares + 1e-06) * (beta_scale * math.log2(math.e))
    scale_ref[...] = jnp.broadcast_to(scale, scale_ref.shape)
    total = jnp.zeros(total_ref.shape, jnp.float32)
    dens = jnp.zeros(dens_ref.shape, jnp.float32)
    total, dens = add_columns(rows_ref[...], scale, col_refs, total, dens)
    total_ref[...] = total
    dens_ref[...] = dens


def middle_kernel(rows_ref, scale_ref, total_ref, dens_ref, *refs):
    col_refs, (total_out, dens_out) = refs[:-2], refs[-2:]
    total, dens = add_columns(
        rows_ref[...], scale_ref[:, 0:1], col_refs, total_ref[...], dens_ref[...]
    )
    total_out[...] = total
    dens_out[...] = dens


def exponent(value):
    return jnp.floor(jnp.log2(jnp.maximum(value, 1e-30)))


def last_kernel(first, padded, rows_ref, scale_ref, total_ref, dens_ref, cols_ref, *out_refs):
    groups = len(out_refs) if padded else len(out_refs) // 2
    size = out_refs[0].shape[0] - (EXTRA if padded else 0)
    mine = slice(first, first + groups * size)
    total, dens = add_columns(
        rows_ref[mine, :],
        scale_ref[mine, 0:1],
        [cols_ref],
        total_ref[mine, :],
        dens_ref[mine, :],
    )
    dens = jnp.sum(dens, axis=1, keepdims=True) * floor_weight
    power = exponent(jnp.max(jnp.abs(total), axis=1, keepdims=True))
    total = total * jnp.exp2(TOP - power)
    dens_power = exponent(dens)
    part = dens * jnp.exp2(-dens_power)
    aside = [power, dens_power]
    for k in range(3):
        piece = part.astype(jnp.bfloat16).astype(jnp.float32)
        aside.append(piece * 2.0 ** (8 * k))
        part = part - piece
    for k in range(groups):
        rows = slice(k * size, (k + 1) * size)
        out_refs[k][:size, :] = total[rows, :]
        if padded:
            aside_ref, top = out_refs[k], size
        else:
            aside_ref, top = out_refs[groups + k], 0
        aside_ref[top:, :] = jnp.zeros((EXTRA, aside_ref.shape[1]), jnp.float32)
        for line, column in enumerate(aside):
            aside_ref[top + line : top + line + 1, :size] = as_row(column[rows, :])


def restore_kernel(half, chosen_ref, *refs):
    refs, (total_ref, dens_ref) = refs[:-2], refs[-2:]
    groups = len(refs) - half
    part_refs = refs[groups - 1 :: -1] + refs[: groups - 1 : -1]
    size = part_refs[half].shape[0]
    chosen = chosen_ref[...]
    sums, dens = [], []
    for k in range(groups):
        aside_ref, top = (part_refs[k], size) if k < half else (part_refs[half + k], 0)
        power, dens_power, *pieces = [
            as_column(aside_ref[top + line : top + line + 1, :size])
            for line in range(5)
        ]
        sums.append(part_refs[k][:size, :] * jnp.exp2(power - TOP))
        part = sum(piece * 2.0 ** (-8 * j) for j, piece in enumerate(pieces))
        dens.append(part * jnp.exp2(dens_power))
    dens_ref[...] = jnp.sum(
        chosen.astype(jnp.float32) * jnp.concatenate(dens, axis=0), axis=0, keepdims=True
    )
    rest = jnp.concatenate(sums, axis=0)
    back = jnp.zeros(rest.shape, jnp.float32)
    for _ in range(2):
        piece = rest.astype(jnp.bfloat16)
        rest = rest - piece.astype(jnp.float32)
        back += lax.dot_general(
            chosen, piece, (((0,), (0,)), ((), ())), preferred_element_type=jnp.float32
        )
    total_ref[...] = back


def on_device(n_gr, n_gc, embeddings, cluster_ids):
    count, width = embeddings.shape
    size = count // n_gr
    own = lax.axis_index("gr").astype(jnp.int32).reshape(1)
    ids = cluster_ids.reshape(1, count)

    chosen, *parts = pl.pallas_call(
        sort_kernel,
        out_shape=[jax.ShapeDtypeStruct((count, count), jnp.bfloat16)]
        + [jax.ShapeDtypeStruct((size, width), jnp.bfloat16)] * n_gr,
        in_specs=[SMEM, HBM, HBM],
        out_specs=[VMEM] * (1 + n_gr),
        scratch_shapes=[
            pltpu.VMEM((1, count), jnp.int32),
            pltpu.VMEM((count, width), embeddings.dtype),
            pltpu.SemaphoreType.DMA,
            pltpu.SemaphoreType.DMA,
        ],
        compiler_params=GRANT,
        name="sort_rows",
    )(own, in_hbm(ids), in_hbm(embeddings))

    def along_gr(part, bits):
        return lax.ppermute(part, "gr", [(i, i ^ bits) for i in range(n_gr)])

    def along_gc(block, bits):
        return lax.ppermute(block, "gc", [(i, i ^ bits) for i in range(n_gc)])

    def other_core(block):
        return along_gc(block, 1)

    def cost(*blocks):
        pairs = count * sum(block.shape[0] for block in blocks)
        return pl.CostEstimate(
            flops=4 * pairs * width,
            bytes_accessed=0,
            transcendentals=pairs,
        )

    held = [parts[0]] + [along_gr(parts[k], k) for k in range(1, n_gr)]
    half = n_gr // 2
    sides = [k for k in range(2, n_gc, 2) if not k & (k - 1)]
    corners = [k for k in range(2, n_gc, 2) if k & (k - 1)]

    def to_side(block, step):
        pairs = [(i, i ^ sides[(step + i % 2) % len(sides)]) for i in range(n_gc)]
        return lax.ppermute(block, "gc", pairs)

    chunks = []
    for pieces in (held[:half], held[half:]):
        block = jnp.concatenate(pieces, axis=0)
        near = [block] + [along_gc(block, k) for k in corners]
        near += [to_side(block, step) for step in range(len(sides))]
        chunks.append(jnp.concatenate(near, axis=0))
    rows = jnp.concatenate(held, axis=0)
    chunks[0], rows = lax.optimization_barrier((chunks[0], rows))
    early = [chunks[0], other_core(chunks[0]), chunks[1]]

    scale, total, dens = pl.pallas_call(
        early_kernel,
        out_shape=[
            jax.ShapeDtypeStruct((count, LANES), jnp.float32),
            jax.ShapeDtypeStruct((count, width), jnp.float32),
            jax.ShapeDtypeStruct((count, LANES), jnp.float32),
        ],
        in_specs=[VMEM] * (1 + len(early)),
        out_specs=[VMEM] * 3,
        compiler_params=GRANT,
        cost_estimate=cost(*early),
        name="early_sums",
    )(rows, *early)
    late = other_core(chunks[1])
    def last_sums(first, padded, out_shape, name):
        return pl.pallas_call(
            functools.partial(last_kernel, first, padded),
            out_shape=out_shape,
            in_specs=[VMEM] * 5,
            out_specs=[VMEM] * len(out_shape),
            compiler_params=GRANT,
            cost_estimate=cost(late),
            name=name,
        )(rows, scale, total, dens, late)

    beside = jax.ShapeDtypeStruct((EXTRA, LANES), jnp.float32)
    piece = jax.ShapeDtypeStruct((size, width), jnp.float32)
    longer = jax.ShapeDtypeStruct((size + EXTRA, width), jnp.float32)
    far = last_sums(half * size, False, [piece] * (n_gr - half) + [beside] * (n_gr - half), "far_sums")
    sums = [*last_sums(0, True, [longer] * half, "near_sums"), *far]

    sent = [part.astype(jnp.float16) for part in sums[:n_gr]]
    back = [sent[0]] + [along_gr(sent[k], k) for k in range(1, n_gr)]
    back = [part.astype(jnp.float32) for part in back]
    back += [along_gr(sums[half + k], k) for k in range(half, n_gr)]
    neighbour_sum, density = pl.pallas_call(
        functools.partial(restore_kernel, half),
        out_shape=[
            jax.ShapeDtypeStruct((count, width), jnp.float32),
            jax.ShapeDtypeStruct((1, count), jnp.float32),
        ],
        in_specs=[VMEM] * (1 + len(back)),
        out_specs=[VMEM, VMEM],
        compiler_params=GRANT,
        name="restore_rows",
    )(chosen, *back[n_gr - 1 :: -1], *back[:n_gr - 1 : -1])
    return (neighbour_sum, density.reshape(count))


def solution(mesh):
    in_specs = (P(("gr", "gc"), None), P(("gr", "gc")))
    out_specs = (P(("gr", "gc"), None), P(("gr", "gc")))
    return jax.shard_map(
        functools.partial(on_device, mesh.shape["gr"], mesh.shape["gc"]),
        mesh=mesh,
        in_specs=in_specs,
        out_specs=out_specs,
        check_vma=False,
    )
```

```python
import functools
import math

import jax
import jax.numpy as jnp
from jax import lax
from jax.experimental import pallas as pl
from jax.experimental.pallas import tpu as pltpu
from jax.sharding import PartitionSpec as P

beta_scale = 16.0
floor_weight = math.exp(-beta_scale)
BLOCK = 512
LANES = 128
EXTRA = 8
TOP = 14.0
VMEM = pl.BlockSpec(memory_space=pltpu.VMEM)
HBM = pl.BlockSpec(memory_space=pltpu.HBM)
SMEM = pl.BlockSpec(memory_space=pltpu.SMEM)
GRANT = pltpu.CompilerParams(vmem_limit_bytes=40 * 1024 * 1024)


def in_hbm(array):
    return pltpu.with_memory_space_constraint(array, pltpu.HBM)


def diagonal(count):
    first = lax.broadcasted_iota(jnp.int32, (count, count), 0)
    second = lax.broadcasted_iota(jnp.int32, (count, count), 1)
    return first == second


def as_row(column):
    return jnp.sum(
        jnp.where(diagonal(column.shape[0]), column, jnp.zeros_like(column)),
        axis=0,
        keepdims=True,
    )


def as_column(row):
    return jnp.sum(
        jnp.where(diagonal(row.shape[1]), row, jnp.zeros_like(row)),
        axis=1,
        keepdims=True,
    )


def placement(own, ids, groups):
    count = ids.shape[1]
    first = lax.broadcasted_iota(jnp.int32, (count, count), 0)
    second = lax.broadcasted_iota(jnp.int32, (count, count), 1)
    earlier = jnp.where((as_column(ids) == ids) & (first < second), 1, 0)
    rank = jnp.sum(earlier, axis=0, keepdims=True)
    slot = (ids ^ own) * (count // groups) + rank
    return jnp.where(first == slot, 1.0, 0.0)


def sort_kernel(own_ref, ids_hbm, rows_hbm, *refs):
    chosen_ref, *out_refs = refs[:-4]
    ids_ref, rows_ref, ids_sem, rows_sem = refs[-4:]
    groups = len(out_refs)
    ids_copy = pltpu.make_async_copy(ids_hbm, ids_ref, ids_sem)
    rows_copy = pltpu.make_async_copy(rows_hbm, rows_ref, rows_sem)
    ids_copy.start()
    rows_copy.start()
    ids_copy.wait()
    chosen = placement(own_ref[0], ids_ref[...], groups).astype(jnp.bfloat16)
    chosen_ref[...] = chosen
    rows_copy.wait()
    ordered = jnp.dot(chosen, rows_ref[...], preferred_element_type=jnp.float32)
    ordered = ordered.astype(jnp.bfloat16)
    size = ordered.shape[0] // groups
    for k, out_ref in enumerate(out_refs):
        out_ref[...] = ordered[k * size : (k + 1) * size, :]


def folded_squares(rows):
    total = 0.0
    for lane in range(0, rows.shape[1], LANES):
        wide = rows[:, lane : lane + LANES].astype(jnp.float32)
        total += wide * wide
    return total


def add_columns(rows, scale, col_refs, total, dens):
    for col_ref in col_refs:
        for start in range(0, col_ref.shape[0], BLOCK):
            cols = col_ref[start : min(start + BLOCK, col_ref.shape[0]), :]
            squares = jnp.sum(folded_squares(cols).T, axis=0, keepdims=True)
            col_inv = lax.rsqrt(squares + 1e-06)
            raw = lax.dot_general(
                rows, cols, (((1,), (1,)), ((), ())), preferred_element_type=jnp.float32
            )
            weight = jnp.exp2(raw * scale * col_inv)
            for lane in range(0, cols.shape[0], LANES):
                dens += weight[:, lane : lane + LANES]
            coef = (weight * (col_inv * floor_weight)).astype(jnp.bfloat16)
            total += jnp.dot(coef, cols, preferred_element_type=jnp.float32)
    return total, dens


def early_kernel(rows_ref, *refs):
    col_refs, (scale_ref, total_ref, dens_ref) = refs[:-3], refs[-3:]
    squares = jnp.sum(folded_squares(rows_ref[...]), axis=1, keepdims=True)
    scale = lax.rsqrt(squares + 1e-06) * (beta_scale * math.log2(math.e))
    scale_ref[...] = jnp.broadcast_to(scale, scale_ref.shape)
    total = jnp.zeros(total_ref.shape, jnp.float32)
    dens = jnp.zeros(dens_ref.shape, jnp.float32)
    total, dens = add_columns(rows_ref[...], scale, col_refs, total, dens)
    total_ref[...] = total
    dens_ref[...] = dens


def middle_kernel(rows_ref, scale_ref, total_ref, dens_ref, *refs):
    col_refs, (total_out, dens_out) = refs[:-2], refs[-2:]
    total, dens = add_columns(
        rows_ref[...], scale_ref[:, 0:1], col_refs, total_ref[...], dens_ref[...]
    )
    total_out[...] = total
    dens_out[...] = dens


def exponent(value):
    return jnp.floor(jnp.log2(jnp.maximum(value, 1e-30)))


def last_kernel(half, rows_ref, scale_ref, total_ref, dens_ref, cols_ref, *out_refs):
    groups = len(out_refs) - half
    size = out_refs[half].shape[0]
    total, dens = add_columns(
        rows_ref[...], scale_ref[:, 0:1], [cols_ref], total_ref[...], dens_ref[...]
    )
    dens = jnp.sum(dens, axis=1, keepdims=True) * floor_weight
    power = exponent(jnp.max(jnp.abs(total), axis=1, keepdims=True))
    total = total * jnp.exp2(TOP - power)
    dens_power = exponent(dens)
    part = dens * jnp.exp2(-dens_power)
    aside = [power, dens_power]
    for k in range(3):
        piece = part.astype(jnp.bfloat16).astype(jnp.float32)
        aside.append(piece * 2.0 ** (8 * k))
        part = part - piece
    for k in range(groups):
        rows = slice(k * size, (k + 1) * size)
        out_refs[k][:size, :] = total[rows, :]
        if k < half:
            aside_ref, top = out_refs[k], size
            aside_ref[size:, :] = jnp.zeros((EXTRA, total.shape[1]), jnp.float32)
        else:
            aside_ref, top = out_refs[half + k], 0
            aside_ref[...] = jnp.zeros(aside_ref.shape, jnp.float32)
        for line, column in enumerate(aside):
            aside_ref[top + line : top + line + 1, :size] = as_row(column[rows, :])


def restore_kernel(half, chosen_ref, *refs):
    refs, (total_ref, dens_ref) = refs[:-2], refs[-2:]
    groups = len(refs) - half
    part_refs = refs[groups - 1 :: -1] + refs[: groups - 1 : -1]
    size = part_refs[half].shape[0]
    chosen = chosen_ref[...]
    sums, dens = [], []
    for k in range(groups):
        aside_ref, top = (part_refs[k], size) if k < half else (part_refs[half + k], 0)
        power, dens_power, *pieces = [
            as_column(aside_ref[top + line : top + line + 1, :size])
            for line in range(5)
        ]
        sums.append(part_refs[k][:size, :] * jnp.exp2(power - TOP))
        part = sum(piece * 2.0 ** (-8 * j) for j, piece in enumerate(pieces))
        dens.append(part * jnp.exp2(dens_power))
    dens_ref[...] = jnp.sum(
        chosen.astype(jnp.float32) * jnp.concatenate(dens, axis=0), axis=0, keepdims=True
    )
    rest = jnp.concatenate(sums, axis=0)
    back = jnp.zeros(rest.shape, jnp.float32)
    for _ in range(2):
        piece = rest.astype(jnp.bfloat16)
        rest = rest - piece.astype(jnp.float32)
        back += lax.dot_general(
            chosen, piece, (((0,), (0,)), ((), ())), preferred_element_type=jnp.float32
        )
    total_ref[...] = back


def on_device(n_gr, n_gc, embeddings, cluster_ids):
    count, width = embeddings.shape
    size = count // n_gr
    own = lax.axis_index("gr").astype(jnp.int32).reshape(1)
    ids = cluster_ids.reshape(1, count)

    chosen, *parts = pl.pallas_call(
        sort_kernel,
        out_shape=[jax.ShapeDtypeStruct((count, count), jnp.bfloat16)]
        + [jax.ShapeDtypeStruct((size, width), jnp.bfloat16)] * n_gr,
        in_specs=[SMEM, HBM, HBM],
        out_specs=[VMEM] * (1 + n_gr),
        scratch_shapes=[
            pltpu.VMEM((1, count), jnp.int32),
            pltpu.VMEM((count, width), embeddings.dtype),
            pltpu.SemaphoreType.DMA,
            pltpu.SemaphoreType.DMA,
        ],
        compiler_params=GRANT,
        name="sort_rows",
    )(own, in_hbm(ids), in_hbm(embeddings))

    def along_gr(part, bits):
        return lax.ppermute(part, "gr", [(i, i ^ bits) for i in range(n_gr)])

    def along_gc(block, bits):
        return lax.ppermute(block, "gc", [(i, i ^ bits) for i in range(n_gc)])

    def other_core(block):
        return along_gc(block, 1)

    def cost(*blocks):
        pairs = count * sum(block.shape[0] for block in blocks)
        return pl.CostEstimate(
            flops=4 * pairs * width,
            bytes_accessed=0,
            transcendentals=pairs,
        )

    held = [parts[0]] + [along_gr(parts[k], k) for k in range(1, n_gr)]
    half = n_gr // 2
    sides = [k for k in range(2, n_gc, 2) if not k & (k - 1)]
    corners = [k for k in range(2, n_gc, 2) if k & (k - 1)]

    def to_side(block, step):
        pairs = [(i, i ^ sides[(step + i % 2) % len(sides)]) for i in range(n_gc)]
        return lax.ppermute(block, "gc", pairs)

    chunks = []
    for k, pieces in enumerate((held[:half], held[half:])):
        block = jnp.concatenate(pieces, axis=0)
        side_blocks = [to_side(block, step) for step in range(len(sides))]
        corner_blocks = [along_gc(block, bits) for bits in corners]
        near = [block] + (corner_blocks + side_blocks if k else side_blocks + corner_blocks)
        chunks.append(jnp.concatenate(near, axis=0))
    rows = jnp.concatenate(held, axis=0)
    chunks[0], rows = lax.optimization_barrier((chunks[0], rows))
    early = [chunks[0], other_core(chunks[0]), chunks[1]]

    scale, total, dens = pl.pallas_call(
        early_kernel,
        out_shape=[
            jax.ShapeDtypeStruct((count, LANES), jnp.float32),
            jax.ShapeDtypeStruct((count, width), jnp.float32),
            jax.ShapeDtypeStruct((count, LANES), jnp.float32),
        ],
        in_specs=[VMEM] * (1 + len(early)),
        out_specs=[VMEM] * 3,
        compiler_params=GRANT,
        cost_estimate=cost(*early),
        name="early_sums",
    )(rows, *early)
    late = other_core(chunks[1])
    sums = pl.pallas_call(
        functools.partial(last_kernel, half),
        out_shape=[jax.ShapeDtypeStruct((size + EXTRA, width), jnp.float32)] * half
        + [jax.ShapeDtypeStruct((size, width), jnp.float32)] * (n_gr - half)
        + [jax.ShapeDtypeStruct((EXTRA, LANES), jnp.float32)] * (n_gr - half),
        in_specs=[VMEM] * 5,
        out_specs=[VMEM] * (2 * n_gr - half),
        compiler_params=GRANT,
        cost_estimate=cost(late),
        name="last_sums",
    )(rows, scale, total, dens, late)

    sent = [part.astype(jnp.float16) for part in sums[:n_gr]]
    back = [sent[0]] + [along_gr(sent[k], k) for k in range(1, n_gr)]
    back = [part.astype(jnp.float32) for part in back]
    back += [along_gr(sums[half + k], k) for k in range(half, n_gr)]
    neighbour_sum, density = pl.pallas_call(
        functools.partial(restore_kernel, half),
        out_shape=[
            jax.ShapeDtypeStruct((count, width), jnp.float32),
            jax.ShapeDtypeStruct((1, count), jnp.float32),
        ],
        in_specs=[VMEM] * (1 + len(back)),
        out_specs=[VMEM, VMEM],
        compiler_params=GRANT,
        name="restore_rows",
    )(chosen, *back[n_gr - 1 :: -1], *back[:n_gr - 1 : -1])
    return (neighbour_sum, density.reshape(count))


def solution(mesh):
    in_specs = (P(("gr", "gc"), None), P(("gr", "gc")))
    out_specs = (P(("gr", "gc"), None), P(("gr", "gc")))
    return jax.shard_map(
        functools.partial(on_device, mesh.shape["gr"], mesh.shape["gc"]),
        mesh=mesh,
        in_specs=in_specs,
        out_specs=out_specs,
        check_vma=False,
    )
```

```python
import functools
import math

import jax
import jax.numpy as jnp
from jax import lax
from jax.experimental import pallas as pl
from jax.experimental.pallas import tpu as pltpu
from jax.sharding import PartitionSpec as P

beta_scale = 16.0
floor_weight = math.exp(-beta_scale)
BLOCK = 256
LANES = 128
EXTRA = 8
TOP = 14.0
VMEM = pl.BlockSpec(memory_space=pltpu.VMEM)
HBM = pl.BlockSpec(memory_space=pltpu.HBM)
SMEM = pl.BlockSpec(memory_space=pltpu.SMEM)
GRANT = pltpu.CompilerParams(vmem_limit_bytes=40 * 1024 * 1024)


def in_hbm(array):
    return pltpu.with_memory_space_constraint(array, pltpu.HBM)


def diagonal(count):
    first = lax.broadcasted_iota(jnp.int32, (count, count), 0)
    second = lax.broadcasted_iota(jnp.int32, (count, count), 1)
    return first == second


def as_row(column):
    return jnp.sum(
        jnp.where(diagonal(column.shape[0]), column, jnp.zeros_like(column)),
        axis=0,
        keepdims=True,
    )


def as_column(row):
    return jnp.sum(
        jnp.where(diagonal(row.shape[1]), row, jnp.zeros_like(row)),
        axis=1,
        keepdims=True,
    )


def placement(own, ids, groups):
    count = ids.shape[1]
    first = lax.broadcasted_iota(jnp.int32, (count, count), 0)
    second = lax.broadcasted_iota(jnp.int32, (count, count), 1)
    earlier = jnp.where((as_column(ids) == ids) & (first < second), 1, 0)
    rank = jnp.sum(earlier, axis=0, keepdims=True)
    slot = (ids ^ own) * (count // groups) + rank
    return jnp.where(first == slot, 1.0, 0.0)


def sort_kernel(own_ref, ids_hbm, rows_hbm, *refs):
    chosen_ref, *out_refs = refs[:-4]
    ids_ref, rows_ref, ids_sem, rows_sem = refs[-4:]
    groups = len(out_refs)
    ids_copy = pltpu.make_async_copy(ids_hbm, ids_ref, ids_sem)
    rows_copy = pltpu.make_async_copy(rows_hbm, rows_ref, rows_sem)
    ids_copy.start()
    rows_copy.start()
    ids_copy.wait()
    chosen = placement(own_ref[0], ids_ref[...], groups).astype(jnp.bfloat16)
    chosen_ref[...] = chosen
    rows_copy.wait()
    ordered = jnp.dot(chosen, rows_ref[...], preferred_element_type=jnp.float32)
    ordered = ordered.astype(jnp.bfloat16)
    size = ordered.shape[0] // groups
    for k, out_ref in enumerate(out_refs):
        out_ref[...] = ordered[k * size : (k + 1) * size, :]


def folded_squares(rows):
    total = 0.0
    for lane in range(0, rows.shape[1], LANES):
        wide = rows[:, lane : lane + LANES].astype(jnp.float32)
        total += wide * wide
    return total


def add_columns(rows, scale, col_refs, total, dens):
    for col_ref in col_refs:
        for start in range(0, col_ref.shape[0], BLOCK):
            cols = col_ref[start : min(start + BLOCK, col_ref.shape[0]), :]
            squares = jnp.sum(folded_squares(cols).T, axis=0, keepdims=True)
            col_inv = lax.rsqrt(squares + 1e-06)
            raw = lax.dot_general(
                rows, cols, (((1,), (1,)), ((), ())), preferred_element_type=jnp.float32
            )
            weight = jnp.exp2(raw * scale * col_inv)
            for lane in range(0, cols.shape[0], LANES):
                dens += weight[:, lane : lane + LANES]
            coef = (weight * (col_inv * floor_weight)).astype(jnp.bfloat16)
            total += jnp.dot(coef, cols, preferred_element_type=jnp.float32)
    return total, dens


def early_kernel(rows_ref, *refs):
    col_refs, (scale_ref, total_ref, dens_ref) = refs[:-3], refs[-3:]
    squares = jnp.sum(folded_squares(rows_ref[...]), axis=1, keepdims=True)
    scale = lax.rsqrt(squares + 1e-06) * (beta_scale * math.log2(math.e))
    scale_ref[...] = jnp.broadcast_to(scale, scale_ref.shape)
    total = jnp.zeros(total_ref.shape, jnp.float32)
    dens = jnp.zeros(dens_ref.shape, jnp.float32)
    total, dens = add_columns(rows_ref[...], scale, col_refs, total, dens)
    total_ref[...] = total
    dens_ref[...] = dens


def middle_kernel(rows_ref, scale_ref, total_ref, dens_ref, *refs):
    col_refs, (total_out, dens_out) = refs[:-2], refs[-2:]
    total, dens = add_columns(
        rows_ref[...], scale_ref[:, 0:1], col_refs, total_ref[...], dens_ref[...]
    )
    total_out[...] = total
    dens_out[...] = dens


def exponent(value):
    return jnp.floor(jnp.log2(jnp.maximum(value, 1e-30)))


def last_kernel(half, rows_ref, scale_ref, total_ref, dens_ref, cols_ref, *out_refs):
    groups = len(out_refs) - half
    size = out_refs[half].shape[0]
    total, dens = add_columns(
        rows_ref[...], scale_ref[:, 0:1], [cols_ref], total_ref[...], dens_ref[...]
    )
    dens = jnp.sum(dens, axis=1, keepdims=True) * floor_weight
    power = exponent(jnp.max(jnp.abs(total), axis=1, keepdims=True))
    total = total * jnp.exp2(TOP - power)
    dens_power = exponent(dens)
    part = dens * jnp.exp2(-dens_power)
    aside = [power, dens_power]
    for k in range(3):
        piece = part.astype(jnp.bfloat16).astype(jnp.float32)
        aside.append(piece * 2.0 ** (8 * k))
        part = part - piece
    for k in range(groups):
        rows = slice(k * size, (k + 1) * size)
        out_refs[k][:size, :] = total[rows, :]
        if k < half:
            aside_ref, top = out_refs[k], size
            aside_ref[size:, :] = jnp.zeros((EXTRA, total.shape[1]), jnp.float32)
        else:
            aside_ref, top = out_refs[half + k], 0
            aside_ref[...] = jnp.zeros(aside_ref.shape, jnp.float32)
        for line, column in enumerate(aside):
            aside_ref[top + line : top + line + 1, :size] = as_row(column[rows, :])


def restore_kernel(half, chosen_ref, *refs):
    refs, (total_ref, dens_ref) = refs[:-2], refs[-2:]
    groups = len(refs) - half
    part_refs = refs[groups - 1 :: -1] + refs[: groups - 1 : -1]
    size = part_refs[half].shape[0]
    chosen = chosen_ref[...]
    sums, dens = [], []
    for k in range(groups):
        aside_ref, top = (part_refs[k], size) if k < half else (part_refs[half + k], 0)
        power, dens_power, *pieces = [
            as_column(aside_ref[top + line : top + line + 1, :size])
            for line in range(5)
        ]
        sums.append(part_refs[k][:size, :] * jnp.exp2(power - TOP))
        part = sum(piece * 2.0 ** (-8 * j) for j, piece in enumerate(pieces))
        dens.append(part * jnp.exp2(dens_power))
    dens_ref[...] = jnp.sum(
        chosen.astype(jnp.float32) * jnp.concatenate(dens, axis=0), axis=0, keepdims=True
    )
    rest = jnp.concatenate(sums, axis=0)
    back = jnp.zeros(rest.shape, jnp.float32)
    for _ in range(2):
        piece = rest.astype(jnp.bfloat16)
        rest = rest - piece.astype(jnp.float32)
        back += lax.dot_general(
            chosen, piece, (((0,), (0,)), ((), ())), preferred_element_type=jnp.float32
        )
    total_ref[...] = back


def on_device(n_gr, n_gc, embeddings, cluster_ids):
    count, width = embeddings.shape
    size = count // n_gr
    own = lax.axis_index("gr").astype(jnp.int32).reshape(1)
    ids = cluster_ids.reshape(1, count)

    chosen, *parts = pl.pallas_call(
        sort_kernel,
        out_shape=[jax.ShapeDtypeStruct((count, count), jnp.bfloat16)]
        + [jax.ShapeDtypeStruct((size, width), jnp.bfloat16)] * n_gr,
        in_specs=[SMEM, HBM, HBM],
        out_specs=[VMEM] * (1 + n_gr),
        scratch_shapes=[
            pltpu.VMEM((1, count), jnp.int32),
            pltpu.VMEM((count, width), embeddings.dtype),
            pltpu.SemaphoreType.DMA,
            pltpu.SemaphoreType.DMA,
        ],
        compiler_params=GRANT,
        name="sort_rows",
    )(own, in_hbm(ids), in_hbm(embeddings))

    def along_gr(part, bits):
        return lax.ppermute(part, "gr", [(i, i ^ bits) for i in range(n_gr)])

    def along_gc(block, bits):
        return lax.ppermute(block, "gc", [(i, i ^ bits) for i in range(n_gc)])

    def other_core(block):
        return along_gc(block, 1)

    def cost(*blocks):
        pairs = count * sum(block.shape[0] for block in blocks)
        return pl.CostEstimate(
            flops=4 * pairs * width,
            bytes_accessed=0,
            transcendentals=pairs,
        )

    held = [parts[0]] + [along_gr(parts[k], k) for k in range(1, n_gr)]
    half = n_gr // 2
    sides = [k for k in range(2, n_gc, 2) if not k & (k - 1)]
    corners = [k for k in range(2, n_gc, 2) if k & (k - 1)]

    def to_side(block, step):
        pairs = [(i, i ^ sides[(step + i % 2) % len(sides)]) for i in range(n_gc)]
        return lax.ppermute(block, "gc", pairs)

    chunks = []
    for pieces in (held[:half], held[half:]):
        block = jnp.concatenate(pieces, axis=0)
        near = [block] + [along_gc(block, k) for k in corners]
        near += [to_side(block, step) for step in range(len(sides))]
        chunks.append(jnp.concatenate(near, axis=0))
    rows = jnp.concatenate(held, axis=0)
    chunks[0], rows = lax.optimization_barrier((chunks[0], rows))
    early = [chunks[0], other_core(chunks[0]), chunks[1]]

    scale, total, dens = pl.pallas_call(
        early_kernel,
        out_shape=[
            jax.ShapeDtypeStruct((count, LANES), jnp.float32),
            jax.ShapeDtypeStruct((count, width), jnp.float32),
            jax.ShapeDtypeStruct((count, LANES), jnp.float32),
        ],
        in_specs=[VMEM] * (1 + len(early)),
        out_specs=[VMEM] * 3,
        compiler_params=GRANT,
        cost_estimate=cost(*early),
        name="early_sums",
    )(rows, *early)
    late = other_core(chunks[1])
    sums = pl.pallas_call(
        functools.partial(last_kernel, half),
        out_shape=[jax.ShapeDtypeStruct((size + EXTRA, width), jnp.float32)] * half
        + [jax.ShapeDtypeStruct((size, width), jnp.float32)] * (n_gr - half)
        + [jax.ShapeDtypeStruct((EXTRA, LANES), jnp.float32)] * (n_gr - half),
        in_specs=[VMEM] * 5,
        out_specs=[VMEM] * (2 * n_gr - half),
        compiler_params=GRANT,
        cost_estimate=cost(late),
        name="last_sums",
    )(rows, scale, total, dens, late)

    sent = [part.astype(jnp.float16) for part in sums[:n_gr]]
    back = [sent[0]] + [along_gr(sent[k], k) for k in range(1, n_gr)]
    back = [part.astype(jnp.float32) for part in back]
    back += [along_gr(sums[half + k], k) for k in range(half, n_gr)]
    neighbour_sum, density = pl.pallas_call(
        functools.partial(restore_kernel, half),
        out_shape=[
            jax.ShapeDtypeStruct((count, width), jnp.float32),
            jax.ShapeDtypeStruct((1, count), jnp.float32),
        ],
        in_specs=[VMEM] * (1 + len(back)),
        out_specs=[VMEM, VMEM],
        compiler_params=GRANT,
        name="restore_rows",
    )(chosen, *back[n_gr - 1 :: -1], *back[:n_gr - 1 : -1])
    return (neighbour_sum, density.reshape(count))


def solution(mesh):
    in_specs = (P(("gr", "gc"), None), P(("gr", "gc")))
    out_specs = (P(("gr", "gc"), None), P(("gr", "gc")))
    return jax.shard_map(
        functools.partial(on_device, mesh.shape["gr"], mesh.shape["gc"]),
        mesh=mesh,
        in_specs=in_specs,
        out_specs=out_specs,
        check_vma=False,
    )
```

```python
import functools
import math

import jax
import jax.numpy as jnp
from jax import lax
from jax.experimental import pallas as pl
from jax.experimental.pallas import tpu as pltpu
from jax.sharding import PartitionSpec as P

beta_scale = 16.0
floor_weight = math.exp(-beta_scale)
BLOCK = 512
LANES = 128
EXTRA = 8
TOP = 14.0
VMEM = pl.BlockSpec(memory_space=pltpu.VMEM)
HBM = pl.BlockSpec(memory_space=pltpu.HBM)
SMEM = pl.BlockSpec(memory_space=pltpu.SMEM)
GRANT = pltpu.CompilerParams(vmem_limit_bytes=40 * 1024 * 1024)


def in_hbm(array):
    return pltpu.with_memory_space_constraint(array, pltpu.HBM)


def diagonal(count):
    first = lax.broadcasted_iota(jnp.int32, (count, count), 0)
    second = lax.broadcasted_iota(jnp.int32, (count, count), 1)
    return first == second


def as_row(column):
    return jnp.sum(
        jnp.where(diagonal(column.shape[0]), column, jnp.zeros_like(column)),
        axis=0,
        keepdims=True,
    )


def as_column(row):
    return jnp.sum(
        jnp.where(diagonal(row.shape[1]), row, jnp.zeros_like(row)),
        axis=1,
        keepdims=True,
    )


def placement(own, ids, groups):
    count = ids.shape[1]
    first = lax.broadcasted_iota(jnp.int32, (count, count), 0)
    second = lax.broadcasted_iota(jnp.int32, (count, count), 1)
    earlier = jnp.where((as_column(ids) == ids) & (first < second), 1, 0)
    rank = jnp.sum(earlier, axis=0, keepdims=True)
    slot = (ids ^ own) * (count // groups) + rank
    return jnp.where(first == slot, 1.0, 0.0)


def sort_kernel(own_ref, ids_hbm, rows_hbm, *refs):
    chosen_ref, *out_refs = refs[:-4]
    ids_ref, rows_ref, ids_sem, rows_sem = refs[-4:]
    groups = len(out_refs)
    ids_copy = pltpu.make_async_copy(ids_hbm, ids_ref, ids_sem)
    rows_copy = pltpu.make_async_copy(rows_hbm, rows_ref, rows_sem)
    ids_copy.start()
    rows_copy.start()
    ids_copy.wait()
    chosen = placement(own_ref[0], ids_ref[...], groups).astype(jnp.bfloat16)
    chosen_ref[...] = chosen
    rows_copy.wait()
    ordered = jnp.dot(chosen, rows_ref[...], preferred_element_type=jnp.float32)
    ordered = ordered.astype(jnp.bfloat16)
    size = ordered.shape[0] // groups
    for k, out_ref in enumerate(out_refs):
        out_ref[...] = ordered[k * size : (k + 1) * size, :]


def folded_squares(rows):
    total = 0.0
    for lane in range(0, rows.shape[1], LANES):
        wide = rows[:, lane : lane + LANES].astype(jnp.float32)
        total += wide * wide
    return total


def add_columns(rows, scale, col_refs, total, dens):
    for col_ref in col_refs:
        for start in range(0, col_ref.shape[0], BLOCK):
            cols = col_ref[start : min(start + BLOCK, col_ref.shape[0]), :]
            squares = jnp.sum(folded_squares(cols).T, axis=0, keepdims=True)
            col_inv = lax.rsqrt(squares + 1e-06)
            raw = lax.dot_general(
                rows, cols, (((1,), (1,)), ((), ())), preferred_element_type=jnp.float32
            )
            weight = jnp.exp2(raw * scale * col_inv)
            for lane in range(0, cols.shape[0], LANES):
                dens += weight[:, lane : lane + LANES]
            coef = (weight * (col_inv * floor_weight)).astype(jnp.bfloat16)
            total += jnp.dot(coef, cols, preferred_element_type=jnp.float32)
    return total, dens


def early_kernel(rows_ref, *refs):
    col_refs, (scale_ref, total_ref, dens_ref) = refs[:-3], refs[-3:]
    squares = jnp.sum(folded_squares(rows_ref[...]), axis=1, keepdims=True)
    scale = lax.rsqrt(squares + 1e-06) * (beta_scale * math.log2(math.e))
    scale_ref[...] = jnp.broadcast_to(scale, scale_ref.shape)
    total = jnp.zeros(total_ref.shape, jnp.float32)
    dens = jnp.zeros(dens_ref.shape, jnp.float32)
    total, dens = add_columns(rows_ref[...], scale, col_refs, total, dens)
    total_ref[...] = total
    dens_ref[...] = dens


def middle_kernel(rows_ref, scale_ref, total_ref, dens_ref, *refs):
    col_refs, (total_out, dens_out) = refs[:-2], refs[-2:]
    total, dens = add_columns(
        rows_ref[...], scale_ref[:, 0:1], col_refs, total_ref[...], dens_ref[...]
    )
    total_out[...] = total
    dens_out[...] = dens


def exponent(value):
    return jnp.floor(jnp.log2(jnp.maximum(value, 1e-30)))


def last_kernel(first, padded, rows_ref, scale_ref, total_ref, dens_ref, cols_ref, *out_refs):
    groups = len(out_refs) if padded else len(out_refs) // 2
    size = out_refs[0].shape[0] - (EXTRA if padded else 0)
    mine = slice(first, first + groups * size)
    total, dens = add_columns(
        rows_ref[mine, :],
        scale_ref[mine, 0:1],
        [cols_ref],
        total_ref[mine, :],
        dens_ref[mine, :],
    )
    dens = jnp.sum(dens, axis=1, keepdims=True) * floor_weight
    power = exponent(jnp.max(jnp.abs(total), axis=1, keepdims=True))
    total = total * jnp.exp2(TOP - power)
    dens_power = exponent(dens)
    part = dens * jnp.exp2(-dens_power)
    aside = [power, dens_power]
    for k in range(3):
        piece = part.astype(jnp.bfloat16).astype(jnp.float32)
        aside.append(piece * 2.0 ** (8 * k))
        part = part - piece
    for k in range(groups):
        rows = slice(k * size, (k + 1) * size)
        out_refs[k][:size, :] = total[rows, :]
        if padded:
            aside_ref, top = out_refs[k], size
        else:
            aside_ref, top = out_refs[groups + k], 0
        aside_ref[top:, :] = jnp.zeros((EXTRA, aside_ref.shape[1]), jnp.float32)
        for line, column in enumerate(aside):
            aside_ref[top + line : top + line + 1, :size] = as_row(column[rows, :])


def restore_kernel(half, chosen_ref, *refs):
    refs, (total_ref, dens_ref) = refs[:-2], refs[-2:]
    groups = len(refs) - half
    part_refs = refs[::-1]
    part_refs = part_refs[:half] + part_refs[groups:] + part_refs[half:groups]
    size = part_refs[half].shape[0]
    chosen = chosen_ref[...]
    sums, dens = [], []
    for k in range(groups):
        aside_ref, top = (part_refs[k], size) if k < half else (part_refs[half + k], 0)
        power, dens_power, *pieces = [
            as_column(aside_ref[top + line : top + line + 1, :size])
            for line in range(5)
        ]
        sums.append(part_refs[k][:size, :] * jnp.exp2(power - TOP))
        part = sum(piece * 2.0 ** (-8 * j) for j, piece in enumerate(pieces))
        dens.append(part * jnp.exp2(dens_power))
    dens_ref[...] = jnp.sum(
        chosen.astype(jnp.float32) * jnp.concatenate(dens, axis=0), axis=0, keepdims=True
    )
    rest = jnp.concatenate(sums, axis=0)
    back = jnp.zeros(rest.shape, jnp.float32)
    for _ in range(2):
        piece = rest.astype(jnp.bfloat16)
        rest = rest - piece.astype(jnp.float32)
        back += lax.dot_general(
            chosen, piece, (((0,), (0,)), ((), ())), preferred_element_type=jnp.float32
        )
    total_ref[...] = back


def on_device(n_gr, n_gc, embeddings, cluster_ids):
    count, width = embeddings.shape
    size = count // n_gr
    own = lax.axis_index("gr").astype(jnp.int32).reshape(1)
    ids = cluster_ids.reshape(1, count)

    chosen, *parts = pl.pallas_call(
        sort_kernel,
        out_shape=[jax.ShapeDtypeStruct((count, count), jnp.bfloat16)]
        + [jax.ShapeDtypeStruct((size, width), jnp.bfloat16)] * n_gr,
        in_specs=[SMEM, HBM, HBM],
        out_specs=[VMEM] * (1 + n_gr),
        scratch_shapes=[
            pltpu.VMEM((1, count), jnp.int32),
            pltpu.VMEM((count, width), embeddings.dtype),
            pltpu.SemaphoreType.DMA,
            pltpu.SemaphoreType.DMA,
        ],
        compiler_params=GRANT,
        name="sort_rows",
    )(own, in_hbm(ids), in_hbm(embeddings))

    def along_gr(part, bits):
        return lax.ppermute(part, "gr", [(i, i ^ bits) for i in range(n_gr)])

    def along_gc(block, bits):
        return lax.ppermute(block, "gc", [(i, i ^ bits) for i in range(n_gc)])

    def other_core(block):
        return along_gc(block, 1)

    def cost(*blocks):
        pairs = count * sum(block.shape[0] for block in blocks)
        return pl.CostEstimate(
            flops=4 * pairs * width,
            bytes_accessed=0,
            transcendentals=pairs,
        )

    held = [parts[0]] + [along_gr(parts[k], k) for k in range(1, n_gr)]
    half = n_gr // 2
    sides = [k for k in range(2, n_gc, 2) if not k & (k - 1)]
    corners = [k for k in range(2, n_gc, 2) if k & (k - 1)]

    def to_side(block, step):
        pairs = [(i, i ^ sides[(step + i % 2) % len(sides)]) for i in range(n_gc)]
        return lax.ppermute(block, "gc", pairs)

    chunks = []
    for pieces in (held[:half], held[half:]):
        block = jnp.concatenate(pieces, axis=0)
        near = [block] + [along_gc(block, k) for k in corners]
        near += [to_side(block, step) for step in range(len(sides))]
        chunks.append(jnp.concatenate(near, axis=0))
    rows = jnp.concatenate(held, axis=0)
    chunks[0], rows = lax.optimization_barrier((chunks[0], rows))
    early = [chunks[0], other_core(chunks[0]), chunks[1]]

    scale, total, dens = pl.pallas_call(
        early_kernel,
        out_shape=[
            jax.ShapeDtypeStruct((count, LANES), jnp.float32),
            jax.ShapeDtypeStruct((count, width), jnp.float32),
            jax.ShapeDtypeStruct((count, LANES), jnp.float32),
        ],
        in_specs=[VMEM] * (1 + len(early)),
        out_specs=[VMEM] * 3,
        compiler_params=GRANT,
        cost_estimate=cost(*early),
        name="early_sums",
    )(rows, *early)
    late = other_core(chunks[1])
    def last_sums(first, padded, out_shape, name):
        return pl.pallas_call(
            functools.partial(last_kernel, first, padded),
            out_shape=out_shape,
            in_specs=[VMEM] * 5,
            out_specs=[VMEM] * len(out_shape),
            compiler_params=GRANT,
            cost_estimate=cost(late),
            name=name,
        )(rows, scale, total, dens, late)

    beside = jax.ShapeDtypeStruct((EXTRA, LANES), jnp.float32)
    piece = jax.ShapeDtypeStruct((size, width), jnp.float32)
    longer = jax.ShapeDtypeStruct((size + EXTRA, width), jnp.float32)
    far = last_sums(half * size, False, [piece] * (n_gr - half) + [beside] * (n_gr - half), "far_sums")
    sums = [*last_sums(0, True, [longer] * half, "near_sums"), *far]

    sent = [part.astype(jnp.float16) for part in sums[:n_gr]]
    back = [sent[0]] + [along_gr(sent[k], k) for k in range(1, n_gr)]
    back = [part.astype(jnp.float32) for part in back]
    back += [along_gr(sums[half + k], k) for k in range(half, n_gr)]
    neighbour_sum, density = pl.pallas_call(
        functools.partial(restore_kernel, half),
        out_shape=[
            jax.ShapeDtypeStruct((count, width), jnp.float32),
            jax.ShapeDtypeStruct((1, count), jnp.float32),
        ],
        in_specs=[VMEM] * (1 + len(back)),
        out_specs=[VMEM, VMEM],
        compiler_params=GRANT,
        name="restore_rows",
    )(chosen, *back[half:n_gr][::-1], *back[n_gr:][::-1], *back[:half][::-1])
    return (neighbour_sum, density.reshape(count))


def solution(mesh):
    in_specs = (P(("gr", "gc"), None), P(("gr", "gc")))
    out_specs = (P(("gr", "gc"), None), P(("gr", "gc")))
    return jax.shard_map(
        functools.partial(on_device, mesh.shape["gr"], mesh.shape["gc"]),
        mesh=mesh,
        in_specs=in_specs,
        out_specs=out_specs,
        check_vma=False,
    )
```

```python
import functools
import math

import jax
import jax.numpy as jnp
from jax import lax
from jax.experimental import pallas as pl
from jax.experimental.pallas import tpu as pltpu
from jax.sharding import PartitionSpec as P

beta_scale = 16.0
floor_weight = math.exp(-beta_scale)
BLOCK = 512
LANES = 128
EXTRA = 8
TOP = 14.0
VMEM = pl.BlockSpec(memory_space=pltpu.VMEM)
HBM = pl.BlockSpec(memory_space=pltpu.HBM)
SMEM = pl.BlockSpec(memory_space=pltpu.SMEM)
GRANT = pltpu.CompilerParams(vmem_limit_bytes=40 * 1024 * 1024)


def in_hbm(array):
    return pltpu.with_memory_space_constraint(array, pltpu.HBM)


def diagonal(count):
    first = lax.broadcasted_iota(jnp.int32, (count, count), 0)
    second = lax.broadcasted_iota(jnp.int32, (count, count), 1)
    return first == second


def as_row(column):
    return jnp.sum(
        jnp.where(diagonal(column.shape[0]), column, jnp.zeros_like(column)),
        axis=0,
        keepdims=True,
    )


def as_column(row):
    return jnp.sum(
        jnp.where(diagonal(row.shape[1]), row, jnp.zeros_like(row)),
        axis=1,
        keepdims=True,
    )


def placement(own, ids, groups):
    count = ids.shape[1]
    first = lax.broadcasted_iota(jnp.int32, (count, count), 0)
    second = lax.broadcasted_iota(jnp.int32, (count, count), 1)
    earlier = jnp.where((as_column(ids) == ids) & (first < second), 1, 0)
    rank = jnp.sum(earlier, axis=0, keepdims=True)
    slot = (ids ^ own) * (count // groups) + rank
    return jnp.where(first == slot, 1.0, 0.0)


def sort_kernel(own_ref, ids_hbm, rows_hbm, *refs):
    chosen_ref, *out_refs = refs[:-4]
    ids_ref, rows_ref, ids_sem, rows_sem = refs[-4:]
    groups = len(out_refs)
    ids_copy = pltpu.make_async_copy(ids_hbm, ids_ref, ids_sem)
    rows_copy = pltpu.make_async_copy(rows_hbm, rows_ref, rows_sem)
    ids_copy.start()
    rows_copy.start()
    ids_copy.wait()
    chosen = placement(own_ref[0], ids_ref[...], groups).astype(jnp.bfloat16)
    chosen_ref[...] = chosen
    rows_copy.wait()
    ordered = jnp.dot(chosen, rows_ref[...], preferred_element_type=jnp.float32)
    ordered = ordered.astype(jnp.bfloat16)
    size = ordered.shape[0] // groups
    for k, out_ref in enumerate(out_refs):
        out_ref[...] = ordered[k * size : (k + 1) * size, :]


def folded_squares(rows):
    total = 0.0
    for lane in range(0, rows.shape[1], LANES):
        wide = rows[:, lane : lane + LANES].astype(jnp.float32)
        total += wide * wide
    return total


def add_columns(rows, scale, col_refs, total, dens):
    for col_ref in col_refs:
        for start in range(0, col_ref.shape[0], BLOCK):
            cols = col_ref[start : min(start + BLOCK, col_ref.shape[0]), :]
            squares = jnp.sum(folded_squares(cols).T, axis=0, keepdims=True)
            col_inv = lax.rsqrt(squares + 1e-06)
            raw = lax.dot_general(
                rows, cols, (((1,), (1,)), ((), ())), preferred_element_type=jnp.float32
            )
            weight = jnp.exp2(raw * scale * col_inv)
            for lane in range(0, cols.shape[0], LANES):
                dens += weight[:, lane : lane + LANES]
            coef = (weight * (col_inv * floor_weight)).astype(jnp.bfloat16)
            total += jnp.dot(coef, cols, preferred_element_type=jnp.float32)
    return total, dens


def early_kernel(rows_ref, *refs):
    col_refs, (scale_ref, total_ref, dens_ref) = refs[:-3], refs[-3:]
    squares = jnp.sum(folded_squares(rows_ref[...]), axis=1, keepdims=True)
    scale = lax.rsqrt(squares + 1e-06) * (beta_scale * math.log2(math.e))
    scale_ref[...] = jnp.broadcast_to(scale, scale_ref.shape)
    total = jnp.zeros(total_ref.shape, jnp.float32)
    dens = jnp.zeros(dens_ref.shape, jnp.float32)
    total, dens = add_columns(rows_ref[...], scale, col_refs, total, dens)
    total_ref[...] = total
    dens_ref[...] = dens


def middle_kernel(rows_ref, scale_ref, total_ref, dens_ref, *refs):
    col_refs, (total_out, dens_out) = refs[:-2], refs[-2:]
    total, dens = add_columns(
        rows_ref[...], scale_ref[:, 0:1], col_refs, total_ref[...], dens_ref[...]
    )
    total_out[...] = total
    dens_out[...] = dens


def exponent(value):
    return jnp.floor(jnp.log2(jnp.maximum(value, 1e-30)))


def last_kernel(half, rows_ref, scale_ref, total_ref, dens_ref, cols_ref, *out_refs):
    groups = len(out_refs) - half
    size = out_refs[half].shape[0]
    total, dens = add_columns(
        rows_ref[...], scale_ref[:, 0:1], [cols_ref], total_ref[...], dens_ref[...]
    )
    dens = jnp.sum(dens, axis=1, keepdims=True) * floor_weight
    power = exponent(jnp.max(jnp.abs(total), axis=1, keepdims=True))
    total = total * jnp.exp2(TOP - power)
    dens_power = exponent(dens)
    part = dens * jnp.exp2(-dens_power)
    aside = [power, dens_power]
    for k in range(3):
        piece = part.astype(jnp.bfloat16).astype(jnp.float32)
        aside.append(piece * 2.0 ** (8 * k))
        part = part - piece
    for k in range(groups):
        rows = slice(k * size, (k + 1) * size)
        out_refs[k][:size, :] = total[rows, :]
        if k < half:
            aside_ref, top = out_refs[k], size
            aside_ref[size:, :] = jnp.zeros((EXTRA, total.shape[1]), jnp.float32)
        else:
            aside_ref, top = out_refs[half + k], 0
            aside_ref[...] = jnp.zeros(aside_ref.shape, jnp.float32)
        for line, column in enumerate(aside):
            aside_ref[top + line : top + line + 1, :size] = as_row(column[rows, :])


def restore_kernel(half, chosen_ref, *refs):
    refs, (total_ref, dens_ref) = refs[:-2], refs[-2:]
    groups = len(refs) - half
    part_refs = refs[groups - 1 :: -1] + refs[: groups - 1 : -1]
    size = part_refs[half].shape[0]
    chosen = chosen_ref[...]
    sums, dens = [], []
    for k in range(groups):
        aside_ref, top = (part_refs[k], size) if k < half else (part_refs[half + k], 0)
        power, dens_power, *pieces = [
            as_column(aside_ref[top + line : top + line + 1, :size])
            for line in range(5)
        ]
        sums.append(part_refs[k][:size, :] * jnp.exp2(power - TOP))
        part = sum(piece * 2.0 ** (-8 * j) for j, piece in enumerate(pieces))
        dens.append(part * jnp.exp2(dens_power))
    dens_ref[...] = jnp.sum(
        chosen.astype(jnp.float32) * jnp.concatenate(dens, axis=0), axis=0, keepdims=True
    )
    rest = jnp.concatenate(sums, axis=0)
    back = jnp.zeros(rest.shape, jnp.float32)
    for _ in range(2):
        piece = rest.astype(jnp.bfloat16)
        rest = rest - piece.astype(jnp.float32)
        back += lax.dot_general(
            chosen, piece, (((0,), (0,)), ((), ())), preferred_element_type=jnp.float32
        )
    total_ref[...] = back


def on_device(n_gr, n_gc, embeddings, cluster_ids):
    count, width = embeddings.shape
    size = count // n_gr
    own = lax.axis_index("gr").astype(jnp.int32).reshape(1)
    ids = cluster_ids.reshape(1, count)

    chosen, *parts = pl.pallas_call(
        sort_kernel,
        out_shape=[jax.ShapeDtypeStruct((count, count), jnp.bfloat16)]
        + [jax.ShapeDtypeStruct((size, width), jnp.bfloat16)] * n_gr,
        in_specs=[SMEM, HBM, HBM],
        out_specs=[VMEM] * (1 + n_gr),
        scratch_shapes=[
            pltpu.VMEM((1, count), jnp.int32),
            pltpu.VMEM((count, width), embeddings.dtype),
            pltpu.SemaphoreType.DMA,
            pltpu.SemaphoreType.DMA,
        ],
        compiler_params=GRANT,
        name="sort_rows",
    )(own, in_hbm(ids), in_hbm(embeddings))

    def along_gr(part, bits):
        return lax.ppermute(part, "gr", [(i, i ^ bits) for i in range(n_gr)])

    def along_gc(block, bits):
        return lax.ppermute(block, "gc", [(i, i ^ bits) for i in range(n_gc)])

    def other_core(block):
        return along_gc(block, 1)

    def cost(*blocks):
        pairs = count * sum(block.shape[0] for block in blocks)
        return pl.CostEstimate(
            flops=4 * pairs * width,
            bytes_accessed=0,
            transcendentals=pairs,
        )

    held = [parts[0]] + [along_gr(parts[k], k) for k in range(1, n_gr)]
    half = n_gr // 2
    sides = [k for k in range(2, n_gc, 2) if not k & (k - 1)]
    corners = [k for k in range(2, n_gc, 2) if k & (k - 1)]

    def to_side(block, step):
        pairs = [(i, i ^ sides[(step + i % 2) % len(sides)]) for i in range(n_gc)]
        return lax.ppermute(block, "gc", pairs)

    chunks = []
    for k, pieces in enumerate((held[:half], held[half:])):
        block = jnp.concatenate(pieces, axis=0)
        near = [block] + [to_side(block, step) for step in range(k)]
        near += [along_gc(block, bits) for bits in corners]
        near += [to_side(block, step) for step in range(k, len(sides))]
        chunks.append(jnp.concatenate(near, axis=0))
    rows = jnp.concatenate(held, axis=0)
    chunks[0], rows = lax.optimization_barrier((chunks[0], rows))
    early = [chunks[0], other_core(chunks[0]), chunks[1]]

    scale, total, dens = pl.pallas_call(
        early_kernel,
        out_shape=[
            jax.ShapeDtypeStruct((count, LANES), jnp.float32),
            jax.ShapeDtypeStruct((count, width), jnp.float32),
            jax.ShapeDtypeStruct((count, LANES), jnp.float32),
        ],
        in_specs=[VMEM] * (1 + len(early)),
        out_specs=[VMEM] * 3,
        compiler_params=GRANT,
        cost_estimate=cost(*early),
        name="early_sums",
    )(rows, *early)
    late = other_core(chunks[1])
    sums = pl.pallas_call(
        functools.partial(last_kernel, half),
        out_shape=[jax.ShapeDtypeStruct((size + EXTRA, width), jnp.float32)] * half
        + [jax.ShapeDtypeStruct((size, width), jnp.float32)] * (n_gr - half)
        + [jax.ShapeDtypeStruct((EXTRA, LANES), jnp.float32)] * (n_gr - half),
        in_specs=[VMEM] * 5,
        out_specs=[VMEM] * (2 * n_gr - half),
        compiler_params=GRANT,
        cost_estimate=cost(late),
        name="last_sums",
    )(rows, scale, total, dens, late)

    sent = [part.astype(jnp.float16) for part in sums[:n_gr]]
    back = [sent[0]] + [along_gr(sent[k], k) for k in range(1, n_gr)]
    back = [part.astype(jnp.float32) for part in back]
    back += [along_gr(sums[half + k], k) for k in range(half, n_gr)]
    neighbour_sum, density = pl.pallas_call(
        functools.partial(restore_kernel, half),
        out_shape=[
            jax.ShapeDtypeStruct((count, width), jnp.float32),
            jax.ShapeDtypeStruct((1, count), jnp.float32),
        ],
        in_specs=[VMEM] * (1 + len(back)),
        out_specs=[VMEM, VMEM],
        compiler_params=GRANT,
        name="restore_rows",
    )(chosen, *back[n_gr - 1 :: -1], *back[:n_gr - 1 : -1])
    return (neighbour_sum, density.reshape(count))


def solution(mesh):
    in_specs = (P(("gr", "gc"), None), P(("gr", "gc")))
    out_specs = (P(("gr", "gc"), None), P(("gr", "gc")))
    return jax.shard_map(
        functools.partial(on_device, mesh.shape["gr"], mesh.shape["gc"]),
        mesh=mesh,
        in_specs=in_specs,
        out_specs=out_specs,
        check_vma=False,
    )
```

```python
import functools
import math

import jax
import jax.numpy as jnp
from jax import lax
from jax.experimental import pallas as pl
from jax.experimental.pallas import tpu as pltpu
from jax.sharding import PartitionSpec as P

beta_scale = 16.0
floor_weight = math.exp(-beta_scale)
BLOCK = 512
LANES = 128
EXTRA = 8
TOP = 14.0
VMEM = pl.BlockSpec(memory_space=pltpu.VMEM)
HBM = pl.BlockSpec(memory_space=pltpu.HBM)
SMEM = pl.BlockSpec(memory_space=pltpu.SMEM)
GRANT = pltpu.CompilerParams(vmem_limit_bytes=40 * 1024 * 1024)


def in_hbm(array):
    return pltpu.with_memory_space_constraint(array, pltpu.HBM)


def diagonal(count):
    first = lax.broadcasted_iota(jnp.int32, (count, count), 0)
    second = lax.broadcasted_iota(jnp.int32, (count, count), 1)
    return first == second


def as_row(column):
    return jnp.sum(
        jnp.where(diagonal(column.shape[0]), column, jnp.zeros_like(column)),
        axis=0,
        keepdims=True,
    )


def as_column(row):
    return jnp.sum(
        jnp.where(diagonal(row.shape[1]), row, jnp.zeros_like(row)),
        axis=1,
        keepdims=True,
    )


def placement(own, ids, groups):
    count = ids.shape[1]
    first = lax.broadcasted_iota(jnp.int32, (count, count), 0)
    second = lax.broadcasted_iota(jnp.int32, (count, count), 1)
    earlier = jnp.where((as_column(ids) == ids) & (first < second), 1, 0)
    rank = jnp.sum(earlier, axis=0, keepdims=True)
    slot = (ids ^ own) * (count // groups) + rank
    return jnp.where(first == slot, 1.0, 0.0)


def sort_kernel(own_ref, ids_hbm, rows_hbm, *refs):
    chosen_ref, *out_refs = refs[:-4]
    ids_ref, rows_ref, ids_sem, rows_sem = refs[-4:]
    groups = len(out_refs)
    ids_copy = pltpu.make_async_copy(ids_hbm, ids_ref, ids_sem)
    count = rows_hbm.shape[0]
    halves = [slice(0, count // 2), slice(count // 2, count)]
    row_copies = [
        pltpu.make_async_copy(rows_hbm.at[half], rows_ref.at[half], rows_sem.at[k])
        for k, half in enumerate(halves)
    ]
    ids_copy.start()
    for row_copy in row_copies:
        row_copy.start()
    ids_copy.wait()
    chosen = placement(own_ref[0], ids_ref[...], groups).astype(jnp.bfloat16)
    chosen_ref[...] = chosen
    ordered = 0.0
    for row_copy, half in zip(row_copies, halves):
        row_copy.wait()
        ordered += jnp.dot(
            chosen[:, half], rows_ref[half, :], preferred_element_type=jnp.float32
        )
    ordered = ordered.astype(jnp.bfloat16)
    size = ordered.shape[0] // groups
    for k, out_ref in enumerate(out_refs):
        out_ref[...] = ordered[k * size : (k + 1) * size, :]


def folded_squares(rows):
    total = 0.0
    for lane in range(0, rows.shape[1], LANES):
        wide = rows[:, lane : lane + LANES].astype(jnp.float32)
        total += wide * wide
    return total


def add_columns(rows, scale, col_refs, total, dens):
    for col_ref in col_refs:
        for start in range(0, col_ref.shape[0], BLOCK):
            cols = col_ref[start : min(start + BLOCK, col_ref.shape[0]), :]
            squares = jnp.sum(folded_squares(cols).T, axis=0, keepdims=True)
            col_inv = lax.rsqrt(squares + 1e-06)
            raw = lax.dot_general(
                rows, cols, (((1,), (1,)), ((), ())), preferred_element_type=jnp.float32
            )
            weight = jnp.exp2(raw * scale * col_inv)
            for lane in range(0, cols.shape[0], LANES):
                dens += weight[:, lane : lane + LANES]
            coef = (weight * (col_inv * floor_weight)).astype(jnp.bfloat16)
            total += jnp.dot(coef, cols, preferred_element_type=jnp.float32)
    return total, dens


def early_kernel(rows_ref, *refs):
    col_refs, (scale_ref, total_ref, dens_ref) = refs[:-3], refs[-3:]
    squares = jnp.sum(folded_squares(rows_ref[...]), axis=1, keepdims=True)
    scale = lax.rsqrt(squares + 1e-06) * (beta_scale * math.log2(math.e))
    scale_ref[...] = jnp.broadcast_to(scale, scale_ref.shape)
    total = jnp.zeros(total_ref.shape, jnp.float32)
    dens = jnp.zeros(dens_ref.shape, jnp.float32)
    total, dens = add_columns(rows_ref[...], scale, col_refs, total, dens)
    total_ref[...] = total
    dens_ref[...] = dens


def middle_kernel(rows_ref, scale_ref, total_ref, dens_ref, *refs):
    col_refs, (total_out, dens_out) = refs[:-2], refs[-2:]
    total, dens = add_columns(
        rows_ref[...], scale_ref[:, 0:1], col_refs, total_ref[...], dens_ref[...]
    )
    total_out[...] = total
    dens_out[...] = dens


def exponent(value):
    return jnp.floor(jnp.log2(jnp.maximum(value, 1e-30)))


def last_kernel(half, rows_ref, scale_ref, total_ref, dens_ref, cols_ref, *out_refs):
    groups = len(out_refs) - half
    size = out_refs[half].shape[0]
    total, dens = add_columns(
        rows_ref[...], scale_ref[:, 0:1], [cols_ref], total_ref[...], dens_ref[...]
    )
    dens = jnp.sum(dens, axis=1, keepdims=True) * floor_weight
    power = exponent(jnp.max(jnp.abs(total), axis=1, keepdims=True))
    total = total * jnp.exp2(TOP - power)
    dens_power = exponent(dens)
    part = dens * jnp.exp2(-dens_power)
    aside = [power, dens_power]
    for k in range(3):
        piece = part.astype(jnp.bfloat16).astype(jnp.float32)
        aside.append(piece * 2.0 ** (8 * k))
        part = part - piece
    for k in range(groups):
        rows = slice(k * size, (k + 1) * size)
        out_refs[k][:size, :] = total[rows, :]
        if k < half:
            aside_ref, top = out_refs[k], size
            aside_ref[size:, :] = jnp.zeros((EXTRA, total.shape[1]), jnp.float32)
        else:
            aside_ref, top = out_refs[half + k], 0
            aside_ref[...] = jnp.zeros(aside_ref.shape, jnp.float32)
        for line, column in enumerate(aside):
            aside_ref[top + line : top + line + 1, :size] = as_row(column[rows, :])


def restore_kernel(half, chosen_ref, *refs):
    refs, (total_ref, dens_ref) = refs[:-2], refs[-2:]
    groups = len(refs) - half
    part_refs = refs[groups - 1 :: -1] + refs[: groups - 1 : -1]
    size = part_refs[half].shape[0]
    chosen = chosen_ref[...]
    sums, dens = [], []
    for k in range(groups):
        aside_ref, top = (part_refs[k], size) if k < half else (part_refs[half + k], 0)
        power, dens_power, *pieces = [
            as_column(aside_ref[top + line : top + line + 1, :size])
            for line in range(5)
        ]
        sums.append(part_refs[k][:size, :] * jnp.exp2(power - TOP))
        part = sum(piece * 2.0 ** (-8 * j) for j, piece in enumerate(pieces))
        dens.append(part * jnp.exp2(dens_power))
    dens_ref[...] = jnp.sum(
        chosen.astype(jnp.float32) * jnp.concatenate(dens, axis=0), axis=0, keepdims=True
    )
    rest = jnp.concatenate(sums, axis=0)
    back = jnp.zeros(rest.shape, jnp.float32)
    for _ in range(2):
        piece = rest.astype(jnp.bfloat16)
        rest = rest - piece.astype(jnp.float32)
        back += lax.dot_general(
            chosen, piece, (((0,), (0,)), ((), ())), preferred_element_type=jnp.float32
        )
    total_ref[...] = back


def on_device(n_gr, n_gc, embeddings, cluster_ids):
    count, width = embeddings.shape
    size = count // n_gr
    own = lax.axis_index("gr").astype(jnp.int32).reshape(1)
    ids = cluster_ids.reshape(1, count)

    chosen, *parts = pl.pallas_call(
        sort_kernel,
        out_shape=[jax.ShapeDtypeStruct((count, count), jnp.bfloat16)]
        + [jax.ShapeDtypeStruct((size, width), jnp.bfloat16)] * n_gr,
        in_specs=[SMEM, HBM, HBM],
        out_specs=[VMEM] * (1 + n_gr),
        scratch_shapes=[
            pltpu.VMEM((1, count), jnp.int32),
            pltpu.VMEM((count, width), embeddings.dtype),
            pltpu.SemaphoreType.DMA,
            pltpu.SemaphoreType.DMA((2,)),
        ],
        compiler_params=GRANT,
        name="sort_rows",
    )(own, in_hbm(ids), in_hbm(embeddings))

    def along_gr(part, bits):
        return lax.ppermute(part, "gr", [(i, i ^ bits) for i in range(n_gr)])

    def along_gc(block, bits):
        return lax.ppermute(block, "gc", [(i, i ^ bits) for i in range(n_gc)])

    def other_core(block):
        return along_gc(block, 1)

    def cost(*blocks):
        pairs = count * sum(block.shape[0] for block in blocks)
        return pl.CostEstimate(
            flops=4 * pairs * width,
            bytes_accessed=0,
            transcendentals=pairs,
        )

    held = [parts[0]] + [along_gr(parts[k], k) for k in range(1, n_gr)]
    half = n_gr // 2
    sides = [k for k in range(2, n_gc, 2) if not k & (k - 1)]
    corners = [k for k in range(2, n_gc, 2) if k & (k - 1)]

    def to_side(block, step):
        pairs = [(i, i ^ sides[(step + i % 2) % len(sides)]) for i in range(n_gc)]
        return lax.ppermute(block, "gc", pairs)

    chunks = []
    for pieces in (held[:half], held[half:]):
        block = jnp.concatenate(pieces, axis=0)
        near = [block] + [along_gc(block, k) for k in corners]
        near += [to_side(block, step) for step in range(len(sides))]
        chunks.append(jnp.concatenate(near, axis=0))
    rows = jnp.concatenate(held, axis=0)
    chunks[0], rows = lax.optimization_barrier((chunks[0], rows))
    early = [chunks[0], other_core(chunks[0]), chunks[1]]

    scale, total, dens = pl.pallas_call(
        early_kernel,
        out_shape=[
            jax.ShapeDtypeStruct((count, LANES), jnp.float32),
            jax.ShapeDtypeStruct((count, width), jnp.float32),
            jax.ShapeDtypeStruct((count, LANES), jnp.float32),
        ],
        in_specs=[VMEM] * (1 + len(early)),
        out_specs=[VMEM] * 3,
        compiler_params=GRANT,
        cost_estimate=cost(*early),
        name="early_sums",
    )(rows, *early)
    late = other_core(chunks[1])
    sums = pl.pallas_call(
        functools.partial(last_kernel, half),
        out_shape=[jax.ShapeDtypeStruct((size + EXTRA, width), jnp.float32)] * half
        + [jax.ShapeDtypeStruct((size, width), jnp.float32)] * (n_gr - half)
        + [jax.ShapeDtypeStruct((EXTRA, LANES), jnp.float32)] * (n_gr - half),
        in_specs=[VMEM] * 5,
        out_specs=[VMEM] * (2 * n_gr - half),
        compiler_params=GRANT,
        cost_estimate=cost(late),
        name="last_sums",
    )(rows, scale, total, dens, late)

    sent = [part.astype(jnp.float16) for part in sums[:n_gr]]
    back = [sent[0]] + [along_gr(sent[k], k) for k in range(1, n_gr)]
    back = [part.astype(jnp.float32) for part in back]
    back += [along_gr(sums[half + k], k) for k in range(half, n_gr)]
    neighbour_sum, density = pl.pallas_call(
        functools.partial(restore_kernel, half),
        out_shape=[
            jax.ShapeDtypeStruct((count, width), jnp.float32),
            jax.ShapeDtypeStruct((1, count), jnp.float32),
        ],
        in_specs=[VMEM] * (1 + len(back)),
        out_specs=[VMEM, VMEM],
        compiler_params=GRANT,
        name="restore_rows",
    )(chosen, *back[n_gr - 1 :: -1], *back[:n_gr - 1 : -1])
    return (neighbour_sum, density.reshape(count))


def solution(mesh):
    in_specs = (P(("gr", "gc"), None), P(("gr", "gc")))
    out_specs = (P(("gr", "gc"), None), P(("gr", "gc")))
    return jax.shard_map(
        functools.partial(on_device, mesh.shape["gr"], mesh.shape["gc"]),
        mesh=mesh,
        in_specs=in_specs,
        out_specs=out_specs,
        check_vma=False,
    )
```
